32 devices in a mesh: dp: 4 (over y, core), ctx: 8 (over z, x).
Axes of the slice: x: 2, y: 2, z: 4, core: 2. Of those that a mesh axis runs over, the one named last changes fastest.
Arguments:
- tokens: bfloat16 [4, 1024, 1024], P('dp', 'ctx'), may hold values from -6 to 6
- out_cotangent: bfloat16 [4, 1024, 1024], P('dp', 'ctx'), may hold values from -6 to 6
- input_gain: bfloat16 [1024], P(('dp', 'ctx')), may hold values from 0.5 to 1.5
- mamba_gate_weight: bfloat16 [1024, 1536], P(('dp', 'ctx')), may hold values from -0.1875 to 0.1875
- mamba_mix_weight: bfloat16 [1024, 1792], P(('dp', 'ctx')), may hold values from -0.1875 to 0.1875
- mamba_step_weight: bfloat16 [1024, 24], P(('dp', 'ctx')), may hold values from -0.1875 to 0.1875
- conv_kernel: bfloat16 [4, 1792], P(None, ('dp', 'ctx')), may hold values from -3 to 3
- conv_offset: bfloat16 [1792], P(('dp', 'ctx')), may hold values from -3 to 3
- step_offset: float32 [24], replicated, may hold values from -5 to -3
- decay_log: float32 [24], replicated, may hold values from -6 to 0
- skip_scale: float32 [24], replicated, may hold values from 0.5 to 1.5
- mamba_norm_gain: bfloat16 [1536], P(('dp', 'ctx')), may hold values from 0.5 to 1.5
- mamba_out_weight: bfloat16 [1536, 1024], P(None, ('dp', 'ctx')), may hold values from -0.15625 to 0.15625
- query_weight: bfloat16 [1024, 512], P(('dp', 'ctx')), may hold values from -0.1875 to 0.1875
- key_weight: bfloat16 [1024, 128], P(('dp', 'ctx')), may hold values from -0.1875 to 0.1875
- value_weight: bfloat16 [1024, 128], P(('dp', 'ctx')), may hold values from -0.1875 to 0.1875
- attention_out_weight: bfloat16 [512, 1024], P(None, ('dp', 'ctx')), may hold values from -6 to 6
- ffn_gain: bfloat16 [1024], P(('dp', 'ctx')), may hold values from 0.5 to 1.5
- feed_gate_weight: bfloat16 [1024, 2048], P(('dp', 'ctx')), may hold values from -0.1875 to 0.1875
- feed_up_weight: bfloat16 [1024, 2048], P(('dp', 'ctx')), may hold values from -0.1875 to 0.1875
- feed_down_weight: bfloat16 [2048, 1024], P(None, ('dp', 'ctx')), may hold values from -0.125 to 0.125
Outputs:
- layer_out: bfloat16 [4, 1024, 1024], P('dp', 'ctx')
- input_gradient: float32 [4, 1024, 1024], P('dp', 'ctx')
- input_gain_gradient: float32 [1024], P(('dp', 'ctx'))
- mamba_gate_gradient: float32 [1024, 1536], P(('dp', 'ctx'))
- mamba_mix_gradient: float32 [1024, 1792], P(('dp', 'ctx'))
- mamba_step_gradient: float32 [1024, 24], P(('dp', 'ctx'))
- conv_kernel_gradient: float32 [4, 1792], P(None, ('dp', 'ctx'))
- conv_offset_gradient: float32 [1792], P(('dp', 'ctx'))
- step_offset_gradient: float32 [24], replicated
- decay_log_gradient: float32 [24], replicated
- skip_scale_gradient: float32 [24], replicated
- mamba_norm_gain_gradient: float32 [1536], P(('dp', 'ctx'))
- mamba_out_gradient: float32 [1536, 1024], P(None, ('dp', 'ctx'))
- query_gradient: float32 [1024, 512], P(('dp', 'ctx'))
- key_gradient: float32 [1024, 128], P(('dp', 'ctx'))
- value_gradient: float32 [1024, 128], P(('dp', 'ctx'))
- attention_out_gradient: float32 [512, 1024], P(None, ('dp', 'ctx'))
- ffn_gain_gradient: float32 [1024], P(('dp', 'ctx'))
- feed_gate_gradient: float32 [1024, 2048], P(('dp', 'ctx'))
- feed_up_gradient: float32 [1024, 2048], P(('dp', 'ctx'))
- feed_down_gradient: float32 [2048, 1024], P(None, ('dp', 'ctx'))
The draws below stay inside these ranges and needn't reach their ends.
All inputs are finite; a program needn't handle non-finite values.
Results may differ from the reference program's by a relative error of at most 0.015.
Values may be sent and summed in bfloat16 or wider, within the bound.
No kernel may reach another device: no remote copies, remote signals or barrier semaphores. Data moves between devices by JAX's collectives and lax.ppermute only.
A program may use at most 256 MiB of HBM per device.

```python
import jax
import jax.numpy as jnp
from jax import lax

D = 1024
DSSM = 1536
MH = 24
MP = 64
NS = 128
KW = 4
AH = 8
KVH = 2
HD = 64
FF = 2048
SPAN = 128
SEQS = 4
LENGTH = 1024
CONV = 1792


def with_spikes(entries, stream_key, source, target, blocks, factor):
    def block_of(position):
        return (jnp.arange(entries.shape[position]) // (entries.shape[position] // blocks)).reshape((-1,) + (1,) * (entries.ndim - 1 - position))

    one_side = jax.random.permutation(stream_key, blocks)[block_of(target)]
    other_side = (block_of(target) + blocks // 2) % blocks
    return jnp.where((block_of(source) == one_side) | (block_of(source) == other_side), factor * entries, entries)


def shard_levels(stream_key, extent, split, smallest, top_value):
    factor_of, own = 1.0, jax.random.fold_in(stream_key, 6)
    for position, blocks in split:
        draws = jnp.exp(jax.random.uniform(jax.random.fold_in(own, position), (blocks,), jnp.float32, smallest / len(split), top_value / len(split)))
        factor_of = factor_of * jnp.repeat(draws, extent[position] // blocks).reshape([-1 if axis == position else 1 for axis in range(len(extent))])
    return factor_of


def scatter_about(stream_key, dims, deviation, reach, cuts=(), held_as=jnp.bfloat16):
    loudness = shard_levels(stream_key, dims, cuts, -0.22, 0.18) if cuts else 1.0
    entries = jax.random.normal(stream_key, dims, jnp.float32) * deviation * loudness
    return jnp.minimum(jnp.maximum(entries, -reach), reach).astype(held_as)


def noise_with(own_key, shape, deviation, reach, cuts, heavy, kind=jnp.bfloat16):
    array = deviation * jax.random.normal(own_key, shape, jnp.float32)
    if cuts:
        array = array * shard_levels(own_key, shape, cuts, -0.22, 0.18)
    return jnp.clip(with_spikes(array, jax.random.fold_in(own_key, 3), *heavy), -reach, reach).astype(kind)


def setup_inputs(seed: int = 0) -> dict:
    arg_keys = jax.random.split(jax.random.key(seed), 22)
    return {
        "tokens": scatter_about(arg_keys[0], (SEQS, LENGTH, D), 1, 6.0, ((0, 4), (1, 8))),
        "out_cotangent": noise_with(arg_keys[1], (SEQS, LENGTH, D), 1, 6.0, ((0, 4), (1, 8)), (1, 2, 8, 2.0)),
        "input_gain": jnp.clip(1.0 + 0.1 * jax.random.normal(arg_keys[2], (D,), jnp.float32), 0.5, 1.5).astype(jnp.bfloat16),
        "mamba_gate_weight": scatter_about(arg_keys[3], (D, DSSM), D ** -0.5, 0.1875, ((0, 32),)),
        "mamba_mix_weight": scatter_about(arg_keys[4], (D, CONV), D ** -0.5, 0.1875, ((0, 32),)),
        "mamba_step_weight": scatter_about(arg_keys[5], (D, MH), D ** -0.5, 0.1875, ((0, 32),)),
        "conv_kernel": scatter_about(arg_keys[6], (KW, CONV), KW ** -0.5, 3.0, ((1, 32),)),
        "conv_offset": scatter_about(arg_keys[7], (CONV,), 0.5, 3.0, ((0, 32),)),
        "step_offset": jnp.clip(jax.random.uniform(arg_keys[8], (MH,), jnp.float32, -5.0, -3.0), -5.0, -3.0),
        "decay_log": jnp.clip(jax.random.uniform(arg_keys[9], (MH,), jnp.float32, -6.0, 0.0), -6.0, 0.0),
        "skip_scale": jnp.clip(jax.random.uniform(arg_keys[10], (MH,), jnp.float32, 0.5, 1.5), 0.5, 1.5),
        "mamba_norm_gain": jnp.clip(1.0 + 0.1 * jax.random.normal(arg_keys[11], (DSSM,), jnp.float32), 0.5, 1.5).astype(jnp.bfloat16),
        "mamba_out_weight": scatter_about(arg_keys[12], (DSSM, D), DSSM ** -0.5, 0.15625, ((1, 32),)),
        "query_weight": scatter_about(arg_keys[13], (D, AH * HD), D ** -0.5, 0.1875, ((0, 32),)),
        "key_weight": scatter_about(arg_keys[14], (D, KVH * HD), D ** -0.5, 0.1875, ((0, 32),)),
        "value_weight": scatter_about(arg_keys[15], (D, KVH * HD), D ** -0.5, 0.1875, ((0, 32),)),
        "attention_out_weight": scatter_about(arg_keys[16], (AH * HD, D), 1, 6.0, ((1, 32),)),
        "ffn_gain": jnp.clip(1.0 + 0.1 * jax.random.normal(arg_keys[17], (D,), jnp.float32), 0.5, 1.5).astype(jnp.bfloat16),
        "feed_gate_weight": scatter_about(arg_keys[18], (D, FF), D ** -0.5, 0.1875, ((0, 32),)),
        "feed_up_weight": scatter_about(arg_keys[19], (D, FF), D ** -0.5, 0.1875, ((0, 32),)),
        "feed_down_weight": scatter_about(arg_keys[20], (FF, D), FF ** -0.5, 0.125, ((1, 32),)),
    }


EPSILON = 1e-05
ROPE_BASE = 100000000000.0
HIGHEST = lax.Precision.HIGHEST
NEGATIVE = -1e+30

def forward_product(left, right):
    return jnp.dot(left, right, preferred_element_type=jnp.float32)

def weight_product(left, right):
    return lax.dot_general(left, right, (((0,), (0,)), ((), ())), preferred_element_type=jnp.float32)

def input_product(upstream, weight):
    return lax.dot_general(upstream, weight, (((1,), (1,)), ((), ())), preferred_element_type=jnp.float32)

def rms_forward(values, gain):
    scale = lax.rsqrt(lax.optimization_barrier(jnp.mean(values * values, -1, keepdims=True)) + EPSILON)
    return (values * scale * gain, scale)

def rms_backward(values, scale, gain, upstream):
    weighted = upstream * gain
    gain_part = lax.optimization_barrier(jnp.sum(upstream * values * scale, 0))
    result = scale * weighted - values * scale ** 3 * lax.optimization_barrier(jnp.mean(weighted * values, -1, keepdims=True))
    return (result, gain_part)

def rope_tables(positions):
    ladder = jnp.arange(HD // 2, dtype=jnp.float32)
    rates = ROPE_BASE ** (-2.0 * ladder / HD)
    angles = positions.astype(jnp.float32)[:, None] * rates[None, :]
    return (jnp.cos(angles), jnp.sin(angles))

def rotate(values, cosine, sine):
    half = values.shape[-1] // 2
    first = values[..., :half]
    second = values[..., half:]
    cosine = cosine[:, None, :]
    sine = sine[:, None, :]
    return jnp.concatenate([first * cosine - second * sine, second * cosine + first * sine], -1)

def mamba_prep(extended, step_rows, kernel, offset, step_offset, decay_log):
    rows = step_rows.shape[0]
    conv = offset[None, :] + kernel[0][None, :] * extended[0:rows]
    for tap in range(1, kernel.shape[0]):
        conv = conv + kernel[tap][None, :] * extended[tap:tap + rows]
    steps = jax.nn.softplus(step_rows + step_offset[None, :])
    curve = jnp.cumsum(-jnp.exp(decay_log)[None, :] * steps, axis=0)
    return (jax.nn.silu(conv), steps, curve)

def mamba_state(conv, steps, curve):
    rows, heads = steps.shape
    signal = conv[:, :DSSM].reshape(rows, heads, MP)
    entry = conv[:, DSSM:DSSM + NS]
    weights = jnp.exp(curve[-1][None, :] - curve) * steps
    state = jnp.einsum('th,thp,tn->hpn', weights, signal, entry, precision=HIGHEST)
    return (jnp.exp(curve[-1]), state)

def mamba_out(conv, steps, curve, gate_rows, skip_scale, norm_gain, state_in):
    rows, heads = steps.shape
    signal = conv[:, :DSSM].reshape(rows, heads, MP)
    entry = conv[:, DSSM:DSSM + NS]
    readout = conv[:, DSSM + NS:]
    causal = jnp.arange(rows)[:, None] >= jnp.arange(rows)[None, :]
    spread = curve.T[:, :, None] - curve.T[:, None, :]
    mixing = jnp.where(causal[None], jnp.exp(jnp.where(causal[None], spread, 0.0)), 0.0)
    intersection = jnp.dot(readout, entry.T, precision=HIGHEST)
    mixing = mixing * intersection[None] * steps.T[:, None, :]
    local_part = jnp.einsum('hts,shp->thp', mixing, signal, precision=HIGHEST)
    carried = jnp.einsum('tn,hpn->thp', readout, state_in, precision=HIGHEST) * jnp.exp(curve)[:, :, None]
    mixed = (local_part + carried + skip_scale[None, :, None] * signal).reshape(rows, DSSM)
    gated = mixed * jax.nn.silu(gate_rows)
    return gated * lax.rsqrt(lax.optimization_barrier(jnp.mean(gated * gated, -1, keepdims=True)) + EPSILON) * norm_gain

def mamba_sequence(mix_rows, step_rows, gate_rows, kernel, offset, step_offset, decay_log, skip_scale, norm_gain):
    length = mix_rows.shape[0]
    padded = jnp.concatenate([jnp.zeros((KW - 1, mix_rows.shape[1]), jnp.float32), mix_rows], 0)

    def one_block(state, index):
        start = index * SPAN
        extended = lax.dynamic_slice_in_dim(padded, start, SPAN + KW - 1, 0)
        raw = lax.dynamic_slice_in_dim(step_rows, start, SPAN, 0)
        gates = lax.dynamic_slice_in_dim(gate_rows, start, SPAN, 0)
        conv, steps, curve = mamba_prep(extended, raw, kernel, offset, step_offset, decay_log)
        total, local_state = mamba_state(conv, steps, curve)
        result = mamba_out(conv, steps, curve, gates, skip_scale, norm_gain, state)
        return (total[:, None, None] * state + local_state, result)
    start_state = jnp.zeros((MH, MP, NS), jnp.float32)
    final, results = lax.scan(one_block, start_state, jnp.arange(length // SPAN, dtype=jnp.int32))
    return results.reshape(length, DSSM)

def attention_forward(query, keys, values):
    length = query.shape[0]
    group = AH // KVH
    scale = HD ** (-0.5)
    keys_wide = keys.astype(jnp.float32)
    values_wide = values.astype(jnp.float32)
    key_index = jnp.arange(length, dtype=jnp.int32)

    def one_block(index):
        start = index * SPAN
        rows = lax.dynamic_slice_in_dim(query, start, SPAN, 0).reshape(SPAN, KVH, group, HD).astype(jnp.float32)
        scores = jnp.einsum('tgjd,sgd->gjts', rows, keys_wide) * scale
        visible = (start + jnp.arange(SPAN, dtype=jnp.int32))[:, None] >= key_index[None, :]
        peak = lax.optimization_barrier(jnp.max(jnp.where(visible, scores, NEGATIVE), -1, keepdims=True))
        weights = jnp.where(visible, jnp.exp(scores - peak), 0.0)
        total = lax.optimization_barrier(jnp.sum(weights, -1, keepdims=True))
        rounded = lax.optimization_barrier(weights.astype(jnp.bfloat16)).astype(jnp.float32)
        mixed = jnp.einsum('gjts,sgd->gjtd', rounded, values_wide) / total
        return (mixed.transpose(2, 0, 1, 3).reshape(SPAN, AH * HD), (peak + jnp.log(total))[..., 0])
    mixed, log_total = lax.map(one_block, jnp.arange(length // SPAN, dtype=jnp.int32))
    return (mixed.reshape(length, AH * HD).astype(jnp.bfloat16), log_total)

def attention_backward(query, keys, values, attended, back_attended, log_total):
    length = query.shape[0]
    group = AH // KVH
    scale = HD ** (-0.5)
    keys_wide = keys.astype(jnp.float32)
    values_wide = values.astype(jnp.float32)
    key_index = jnp.arange(length, dtype=jnp.int32)

    def one_block(carry, inputs):
        back_keys, back_values = carry
        index, block_total = inputs
        start = index * SPAN
        rows = lax.dynamic_slice_in_dim(query, start, SPAN, 0).reshape(SPAN, KVH, group, HD).astype(jnp.float32)
        outs = lax.dynamic_slice_in_dim(attended, start, SPAN, 0).reshape(SPAN, KVH, group, HD).astype(jnp.float32)
        upstream = lax.dynamic_slice_in_dim(back_attended, start, SPAN, 0).reshape(SPAN, KVH, group, HD).astype(jnp.float32)
        delta = lax.optimization_barrier(jnp.sum(upstream * outs, -1)).transpose(1, 2, 0)
        scores = jnp.einsum('tgjd,sgd->gjts', rows, keys_wide) * scale
        visible = (start + jnp.arange(SPAN, dtype=jnp.int32))[:, None] >= key_index[None, :]
        chance = jnp.where(visible, jnp.exp(scores - block_total[..., None]), 0.0)
        low_chance = lax.optimization_barrier(chance.astype(jnp.bfloat16)).astype(jnp.float32)
        back_values = back_values + jnp.einsum('gjts,tgjd->sgd', low_chance, upstream)
        back_chance = jnp.einsum('tgjd,sgd->gjts', upstream, values_wide)
        back_scores = (chance * (back_chance - delta[..., None]) * scale).astype(jnp.bfloat16)
        back_scores = lax.optimization_barrier(back_scores).astype(jnp.float32)
        back_rows = jnp.einsum('gjts,sgd->tgjd', back_scores, keys_wide)
        back_keys = back_keys + jnp.einsum('gjts,tgjd->sgd', back_scores, rows)
        return ((back_keys, back_values), back_rows.reshape(SPAN, AH, HD))
    empty = jnp.zeros((length, KVH, HD), jnp.float32)
    (back_keys, back_values), back_query = lax.scan(one_block, (empty, empty), (jnp.arange(length // SPAN, dtype=jnp.int32), log_total))
    return (back_query.reshape(length, AH, HD), back_keys, back_values)

def one_sequence(hidden_in, upstream, params):
    input_gain, gate_weight, mix_weight, step_weight, conv_kernel, conv_offset, step_offset, decay_log, skip_scale, mamba_gain, mamba_out_weight, query_weight, key_weight, value_weight, attention_out_weight, ffn_gain, feed_gate, feed_up, feed_down = params
    length = hidden_in.shape[0]
    normed, scale_one = rms_forward(hidden_in, input_gain)
    low_normed = normed.astype(jnp.bfloat16)
    gate_rows = forward_product(low_normed, gate_weight)
    mix_rows = forward_product(low_normed, mix_weight).astype(jnp.bfloat16)
    step_rows = forward_product(low_normed, step_weight)
    mix_wide = lax.optimization_barrier(mix_rows).astype(jnp.float32)
    mamba_result, mamba_pull = jax.vjp(mamba_sequence, mix_wide, step_rows, gate_rows, conv_kernel, conv_offset, step_offset, decay_log, skip_scale, mamba_gain)
    mamba_rows = mamba_result.astype(jnp.bfloat16)
    mamba_branch = forward_product(mamba_rows, mamba_out_weight)
    cosine, sine = rope_tables(jnp.arange(length, dtype=jnp.int32))
    query = rotate(forward_product(low_normed, query_weight).reshape(length, AH, HD), cosine, sine).astype(jnp.bfloat16)
    keys = rotate(forward_product(low_normed, key_weight).reshape(length, KVH, HD), cosine, sine).astype(jnp.bfloat16)
    values = forward_product(low_normed, value_weight).astype(jnp.bfloat16).reshape(length, KVH, HD)
    attended, log_total = attention_forward(query, keys, values)
    attention_branch = forward_product(attended, attention_out_weight)
    middle = hidden_in + mamba_branch + attention_branch
    normed_two, scale_two = rms_forward(middle, ffn_gain)
    low_two = normed_two.astype(jnp.bfloat16)
    gate_pre = forward_product(low_two, feed_gate)
    up_pre = forward_product(low_two, feed_up)
    activation = (jax.nn.silu(gate_pre) * up_pre).astype(jnp.bfloat16)
    layer_out = (middle + forward_product(activation, feed_down)).astype(jnp.bfloat16)
    gradient_down = weight_product(activation, upstream)
    back_activation = input_product(upstream, feed_down)
    sigmoid = jax.nn.sigmoid(gate_pre)
    back_gate = (back_activation * up_pre * sigmoid * (1.0 + gate_pre * (1.0 - sigmoid))).astype(jnp.bfloat16)
    back_up = (back_activation * jax.nn.silu(gate_pre)).astype(jnp.bfloat16)
    gradient_feed_gate = weight_product(low_two, back_gate)
    gradient_feed_up = weight_product(low_two, back_up)
    back_normed_two = input_product(back_gate, feed_gate) + input_product(back_up, feed_up)
    back_middle, gradient_gain_two = rms_backward(middle, scale_two, ffn_gain, back_normed_two)
    back_middle = back_middle + upstream.astype(jnp.float32)
    low_middle = back_middle.astype(jnp.bfloat16)
    gradient_mamba_out = weight_product(mamba_rows, low_middle)
    back_mamba_rows = input_product(low_middle, mamba_out_weight)
    gradient_attention_out = weight_product(attended, low_middle)
    back_attended = input_product(low_middle, attention_out_weight).astype(jnp.bfloat16)
    back_query_turned, back_keys_turned, back_values_full = attention_backward(query, keys, values, attended, back_attended, log_total)
    back_query = rotate(back_query_turned, cosine, -sine).reshape(length, AH * HD).astype(jnp.bfloat16)
    back_keys = rotate(back_keys_turned, cosine, -sine).reshape(length, KVH * HD).astype(jnp.bfloat16)
    back_values = back_values_full.reshape(length, KVH * HD).astype(jnp.bfloat16)
    mamba_grads = mamba_pull(back_mamba_rows)
    low_mix = mamba_grads[0].astype(jnp.bfloat16)
    low_step = mamba_grads[1].astype(jnp.bfloat16)
    low_gate = mamba_grads[2].astype(jnp.bfloat16)
    back_normed = input_product(low_gate, gate_weight) + input_product(low_mix, mix_weight) + input_product(low_step, step_weight)
    back_normed = back_normed + input_product(back_query, query_weight) + input_product(back_keys, key_weight) + input_product(back_values, value_weight)
    back_hidden, gradient_gain_one = rms_backward(hidden_in, scale_one, input_gain, back_normed)
    gradients = (gradient_gain_one, weight_product(low_normed, low_gate), weight_product(low_normed, low_mix), weight_product(low_normed, low_step), mamba_grads[3], mamba_grads[4], mamba_grads[5], mamba_grads[6], mamba_grads[7], mamba_grads[8], gradient_mamba_out, weight_product(low_normed, back_query), weight_product(low_normed, back_keys), weight_product(low_normed, back_values), gradient_attention_out, gradient_gain_two, gradient_feed_gate, gradient_feed_up, gradient_down)
    return ((layer_out, back_hidden + back_middle), gradients)

def reference(tokens, out_cotangent, input_gain, mamba_gate_weight, mamba_mix_weight, mamba_step_weight, conv_kernel, conv_offset, step_offset, decay_log, skip_scale, mamba_norm_gain, mamba_out_weight, query_weight, key_weight, value_weight, attention_out_weight, ffn_gain, feed_gate_weight, feed_up_weight, feed_down_weight):
    params = (input_gain.astype(jnp.float32), mamba_gate_weight, mamba_mix_weight, mamba_step_weight, conv_kernel.astype(jnp.float32), conv_offset.astype(jnp.float32), step_offset, decay_log, skip_scale, mamba_norm_gain.astype(jnp.float32), mamba_out_weight, query_weight, key_weight, value_weight, attention_out_weight, ffn_gain.astype(jnp.float32), feed_gate_weight, feed_up_weight, feed_down_weight)
    start_sums = jax.tree.map(lambda item: jnp.zeros(item.shape, jnp.float32), params)

    def sequence_step(sums, index):
        outputs, gradients = one_sequence(tokens[index].astype(jnp.float32), out_cotangent[index], params)
        return (jax.tree.map(jnp.add, sums, gradients), outputs)
    sums, outputs = lax.scan(sequence_step, start_sums, jnp.arange(SEQS, dtype=jnp.int32))
    layer_out, input_gradient = outputs
    return (layer_out, input_gradient, sums[0], sums[1], sums[2], sums[3], sums[4], sums[5], sums[6], sums[7], sums[8], sums[9], sums[10], sums[11], sums[12], sums[13], sums[14], sums[15], sums[16], sums[17], sums[18])
```

```python
import jax
import jax.numpy as jnp
from jax import lax
from jax.sharding import PartitionSpec as P

D = 1024
DSSM = 1536
MH = 24
MP = 64
NS = 128
KW = 4
AH = 8
KVH = 2
HD = 64
FF = 2048
CONV = DSSM + 2 * NS

TP = 4
SW = DSSM // TP
SH = MH // TP
QW = AH * HD // TP
FW = FF // TP
MIXW = SW + 2 * NS
STEP_AT = SW + MIXW + QW + 2 * HD
VEC = 16
WIDE = 1408

EPSILON = 1e-05
ROPE_BASE = 100000000000.0
HIGHEST = lax.Precision.HIGHEST
NEGATIVE = -1e30
BOTH = ("dp", "ctx")
bf16 = jnp.bfloat16
f32 = jnp.float32


def forward_product(left, right):
    return jnp.dot(left, right, preferred_element_type=f32)


def weight_product(left, right):
    return lax.dot_general(
        left, right, (((0,), (0,)), ((), ())), preferred_element_type=f32
    ).astype(bf16)


def input_product(upstream, weight):
    return lax.dot_general(
        upstream, weight, (((1,), (1,)), ((), ())), preferred_element_type=f32
    )


def swap_core(value):
    pairs = [(i, i ^ 1) for i in range(lax.axis_size("dp"))]
    return lax.ppermute(value, "dp", pairs)


def swap_side(value):
    pairs = [(i, i ^ 1) for i in range(lax.axis_size("ctx"))]
    return lax.ppermute(value, "ctx", pairs)


def swap_both(value):
    blocks = lax.axis_size("ctx")
    count = lax.axis_size("dp") * blocks
    pairs = [(i, ((i // blocks) ^ 1) * blocks + ((i % blocks) ^ 1)) for i in range(count)]
    return lax.ppermute(value, BOTH, pairs)


def move_spans(value, by):
    blocks = lax.axis_size("ctx")
    pairs = [(i, i + 2 * by) for i in range(blocks) if 0 <= i + 2 * by < blocks]
    return lax.ppermute(value, "ctx", pairs)


def group_gather(value, side):
    other = swap_side(value)
    first = side == 0
    mine = jnp.concatenate([jnp.where(first, value, other), jnp.where(first, other, value)], 0)
    return jnp.concatenate([mine, swap_core(mine)], 0)


def group_scatter(partial, side):
    span = partial.shape[0] // 2
    rows = span // 2
    mine = partial[:span] + swap_core(partial[span:])
    first = side == 0
    keep = jnp.where(first, mine[:rows], mine[rows:])
    send = jnp.where(first, mine[rows:], mine[:rows]).astype(bf16)
    return keep + swap_side(send).astype(f32)


def group_sum(value):
    span = value.shape[0] // 2
    other = swap_core(value)
    value = value + jnp.concatenate([other[span:], other[:span]], 0)
    return value + swap_side(value)


def group_swap(parts, rank):
    def at(index):
        return lax.dynamic_index_in_dim(parts, index, 0, keepdims=True)

    pieces = (
        (rank, at(rank)),
        (rank ^ 1, swap_side(at(rank ^ 1))),
        (rank ^ 2, swap_core(at(rank ^ 2))),
        (rank ^ 3, swap_both(at(rank ^ 3))),
    )
    result = jnp.zeros_like(parts)
    for index, piece in pieces:
        result = lax.dynamic_update_slice_in_dim(result, piece, index, 0)
    return result


def rope_tables(positions):
    ladder = jnp.arange(HD // 2, dtype=f32)
    rates = ROPE_BASE ** (-2.0 * ladder / HD)
    angles = positions.astype(f32)[:, None] * rates[None, :]
    return (jnp.cos(angles), jnp.sin(angles))


def rotate(values, cosine, sine):
    half = values.shape[-1] // 2
    first = values[..., :half]
    second = values[..., half:]
    cosine = cosine[:, None, :]
    sine = sine[:, None, :]
    return jnp.concatenate([first * cosine - second * sine, second * cosine + first * sine], -1)


def mamba_prep(extended, step_rows, kernel, offset, step_offset, decay_log):
    rows = step_rows.shape[1]
    conv = offset + kernel[0] * extended[:, 0:rows]
    for tap in range(1, KW):
        conv = conv + kernel[tap] * extended[:, tap : tap + rows]
    steps = jax.nn.softplus(step_rows + step_offset)
    rate = -jnp.exp(decay_log) * steps
    lower = jnp.tril(jnp.ones((rows, rows), f32))
    curve = jnp.einsum("ts,bsh->bth", lower, rate, precision=HIGHEST)
    return (jax.nn.silu(conv), steps, curve)


def mamba_state(conv, steps, curve):
    batch, rows, heads = steps.shape
    signal = conv[..., :SW].reshape(batch, rows, heads, MP)
    entry = conv[..., SW : SW + NS]
    weights = jnp.exp(curve[:, -1:] - curve) * steps
    scaled = weights[..., None] * signal
    state = jnp.einsum("bthp,btn->bhpn", scaled, entry, precision=HIGHEST)
    return (curve[:, -1], state)


def mamba_out(conv, steps, curve, skip_scale, state_in):
    batch, rows, heads = steps.shape
    signal = conv[..., :SW].reshape(batch, rows, heads, MP)
    entry = conv[..., SW : SW + NS]
    readout = conv[..., SW + NS :]
    causal = jnp.tril(jnp.ones((rows, rows), jnp.bool_))
    turned = curve.transpose(0, 2, 1)
    spread = turned[:, :, :, None] - turned[:, :, None, :]
    mixing = jnp.where(causal, jnp.exp(jnp.where(causal, spread, 0.0)), 0.0)
    intersection = jnp.einsum("btn,bsn->bts", readout, entry, precision=HIGHEST)
    mixing = mixing * intersection[:, None] * steps.transpose(0, 2, 1)[:, :, None, :]
    local_part = jnp.einsum("bhts,bshp->bthp", mixing, signal, precision=HIGHEST)
    carried = (
        jnp.einsum("btn,bhpn->bthp", readout, state_in, precision=HIGHEST)
        * jnp.exp(curve)[..., None]
    )
    mixed = local_part + carried + skip_scale[:, None] * signal
    return mixed.reshape(batch * rows, heads * MP)


def visible_keys(span, spans, heads, at):
    query = jnp.arange(heads * span, dtype=jnp.int32)[:, None] % span
    key = jnp.arange(spans * span, dtype=jnp.int32)[None, :]
    back = key // span
    return jnp.where(back == 0, key <= query, back <= at)


def attend(query, keys, values, visible):
    scores = jnp.einsum("bqd,bkd->bqk", query, keys, preferred_element_type=f32) * HD ** (-0.5)
    scores = jnp.where(visible, scores, NEGATIVE)
    peak = jnp.max(scores, -1, keepdims=True)
    weights = jnp.exp(scores - peak)
    total = jnp.sum(weights, -1, keepdims=True)
    summed = jnp.einsum("bqk,bkd->bqd", weights.astype(bf16), values, preferred_element_type=f32)
    return (summed / total, peak + jnp.log(total))


def attend_back(query, keys, values, visible, back, log_total, delta):
    scale = HD ** (-0.5)
    scores = jnp.einsum("bqd,bkd->bqk", query, keys, preferred_element_type=f32) * scale
    chance = jnp.where(visible, jnp.exp(scores - log_total), 0.0)
    back_values = jnp.einsum(
        "bqk,bqd->bkd", chance.astype(bf16), back, preferred_element_type=f32
    )
    back_chance = jnp.einsum("bqd,bkd->bqk", back, values, preferred_element_type=f32)
    back_scores = (chance * (back_chance - delta) * scale).astype(bf16)
    back_query = jnp.einsum("bqk,bkd->bqd", back_scores, keys, preferred_element_type=f32)
    back_keys = jnp.einsum("bqk,bqd->bkd", back_scores, query, preferred_element_type=f32)
    return (back_query, jnp.concatenate([back_keys, back_values], -1))


def local(
    tokens,
    out_cotangent,
    input_gain,
    mamba_gate_weight,
    mamba_mix_weight,
    mamba_step_weight,
    conv_kernel,
    conv_offset,
    step_offset,
    decay_log,
    skip_scale,
    mamba_norm_gain,
    mamba_out_weight,
    query_weight,
    key_weight,
    value_weight,
    attention_out_weight,
    ffn_gain,
    feed_gate_weight,
    feed_up_weight,
    feed_down_weight,
):
    rows = tokens.shape[1]
    span = 2 * rows
    count = 2 * span
    pairs, spans = lax.axis_size("dp") // 2, lax.axis_size("ctx") // 2
    devices = 4 * pairs * spans
    dp_at, ctx_at = lax.axis_index("dp"), lax.axis_index("ctx")
    side, span_at = ctx_at % 2, ctx_at // 2
    rank = (dp_at % 2) * 2 + side
    part = D // devices
    conv_part = CONV // devices
    gain_part = DSSM // devices
    groups = [
        [(y * 2 + c) * 2 * spans + z * 2 + x for y in range(pairs) for z in range(spans)]
        for c in range(2)
        for x in range(2)
    ]

    def order(value):
        lead = value.shape[:-1]
        value = value.reshape(*lead, pairs, 2, spans, 2 * part)
        return jnp.swapaxes(value, -3, -2).reshape(*lead, D)

    def disorder(value):
        lead = value.shape[:-1]
        value = value.reshape(*lead, pairs, spans, 2, 2 * part)
        return jnp.swapaxes(value, -3, -2).reshape(*lead, D)

    def gather(value):
        return lax.all_gather(value, BOTH, axis=0, tiled=True, axis_index_groups=groups)

    def scatter(value):
        return lax.psum_scatter(
            value, BOTH, scatter_dimension=0, tiled=True, axis_index_groups=groups
        )

    vector = jnp.concatenate(
        [
            input_gain,
            ffn_gain,
            conv_kernel.reshape(-1),
            conv_offset,
            mamba_norm_gain,
        ]
    )
    vector = jnp.pad(vector, (0, part * VEC - vector.shape[0])).reshape(part, VEC)

    def mixer_part(s):
        kv = s // 2
        return jnp.concatenate(
            [
                mamba_gate_weight[:, SW * s : SW * (s + 1)],
                mamba_mix_weight[:, SW * s : SW * (s + 1)],
                mamba_mix_weight[:, DSSM:],
                query_weight[:, QW * s : QW * (s + 1)],
                key_weight[:, HD * kv : HD * (kv + 1)],
                value_weight[:, HD * kv : HD * (kv + 1)],
                mamba_step_weight[:, SH * s : SH * (s + 1)],
                vector,
                jnp.zeros((part, WIDE - STEP_AT - SH - VEC), bf16),
            ],
            1,
        )

    mamba_out_turned = mamba_out_weight.T
    attention_out_turned = attention_out_weight.T
    feed_down_turned = feed_down_weight.T

    def feed_part(s):
        return jnp.concatenate(
            [
                mamba_out_turned[:, SW * s : SW * (s + 1)],
                attention_out_turned[:, QW * s : QW * (s + 1)],
                feed_gate_weight[:, FW * s : FW * (s + 1)],
                feed_up_weight[:, FW * s : FW * (s + 1)],
                feed_down_turned[:, FW * s : FW * (s + 1)],
            ],
            1,
        )

    mixer_own = group_swap(jnp.stack([mixer_part(s) for s in range(TP)]), rank)
    mixer = gather(mixer_own.reshape(TP * part, WIDE))
    feed_own = group_swap(jnp.stack([feed_part(s) for s in range(TP)]), rank)
    feed_own, mixer = lax.optimization_barrier((feed_own, mixer))
    feed = gather(feed_own.reshape(TP * part, feed_own.shape[-1]))
    full_out = feed[:, : SW + QW]
    full_gate_up = feed[:, SW + QW : SW + QW + 2 * FW]
    full_down = feed[:, SW + QW + 2 * FW :]

    vectors = mixer[:, STEP_AT + SH : STEP_AT + SH + VEC].reshape(devices, part * VEC)
    full_gain = vectors[:, :part].reshape(D).astype(f32)
    full_gain_two = vectors[:, part : 2 * part].reshape(D).astype(f32)
    natural = vectors.reshape(pairs, spans, 2, 2, part * VEC)
    natural = natural.transpose(0, 2, 1, 3, 4).reshape(devices, part * VEC)
    at = 2 * part
    all_kernel = natural[:, at : at + KW * conv_part].reshape(devices, KW, conv_part)
    all_kernel = all_kernel.transpose(1, 0, 2).reshape(KW, CONV)
    at += KW * conv_part
    all_offset = natural[:, at : at + conv_part].reshape(1, CONV)
    at += conv_part
    all_mamba_gain = natural[:, at : at + gain_part].reshape(DSSM)
    taps = jnp.concatenate([all_kernel, all_offset], 0)
    taps = jnp.concatenate(
        [lax.dynamic_slice_in_dim(taps, rank * SW, SW, 1), taps[:, DSSM:]], 1
    ).astype(f32)
    kernel, offset = taps[:KW], taps[KW]
    mamba_gain = lax.dynamic_slice_in_dim(all_mamba_gain, rank * SW, SW, 0).astype(f32)
    own_step_offset = lax.dynamic_slice_in_dim(step_offset, rank * SH, SH, 0)
    own_decay_log = lax.dynamic_slice_in_dim(decay_log, rank * SH, SH, 0)
    own_skip = lax.dynamic_slice_in_dim(skip_scale, rank * SH, SH, 0)

    own_low = order(tokens[0])
    own_hidden = own_low.astype(f32)
    own_scale_one = lax.rsqrt(jnp.mean(own_hidden * own_hidden, -1, keepdims=True) + EPSILON)
    hidden = group_gather(own_low, side).astype(f32)
    own_cotangent = order(out_cotangent[0])
    upstream = group_gather(own_cotangent, side)
    scale_one = lax.rsqrt(jnp.mean(hidden * hidden, -1, keepdims=True) + EPSILON)
    low_normed = (hidden * scale_one * full_gain).astype(bf16)

    projected = forward_product(low_normed, mixer)
    gate_rows = projected[:, :SW]
    mix_rows = projected[:, SW : SW + MIXW].astype(bf16).reshape(2, span, MIXW)
    at = SW + MIXW
    query_rows = projected[:, at : at + QW]
    key_rows = projected[:, at + QW : at + QW + HD]
    value_rows = projected[:, at + QW + HD : STEP_AT]
    step_rows = projected[:, STEP_AT : STEP_AT + SH].reshape(2, span, SH)

    positions = span_at * span + jnp.arange(span, dtype=jnp.int32)
    cosine, sine = rope_tables(positions)
    heads = QW // HD
    query = rotate(query_rows.reshape(2, span, heads, HD), cosine, sine).astype(bf16)
    query = query.transpose(0, 2, 1, 3).reshape(2, heads * span, HD)
    keys = rotate(key_rows.reshape(2, span, 1, HD), cosine, sine).reshape(2, span, HD)
    key_value = jnp.concatenate([keys, value_rows.reshape(2, span, HD)], -1).astype(bf16)
    reached = [key_value] + [move_spans(key_value, s) for s in range(1, spans)]
    key_values = jnp.concatenate(reached, 1)
    all_keys, all_values = key_values[..., :HD], key_values[..., HD:]
    visible = visible_keys(span, spans, heads, span_at)

    rim = move_spans(mix_rows[:, span - (KW - 1) :], 1)
    extended = jnp.concatenate([rim, mix_rows], 1).astype(f32)
    (conv, steps, curve), prep_pull = jax.vjp(
        mamba_prep, extended, step_rows, kernel, offset, own_step_offset, own_decay_log
    )
    (log_decay, local_state), state_pull = jax.vjp(mamba_state, conv, steps, curve)
    low_state = local_state.astype(bf16)
    states = [move_spans(low_state, s) for s in range(1, spans)]
    decays = [move_spans(log_decay, s) for s in range(1, spans)]
    factors = []
    between = jnp.zeros_like(log_decay)
    for s in range(1, spans):
        factors.append(jnp.exp(between)[:, :, None, None])
        between = between + decays[s - 1]
    state_in = sum(factor * state.astype(f32) for factor, state in zip(factors, states))

    attended_rows, log_total = attend(query, all_keys, all_values, visible)

    def join(value):
        return value.reshape(2, heads, span, HD).transpose(0, 2, 1, 3).reshape(count, QW)

    def split(value):
        return value.reshape(2, span, heads, HD).transpose(0, 2, 1, 3).reshape(2, heads * span, HD)

    attended = join(attended_rows).astype(bf16)

    mixed, out_pull = jax.vjp(mamba_out, conv, steps, curve, own_skip, state_in)
    gate_sigmoid = jax.nn.sigmoid(gate_rows)
    gate_silu = gate_rows * gate_sigmoid
    gated = mixed * gate_silu
    square = group_sum(jnp.sum(gated * gated, -1))
    mamba_scale = lax.rsqrt(square / DSSM + EPSILON)[:, None]
    mamba_rows = (gated * mamba_scale * mamba_gain).astype(bf16)
    branches = jnp.concatenate([mamba_rows, attended], 1)
    middle = own_hidden + group_scatter(input_product(branches, full_out), side)

    scale_two = lax.rsqrt(jnp.mean(middle * middle, -1, keepdims=True) + EPSILON)
    low_two = group_gather((middle * scale_two * full_gain_two).astype(bf16), side)
    pre = forward_product(low_two, full_gate_up)
    gate_pre, up_pre = pre[:, :FW], pre[:, FW:]
    sigmoid = jax.nn.sigmoid(gate_pre)
    silu = gate_pre * sigmoid
    activation = (silu * up_pre).astype(bf16)

    back_activation = forward_product(upstream, full_down)
    back_gate = (back_activation * up_pre * sigmoid * (1.0 + gate_pre * (1.0 - sigmoid))).astype(
        bf16
    )
    back_up = (back_activation * silu).astype(bf16)
    back_feed = jnp.concatenate([back_gate, back_up], 1)
    back_normed_two = group_scatter(input_product(back_feed, full_gate_up), side)
    weighted = back_normed_two * full_gain_two
    gradient_gain_two = jnp.sum(back_normed_two * middle * scale_two, 0)
    back_middle = (
        own_cotangent.astype(f32)
        + scale_two * weighted
        - middle * scale_two**3 * jnp.mean(weighted * middle, -1, keepdims=True)
    )
    low_middle = group_gather(back_middle.astype(bf16), side)

    gradient_feed = scatter(
        jnp.concatenate(
            [
                weight_product(low_middle, branches),
                weight_product(low_two, back_feed),
                weight_product(upstream, activation),
            ],
            1,
        )
    )
    layer_out = middle + group_scatter(input_product(activation, full_down), side)

    back_branches = forward_product(low_middle, full_out)
    back_attended = back_branches[:, SW:].astype(bf16)
    back_rows = back_branches[:, :SW]
    wide_back = back_attended.astype(f32) * attended.astype(f32)
    delta = jnp.sum(split(wide_back), -1, keepdims=True)
    back_turned, back_key_values = attend_back(
        query, all_keys, all_values, visible, split(back_attended), log_total, delta
    )
    low_key_values = back_key_values.astype(bf16).reshape(2, spans, span, 2 * HD)
    back_key_value = back_key_values[:, :span]
    for s in range(1, spans):
        back_key_value = back_key_value + move_spans(low_key_values[:, s], -s).astype(f32)
    back_query = rotate(join(back_turned).reshape(2, span, heads, HD), cosine, -sine)
    back_keys = rotate(back_key_value[..., :HD].reshape(2, span, 1, HD), cosine, -sine)

    weighted = back_rows * mamba_gain
    gradient_mamba_gain = jnp.sum(back_rows * gated * mamba_scale, 0)
    product = group_sum(jnp.sum(weighted * gated, -1))[:, None] / DSSM
    back_gated = mamba_scale * weighted - gated * mamba_scale**3 * product
    back_mixed = back_gated * gate_silu
    low_gate = (
        back_gated * mixed * gate_sigmoid * (1.0 + gate_rows * (1.0 - gate_sigmoid))
    ).astype(bf16)
    out_grads = out_pull(back_mixed)
    next_back = jnp.zeros_like(local_state)
    for s in range(1, spans):
        sent = (factors[s - 1] * out_grads[4]).astype(bf16)
        next_back = next_back + move_spans(sent, -s).astype(f32)
    decay_back = jnp.sum(next_back * state_in, axis=(2, 3)) * jnp.exp(log_decay)
    state_grads = state_pull((decay_back, next_back))
    prep_grads = prep_pull(
        (
            out_grads[0] + state_grads[0],
            out_grads[1] + state_grads[1],
            out_grads[2] + state_grads[2],
        )
    )
    back_extended = prep_grads[0]
    returned = move_spans(back_extended[:, : KW - 1], -1)
    back_mix = back_extended[:, KW - 1 :]
    back_mix = jnp.concatenate(
        [back_mix[:, : span - (KW - 1)], back_mix[:, span - (KW - 1) :] + returned], 1
    )
    back_all = jnp.concatenate(
        [
            low_gate,
            back_mix.reshape(count, MIXW).astype(bf16),
            back_query.reshape(count, QW).astype(bf16),
            back_keys.reshape(count, HD).astype(bf16),
            back_key_value[..., HD:].reshape(count, HD).astype(bf16),
            prep_grads[1].reshape(count, SH).astype(bf16),
            jnp.zeros((count, WIDE - STEP_AT - SH), bf16),
        ],
        1,
    )
    gradient_mixer = scatter(weight_product(low_normed, back_all))
    back_normed = group_scatter(input_product(back_all, mixer), side)
    weighted = back_normed * full_gain
    gradient_gain_one = jnp.sum(back_normed * own_hidden * own_scale_one, 0)
    input_gradient = (
        back_middle
        + own_scale_one * weighted
        - own_hidden * own_scale_one**3 * jnp.mean(weighted * own_hidden, -1, keepdims=True)
    )

    def placed(value, width):
        wide = jnp.zeros(value.shape[:-1] + (width,), f32)
        return lax.dynamic_update_slice_in_dim(
            wide, value, rank * value.shape[-1], value.ndim - 1
        )

    tap_grads = jnp.concatenate([prep_grads[2], prep_grads[3][None]], 0)
    tap_grads = jnp.concatenate([placed(tap_grads[:, :SW], DSSM), tap_grads[:, SW:]], 1)
    head_grads = jnp.stack([prep_grads[4], prep_grads[5], out_grads[3]])
    gain_grads, tap_grads, mamba_gain_grad, head_grads = lax.psum(
        (
            jnp.stack([gradient_gain_one, gradient_gain_two]),
            tap_grads,
            placed(gradient_mamba_gain, DSSM),
            placed(head_grads, MH),
        ),
        BOTH,
    )
    feature_at = ((dp_at // 2 * spans + span_at) * TP + rank) * part
    own_gains = lax.dynamic_slice_in_dim(gain_grads, feature_at, part, 1)
    device_at = dp_at * 2 * spans + ctx_at
    own_taps = lax.dynamic_slice_in_dim(tap_grads, device_at * conv_part, conv_part, 1)
    own_mamba_gain = lax.dynamic_slice_in_dim(
        mamba_gain_grad, device_at * gain_part, gain_part, 0
    )

    feed_parts = group_swap(gradient_feed.reshape(TP, part, -1), rank).astype(f32)
    mixer_parts = group_swap(gradient_mixer.reshape(TP, part, WIDE), rank).astype(f32)

    def columns(parts, start, width):
        piece = parts[:, :, start : start + width]
        return piece.transpose(1, 0, 2).reshape(part, TP * width)

    def shared(start):
        piece = mixer_parts[:, :, start : start + HD].reshape(KVH, TP // KVH, part, HD)
        return jnp.sum(piece, 1).transpose(1, 0, 2).reshape(part, KVH * HD)

    at = SW + MIXW
    mix_gradient = jnp.concatenate(
        [
            columns(mixer_parts, SW, SW),
            jnp.sum(mixer_parts[:, :, 2 * SW : SW + MIXW], 0),
        ],
        1,
    )
    return (
        disorder(layer_out.astype(bf16))[None],
        disorder(input_gradient)[None],
        own_gains[0],
        columns(mixer_parts, 0, SW),
        mix_gradient,
        columns(mixer_parts, STEP_AT, SH),
        own_taps[:KW],
        own_taps[KW],
        head_grads[0],
        head_grads[1],
        head_grads[2],
        own_mamba_gain,
        columns(feed_parts, 0, SW).T,
        columns(mixer_parts, at, QW),
        shared(at + QW),
        shared(at + QW + HD),
        columns(feed_parts, SW, QW).T,
        own_gains[1],
        columns(feed_parts, SW + QW, FW),
        columns(feed_parts, SW + QW + FW, FW),
        columns(feed_parts, SW + QW + 2 * FW, FW).T,
    )


def solution(mesh):
    both = BOTH
    tokens = P("dp", "ctx", None)
    first = P(both, None)
    second = P(None, both)
    vector = P(both)
    whole = P()
    weights = (
        vector,
        first,
        first,
        first,
        second,
        vector,
        whole,
        whole,
        whole,
        vector,
        second,
        first,
        first,
        first,
        second,
        vector,
        first,
        first,
        second,
    )
    return jax.shard_map(
        local,
        mesh=mesh,
        in_specs=(tokens, tokens) + weights,
        out_specs=(tokens, tokens) + weights,
        check_vma=False,
    )
```

```python
import jax
import jax.numpy as jnp
from jax import lax
from jax.experimental import pallas as pl
from jax.experimental.pallas import tpu as pltpu
from jax.sharding import PartitionSpec as P

D = 1024
DSSM = 1536
MH = 24
MP = 64
NS = 128
KW = 4
AH = 8
KVH = 2
HD = 64
FF = 2048
CONV = DSSM + 2 * NS

TP = 4
SW = DSSM // TP
SH = MH // TP
QW = AH * HD // TP
FW = FF // TP
MIXW = SW + 2 * NS
STEP_AT = MIXW + QW + 2 * HD
VEC = 16
WIDE = 1024

EPSILON = 1e-05
ROPE_BASE = 100000000000.0
HIGHEST = lax.Precision.HIGHEST
NEGATIVE = -1e30
BOTH = ("dp", "ctx")
bf16 = jnp.bfloat16
f32 = jnp.float32


def forward_product(left, right):
    return jnp.dot(left, right, preferred_element_type=f32)


def input_product(upstream, weight):
    return lax.dot_general(
        upstream, weight, (((1,), (1,)), ((), ())), preferred_element_type=f32
    )


def swap_core(value):
    pairs = [(i, i ^ 1) for i in range(lax.axis_size("dp"))]
    return lax.ppermute(value, "dp", pairs)


def swap_side(value):
    pairs = [(i, i ^ 1) for i in range(lax.axis_size("ctx"))]
    return lax.ppermute(value, "ctx", pairs)


def swap_both(value):
    blocks = lax.axis_size("ctx")
    count = lax.axis_size("dp") * blocks
    pairs = [(i, ((i // blocks) ^ 1) * blocks + ((i % blocks) ^ 1)) for i in range(count)]
    return lax.ppermute(value, BOTH, pairs)


def move_spans(value, by):
    blocks = lax.axis_size("ctx")
    pairs = [(i, i + 2 * by) for i in range(blocks) if 0 <= i + 2 * by < blocks]
    return lax.ppermute(value, "ctx", pairs)


def group_gather(value, side):
    other = swap_side(value)
    first = side == 0
    mine = jnp.concatenate([jnp.where(first, value, other), jnp.where(first, other, value)], 0)
    return jnp.concatenate([mine, swap_core(mine)], 0)


def group_scatter(partial, side):
    span = partial.shape[0] // 2
    rows = span // 2
    mine = partial[:span] + swap_core(partial[span:])
    first = side == 0
    keep = jnp.where(first, mine[:rows], mine[rows:])
    send = jnp.where(first, mine[rows:], mine[:rows]).astype(bf16)
    return keep + swap_side(send).astype(f32)


def group_sum(value):
    span = value.shape[0] // 2
    other = swap_core(value)
    value = value + jnp.concatenate([other[span:], other[:span]], 0)
    return value + swap_side(value)


def group_swap(parts, rank):
    def at(index):
        return lax.dynamic_index_in_dim(parts, index, 0, keepdims=True)

    pieces = (
        (rank, at(rank)),
        (rank ^ 1, swap_side(at(rank ^ 1))),
        (rank ^ 2, swap_core(at(rank ^ 2))),
        (rank ^ 3, swap_both(at(rank ^ 3))),
    )
    result = jnp.zeros_like(parts)
    for index, piece in pieces:
        result = lax.dynamic_update_slice_in_dim(result, piece, index, 0)
    return result


def call(body, grid, in_specs, out_specs, out_shape, scratch=()):
    return pl.pallas_call(
        body,
        grid=grid,
        in_specs=in_specs,
        out_specs=out_specs,
        out_shape=out_shape,
        scratch_shapes=list(scratch),
        compiler_params=pltpu.CompilerParams(vmem_limit_bytes=48 * 1024 * 1024),
    )


def shape(*dims, dtype=f32):
    return jax.ShapeDtypeStruct(dims, dtype)


def row_block(rows, width):
    return pl.BlockSpec((rows, width), lambda b: (b, 0))


def seq_block(*dims):
    return pl.BlockSpec((1,) + dims, lambda b: (b,) + (0,) * len(dims))


def fixed(*dims):
    return pl.BlockSpec(dims, lambda b: (0,) * len(dims))


SCALAR = pl.BlockSpec(memory_space=pltpu.SMEM)


def product(left, right, left_dim=1, right_dim=0):
    return lax.dot_general(
        left, right, (((left_dim,), (right_dim,)), ((), ())), preferred_element_type=f32
    )


def halves(value):
    high = value.astype(bf16)
    return high, (value - high.astype(f32)).astype(bf16)


def fine_product(left, right, left_dim=1, right_dim=0):
    left_high, left_low = halves(left)
    right_high, right_low = halves(right)
    return (
        product(left_high, right_high, left_dim, right_dim)
        + product(left_high, right_low, left_dim, right_dim)
        + product(left_low, right_high, left_dim, right_dim)
    )


def head_mask():
    row = lax.broadcasted_iota(jnp.int32, (128, SW), 0)
    column = lax.broadcasted_iota(jnp.int32, (128, SW), 1)
    return jnp.where(column // MP == row, 1.0, 0.0).astype(bf16)


def spread_heads(value, mask):
    high, low = halves(value)
    return product(high, mask) + product(low, mask)


def sum_heads(value, mask):
    high, low = halves(value)
    return product(high, mask, 1, 1) + product(low, mask, 1, 1)


def rope_tables(positions):
    ladder = jnp.arange(HD // 2, dtype=f32)
    rates = ROPE_BASE ** (-2.0 * ladder / HD)
    angles = positions.astype(f32)[:, None] * rates[None, :]
    cosine, sine = jnp.cos(angles), jnp.sin(angles)
    return (
        jnp.concatenate([cosine] * 4, 1),
        jnp.concatenate([-sine, sine, -sine, sine], 1),
    )


def turn(value, cosine, sine):
    lane = lax.broadcasted_iota(jnp.int32, value.shape, 1)
    half = HD // 2
    other = jnp.where(
        lane % HD < half, pltpu.roll(value, 128 - half, 1), pltpu.roll(value, half, 1)
    )
    return value * cosine + other * sine


def turn_first(value, cosine, sine):
    lane = lax.broadcasted_iota(jnp.int32, value.shape, 1)
    return jnp.where(lane < HD, turn(value, cosine, sine), value)


def project_kernel(
    hidden, gain, weight, cosine, sine, normed_out, mix_out, query_out, key_value_out, step_out
):
    wide = hidden[...].astype(f32)
    scale = lax.rsqrt(jnp.mean(wide * wide, -1, keepdims=True) + EPSILON)
    normed = (wide * scale * gain[...]).astype(bf16)
    normed_out[...] = normed
    rows = product(normed, weight[...])
    mix_out[...] = rows[:, :MIXW].astype(bf16)
    at = MIXW
    query_out[...] = turn(rows[:, at : at + QW], cosine[...], sine[...]).astype(bf16)
    at += QW
    pair = turn_first(rows[:, at : at + 2 * HD], cosine[...], sine[...])
    key_value_out[...] = pair.astype(bf16)
    tail = rows[:, STEP_AT:]
    lane = lax.broadcasted_iota(jnp.int32, tail.shape, 1)
    step_out[...] = jnp.where(lane < SH, tail, 0.0)


def project(hidden, gain, weight, cosine, sine):
    count = hidden.shape[0]
    span = count // 2
    return call(
        project_kernel,
        (2,),
        [
            row_block(span, D),
            fixed(1, D),
            fixed(D, WIDE),
            fixed(span, 128),
            fixed(span, 128),
        ],
        [
            row_block(span, D),
            row_block(span, MIXW),
            row_block(span, QW),
            row_block(span, 128),
            row_block(span, 128),
        ],
        [
            shape(count, D, dtype=bf16),
            shape(count, MIXW, dtype=bf16),
            shape(count, QW, dtype=bf16),
            shape(count, 128, dtype=bf16),
            shape(count, 128),
        ],
    )(hidden, gain, weight, cosine, sine)


def visible_keys(span, keys, at):
    query = lax.broadcasted_iota(jnp.int32, (span, keys), 0)
    key = lax.broadcasted_iota(jnp.int32, (span, keys), 1)
    return (key < span) & (key <= query) | (key >= span) & (key < (at + 1) * span)


def attend_kernel(at, query, key_value, attended_out, total_out):
    span, keys = query.shape[0], key_value.shape[1]
    visible = visible_keys(span, keys, at[0])
    pair = key_value[0]
    for h in range(QW // HD):
        part = slice(h * HD, (h + 1) * HD)
        scores = product(query[:, part], pair[:, :HD], 1, 1) * HD ** (-0.5)
        scores = jnp.where(visible, scores, NEGATIVE)
        peak = jnp.max(scores, -1, keepdims=True)
        weights = jnp.exp(scores - peak)
        total = jnp.sum(weights, -1, keepdims=True)
        summed = product(weights.astype(bf16), pair[:, HD:])
        attended_out[:, part] = (summed / total).astype(bf16)
        total_out[:, part] = jnp.broadcast_to(peak + jnp.log(total), (span, HD))


def attend(at, query, key_values):
    count = query.shape[0]
    span = count // 2
    return call(
        attend_kernel,
        (2,),
        [SCALAR, row_block(span, QW), seq_block(*key_values.shape[1:])],
        [row_block(span, QW), row_block(span, QW)],
        [shape(count, QW, dtype=bf16), shape(count, QW)],
    )(at, query, key_values)


def attend_back_kernel(
    at, query, key_value, attended, log_total, back, cosine, sine, query_out, own_out, other_out
):
    span, keys = query.shape[0], key_value.shape[1]
    scale = HD ** (-0.5)
    visible = visible_keys(span, keys, at[0])
    pair = key_value[0]
    back_pair = jnp.zeros((keys, 2 * HD), f32)
    turned = []
    for h in range(QW // HD):
        part = slice(h * HD, (h + 1) * HD)
        head = query[:, part]
        upstream = back[:, part]
        delta = jnp.sum(
            upstream.astype(f32) * attended[:, part].astype(f32), -1, keepdims=True
        )
        scores = product(head, pair[:, :HD], 1, 1) * scale
        chance = jnp.where(visible, jnp.exp(scores - log_total[:, part][:, :1]), 0.0)
        back_chance = product(upstream, pair[:, HD:], 1, 1)
        back_scores = (chance * (back_chance - delta) * scale).astype(bf16)
        turned.append(product(back_scores, pair[:, :HD]))
        back_pair = back_pair + jnp.concatenate(
            [product(back_scores, head, 0, 0), product(chance.astype(bf16), upstream, 0, 0)], 1
        )
    query_out[...] = turn(jnp.concatenate(turned, 1), cosine[...], -sine[...]).astype(bf16)
    own_out[0] = back_pair[:span]
    other_out[0] = back_pair[span:].astype(bf16)


def attend_back(at, query, key_values, attended, log_total, back, cosine, sine):
    count = query.shape[0]
    span = count // 2
    keys = key_values.shape[1]
    return call(
        attend_back_kernel,
        (2,),
        [SCALAR, row_block(span, QW), seq_block(keys, 2 * HD)]
        + [row_block(span, QW)] * 3
        + [fixed(span, 128)] * 2,
        [row_block(span, QW), seq_block(span, 2 * HD), seq_block(keys - span, 2 * HD)],
        [
            shape(count, QW, dtype=bf16),
            shape(2, span, 2 * HD),
            shape(2, keys - span, 2 * HD, dtype=bf16),
        ],
    )(at, query, key_values, attended, log_total, back, cosine, sine)


LEAD = 8


def extend(scratch, rim, mix):
    scratch[0:LEAD] = rim[0].astype(f32)
    scratch[LEAD:] = mix[...].astype(f32)


def prep_kernel(rim, mix, step, taps, heads, conv_out, prep_out, turned_out, message_out, ext):
    rows = mix.shape[0]
    extend(ext, rim, mix)
    conv = taps[KW : KW + 1] + taps[0:1] * ext[pl.ds(LEAD - KW + 1, rows)]
    for tap in range(1, KW):
        conv = conv + taps[tap : tap + 1] * ext[pl.ds(LEAD - KW + 1 + tap, rows)]
    conv = conv / (1.0 + jnp.exp(-conv))
    conv_out[...] = conv
    lane = lax.broadcasted_iota(jnp.int32, step.shape, 1)
    raw = step[...] + heads[0:1]
    steps = jnp.maximum(raw, 0.0) + jnp.log1p(jnp.exp(-jnp.abs(raw)))
    steps = jnp.where(lane < SH, steps, 0.0)
    rate = -jnp.exp(heads[1:2]) * steps
    below = lax.broadcasted_iota(jnp.int32, (rows, rows), 0)
    along = lax.broadcasted_iota(jnp.int32, (rows, rows), 1)
    lower = jnp.where(below >= along, 1.0, 0.0)
    curve = lax.dot_general(
        lower, rate, (((1,), (0,)), ((), ())), precision=HIGHEST, preferred_element_type=f32
    )
    prep_out[:, :128] = steps
    prep_out[:, 128:] = curve
    turned_out[0, :8] = steps.T[:8]
    turned_out[0, 8:] = curve.T[:8]
    last = curve[rows - 1 : rows]
    weights = jnp.exp(last - curve) * steps
    mask = head_mask()
    scaled = spread_heads(weights, mask) * conv[:, :SW]
    state = fine_product(scaled, conv[:, SW : SW + NS], 0, 0)
    message_out[0, :SW] = state.astype(bf16)
    high = last.astype(bf16)
    low = (last - high.astype(f32)).astype(bf16)
    row = lax.broadcasted_iota(jnp.int32, (16, 128), 0)
    tail = jnp.where(row == 0, high.astype(f32), jnp.where(row == 1, low.astype(f32), 0.0))
    message_out[0, SW:] = tail.astype(bf16)


def prep(rim, mix, step, taps, heads):
    count = mix.shape[0]
    rows = count // 2
    return call(
        prep_kernel,
        (2,),
        [
            seq_block(LEAD, MIXW),
            row_block(rows, MIXW),
            row_block(rows, 128),
            fixed(8, MIXW),
            fixed(8, 128),
        ],
        [
            row_block(rows, MIXW),
            row_block(rows, 256),
            seq_block(16, rows),
            seq_block(SW + 16, NS),
        ],
        [
            shape(count, MIXW),
            shape(count, 256),
            shape(2, 16, rows),
            shape(2, SW + 16, NS, dtype=bf16),
        ],
        [pltpu.VMEM((LEAD + rows, MIXW), f32)],
    )(rim, mix, step, taps, heads)


def head_column(tail):
    row = lax.broadcasted_iota(jnp.int32, (SW, 128), 0)
    lane = lax.broadcasted_iota(jnp.int32, (SW, 128), 1)
    return jnp.sum(jnp.where(row // MP == lane, tail, 0.0), 1, keepdims=True)


def decay_of(message, at):
    return message[0, at : at + 1].astype(f32) + message[0, at + 1 : at + 2].astype(f32)


def scan_kernel(
    parts, normed, gate_weight, conv, prep, turned, skip, *refs
):
    messages = refs[:parts]
    gate_out, mixed_out, state_out, square_out = refs[parts:]
    rows = conv.shape[0]
    gate = product(normed[...], gate_weight[...])
    gate_out[...] = gate
    between = jnp.zeros((1, 128), f32)
    state = jnp.zeros((SW, NS), f32)
    for message in messages:
        state = state + jnp.exp(head_column(between)) * message[0, :SW].astype(f32)
        between = between + decay_of(message, SW)
    state_out[0] = state
    entry = conv[:, SW : SW + NS]
    readout = conv[:, SW + NS :]
    meeting = fine_product(readout, entry, 1, 1)
    below = lax.broadcasted_iota(jnp.int32, (rows, rows), 0)
    along = lax.broadcasted_iota(jnp.int32, (rows, rows), 1)
    causal = below >= along
    meeting = jnp.where(causal, meeting, 0.0)
    parts_out = []
    for h in range(SH):
        spread = prep[:, 128 + h : 129 + h] - turned[0, 8 + h : 9 + h]
        mixing = jnp.exp(jnp.where(causal, spread, 0.0)) * meeting * turned[0, h : h + 1]
        signal = conv[:, MP * h : MP * (h + 1)].astype(bf16)
        parts_out.append(product(mixing.astype(bf16), signal))
    signal = conv[:, :SW]
    carried = fine_product(readout, state, 1, 1)
    grown = spread_heads(jnp.exp(prep[:, 128:]), head_mask())
    mixed = jnp.concatenate(parts_out, 1) + carried * grown + skip[...] * signal
    mixed_out[...] = mixed
    gated = mixed * gate / (1.0 + jnp.exp(-gate))
    square_out[...] = jnp.broadcast_to(jnp.sum(gated * gated, 1, keepdims=True), (rows, 128))


def scan(normed, feed, conv, prepared, turned, skip, messages):
    count = conv.shape[0]
    rows = count // 2
    return call(
        lambda *refs: scan_kernel(len(messages), *refs),
        (2,),
        [
            row_block(rows, D),
            fixed(D, SW),
            row_block(rows, MIXW),
            row_block(rows, 256),
            seq_block(16, rows),
            fixed(1, SW),
        ]
        + [seq_block(SW + 16, NS)] * len(messages),
        [
            row_block(rows, SW),
            row_block(rows, SW),
            seq_block(SW, NS),
            row_block(rows, 128),
        ],
        [shape(count, SW), shape(count, SW), shape(2, SW, NS), shape(count, 128)],
    )(normed, feed, conv, prepared, turned, skip, *messages)


def scan_back_kernel(parts, back, conv, prep, turned, skip, state, *refs):
    tails = refs[:parts]
    conv_out, prep_out, skip_out = refs[parts : parts + 3]
    sent_out = refs[parts + 3 :]
    rows = conv.shape[0]
    mask = head_mask()
    entry = conv[:, SW : SW + NS]
    readout = conv[:, SW + NS :]
    signal = conv[:, :SW]
    upstream = back[...]
    meeting = fine_product(readout, entry, 1, 1)
    below = lax.broadcasted_iota(jnp.int32, (rows, rows), 0)
    along = lax.broadcasted_iota(jnp.int32, (rows, rows), 1)
    causal = below >= along
    back_meeting = jnp.zeros((rows, rows), f32)
    lane = lax.broadcasted_iota(jnp.int32, (rows, 128), 1)
    place = lax.broadcasted_iota(jnp.int32, (8, rows), 0)
    back_steps = jnp.zeros((8, rows), f32)
    curve_along = jnp.zeros((8, rows), f32)
    back_curve = jnp.zeros((rows, 128), f32)
    back_signal = []
    for h in range(SH):
        part = slice(MP * h, MP * (h + 1))
        spread = prep[:, 128 + h : 129 + h] - turned[0, 8 + h : 9 + h]
        decay = jnp.where(causal, jnp.exp(jnp.where(causal, spread, 0.0)), 0.0)
        step = turned[0, h : h + 1]
        head_back = upstream[:, part].astype(bf16)
        back_mixing = product(head_back, signal[:, part].astype(bf16), 1, 1) * decay
        back_meeting = back_meeting + back_mixing * step
        scaled = back_mixing * meeting
        down = jnp.sum(scaled, 0, keepdims=True)
        across = jnp.sum(scaled * step, 1, keepdims=True)
        back_steps = jnp.where(place == h, down, back_steps)
        curve_along = jnp.where(place == h, -down * step, curve_along)
        back_curve = jnp.where(lane == h, across, back_curve)
        mixing = (decay * meeting * step).astype(bf16)
        back_signal.append(product(mixing, head_back, 0, 0))
    fold = jnp.concatenate([back_steps, curve_along, jnp.zeros((112, rows), f32)], 0).T
    grown = spread_heads(jnp.exp(prep[:, 128:]), mask)
    back_carried = upstream * grown
    carried = fine_product(readout, state[0], 1, 1)
    back_curve = back_curve + sum_heads(back_carried * carried, mask)
    back_curve = back_curve + jnp.where(lane < SH, pltpu.roll(fold, 120, 1), 0.0)
    conv_out[:, :SW] = jnp.concatenate(back_signal, 1) + skip[...] * upstream
    conv_out[:, SW : SW + NS] = fine_product(back_meeting, readout, 0, 0)
    conv_out[:, SW + NS :] = fine_product(back_meeting, entry) + fine_product(
        back_carried, state[0]
    )
    prep_out[:, :128] = jnp.where(lane < SH, fold, 0.0)
    prep_out[:, 128:] = back_curve
    back_skip = jnp.sum(upstream * signal, 0, keepdims=True)
    skip_out[0] = jnp.broadcast_to(sum_heads(jnp.broadcast_to(back_skip, (8, SW)), mask), (8, 128))
    back_state = fine_product(back_carried, readout, 0, 0)
    between = jnp.zeros((1, 128), f32)
    for tail, sent in zip(tails, sent_out):
        sent[0] = (jnp.exp(head_column(between)) * back_state).astype(bf16)
        between = between + decay_of(tail, 0)


def scan_back(back, conv, prepared, turned, skip, state, messages):
    count = conv.shape[0]
    rows = count // 2
    tail = pl.BlockSpec((1, 16, NS), lambda b: (b, SW // 16, 0))
    return call(
        lambda *refs: scan_back_kernel(len(messages), *refs),
        (2,),
        [
            row_block(rows, SW),
            row_block(rows, MIXW),
            row_block(rows, 256),
            seq_block(16, rows),
            fixed(1, SW),
            seq_block(SW, NS),
        ]
        + [tail] * len(messages),
        [row_block(rows, MIXW), row_block(rows, 256), seq_block(8, 128)]
        + [seq_block(SW, NS)] * len(messages),
        [shape(count, MIXW), shape(count, 256), shape(2, 8, 128)]
        + [shape(2, SW, NS, dtype=bf16)] * len(messages),
    )(back, conv, prepared, turned, skip, state, *messages)


def prep_back_kernel(
    parts,
    rim,
    mix,
    step,
    taps,
    heads,
    conv,
    prep,
    state,
    back_conv,
    back_prep,
    back_skip,
    *refs,
):
    received = refs[:parts]
    mix_out, step_out, rim_out, tap_out, head_out, ext, padded = refs[parts:]
    rows = mix.shape[0]
    mask = head_mask()
    next_back = jnp.zeros((SW, NS), f32)
    for piece in received:
        next_back = next_back + piece[0].astype(f32)
    steps, curve = prep[:, :128], prep[:, 128:]
    last = curve[rows - 1 : rows]
    decay = jnp.exp(last - curve)
    wide = spread_heads(decay * steps, mask)
    signal = conv[:, :SW]
    entry = conv[:, SW : SW + NS]
    back_scaled = fine_product(entry, next_back, 1, 1)
    back_weights = sum_heads(back_scaled * signal, mask)
    both = back_weights * decay
    back_steps = back_prep[:, :128] + both
    weighed = both * steps
    whole = jnp.sum(next_back * state[0], 1, keepdims=True)
    row = lax.broadcasted_iota(jnp.int32, (SW, 128), 0)
    lane = lax.broadcasted_iota(jnp.int32, (SW, 128), 1)
    whole = jnp.sum(jnp.where(row // MP == lane, whole, 0.0), 0, keepdims=True) * jnp.exp(last)
    at_last = lax.broadcasted_iota(jnp.int32, (rows, 128), 0) == rows - 1
    back_curve = back_prep[:, 128:] - weighed
    back_curve = back_curve + jnp.where(
        at_last, jnp.sum(weighed, 0, keepdims=True) + whole, 0.0
    )
    below = lax.broadcasted_iota(jnp.int32, (rows, rows), 0)
    along = lax.broadcasted_iota(jnp.int32, (rows, rows), 1)
    upper = jnp.where(below <= along, 1.0, 0.0)
    back_rate = lax.dot_general(
        upper, back_curve, (((1,), (0,)), ((), ())), precision=HIGHEST, preferred_element_type=f32
    )
    pace = -jnp.exp(heads[1:2])
    back_decay = jnp.sum(back_rate * pace * steps, 0, keepdims=True)
    raw = step[...] + heads[0:1]
    back_steps = (back_steps + back_rate * pace) / (1.0 + jnp.exp(-raw))
    wide_lane = lax.broadcasted_iota(jnp.int32, (rows, 128), 1)
    back_steps = jnp.where(wide_lane < SH, back_steps, 0.0)
    step_out[...] = back_steps
    place = lax.broadcasted_iota(jnp.int32, (8, 128), 0)
    total = jnp.where(place == 0, jnp.sum(back_steps, 0, keepdims=True), 0.0)
    total = jnp.where(place == 1, back_decay, total)
    head_out[0] = jnp.where(place == 2, back_skip[0], total)

    extend(ext, rim, mix)
    before = taps[KW : KW + 1] + taps[0:1] * ext[pl.ds(LEAD - KW + 1, rows)]
    for tap in range(1, KW):
        before = before + taps[tap : tap + 1] * ext[pl.ds(LEAD - KW + 1 + tap, rows)]
    sigmoid = 1.0 / (1.0 + jnp.exp(-before))
    slope = sigmoid * (1.0 + before * (1.0 - sigmoid))
    scaled = wide * signal
    upstream = jnp.concatenate(
        [
            back_conv[:, :SW] + back_scaled * wide,
            back_conv[:, SW : SW + NS] + fine_product(scaled, next_back),
            back_conv[:, SW + NS :],
        ],
        1,
    )
    back = upstream * slope
    place = lax.broadcasted_iota(jnp.int32, (8, MIXW), 0)
    sums = jnp.where(place == KW, jnp.sum(back, 0, keepdims=True), 0.0)
    for tap in range(KW):
        moved = jnp.sum(back * ext[pl.ds(LEAD - KW + 1 + tap, rows)], 0, keepdims=True)
        sums = jnp.where(place == tap, moved, sums)
    tap_out[0] = sums
    padded[0:LEAD] = jnp.zeros((LEAD, MIXW), f32)
    padded[LEAD : LEAD + rows] = back
    padded[LEAD + rows :] = jnp.zeros((LEAD, MIXW), f32)
    result = taps[KW - 1 : KW] * back
    first = jnp.zeros((LEAD, MIXW), f32)
    for tap in range(KW):
        if tap < KW - 1:
            result = result + taps[tap : tap + 1] * padded[pl.ds(LEAD + KW - 1 - tap, rows)]
        first = first + taps[tap : tap + 1] * padded[pl.ds(LEAD - tap, LEAD)]
    mix_out[...] = result
    rim_out[0] = jnp.where(place < KW - 1, first, 0.0)


def prep_back(rim, mix, step, taps, heads, conv, prepared, state, back_conv, back_prep, back_skip, received):
    count = mix.shape[0]
    rows = count // 2
    return call(
        lambda *refs: prep_back_kernel(len(received), *refs),
        (2,),
        [
            seq_block(LEAD, MIXW),
            row_block(rows, MIXW),
            row_block(rows, 128),
            fixed(8, MIXW),
            fixed(8, 128),
            row_block(rows, MIXW),
            row_block(rows, 256),
            seq_block(SW, NS),
            row_block(rows, MIXW),
            row_block(rows, 256),
            seq_block(8, 128),
        ]
        + [seq_block(SW, NS)] * len(received),
        [
            row_block(rows, MIXW),
            row_block(rows, 128),
            seq_block(LEAD, MIXW),
            seq_block(8, MIXW),
            seq_block(8, 128),
        ],
        [
            shape(count, MIXW),
            shape(count, 128),
            shape(2, LEAD, MIXW),
            shape(2, 8, MIXW),
            shape(2, 8, 128),
        ],
        [
            pltpu.VMEM((LEAD + rows, MIXW), f32),
            pltpu.VMEM((rows + 2 * LEAD, MIXW), f32),
        ],
    )(
        rim,
        mix,
        step,
        taps,
        heads,
        conv,
        prepared,
        state,
        back_conv,
        back_prep,
        back_skip,
        *received,
    )


def assemble_kernel(parts, gate, mix, rim, step, query, own, cosine, sine, *refs):
    received, out = refs[:parts], refs[parts]
    rows = mix.shape[0]
    out[:, :SW] = gate[...]
    mixed = slice(SW, SW + MIXW)
    out[:, mixed] = mix[...].astype(bf16)
    tail = mix[rows - 16 :]
    returned = jnp.concatenate([jnp.zeros((16 - LEAD, MIXW), f32), rim[0]], 0)
    tail = tail + pltpu.roll(returned, LEAD - KW + 1, 0)
    out[rows - 16 :, mixed] = tail.astype(bf16)
    at = SW + MIXW
    out[:, at : at + QW] = query[...]
    pair = own[0]
    for piece in received:
        pair = pair + piece[0].astype(f32)
    at += QW
    out[:, at : at + 2 * HD] = turn_first(pair, cosine[...], -sine[...]).astype(bf16)
    out[:, SW + STEP_AT :] = step[...].astype(bf16)


def assemble(gate, mix, rim, step, query, own, received, cosine, sine):
    count = mix.shape[0]
    rows = count // 2
    return call(
        lambda *refs: assemble_kernel(len(received), *refs),
        (2,),
        [
            row_block(rows, SW),
            row_block(rows, MIXW),
            seq_block(LEAD, MIXW),
            row_block(rows, 128),
            row_block(rows, QW),
            seq_block(rows, 2 * HD),
            fixed(rows, 128),
            fixed(rows, 128),
        ]
        + [seq_block(rows, 2 * HD)] * len(received),
        row_block(rows, SW + WIDE),
        shape(count, SW + WIDE, dtype=bf16),
    )(gate, mix, rim, step, query, own, cosine, sine, *received)


def sums_kernel(first_left, first_right, second_left, second_right, out):
    width = first_right.shape[1]
    out[:, :width] = product(first_left[...], first_right[...], 0, 0).astype(bf16)
    out[:, width:] = product(second_left[...], second_right[...], 0, 0).astype(bf16)


def weight_sums(first_left, first_right, second_left, second_right):
    count = first_left.shape[0]
    wide, more = first_right.shape[1], second_right.shape[1]
    rows = 256
    left = pl.BlockSpec((count, rows), lambda b: (0, b))
    return call(
        sums_kernel,
        (D // rows,),
        [left, fixed(count, wide), left, fixed(count, more)],
        row_block(rows, wide + more),
        shape(D, wide + more, dtype=bf16),
    )(first_left, first_right, second_left, second_right)


def local(
    tokens,
    out_cotangent,
    input_gain,
    mamba_gate_weight,
    mamba_mix_weight,
    mamba_step_weight,
    conv_kernel,
    conv_offset,
    step_offset,
    decay_log,
    skip_scale,
    mamba_norm_gain,
    mamba_out_weight,
    query_weight,
    key_weight,
    value_weight,
    attention_out_weight,
    ffn_gain,
    feed_gate_weight,
    feed_up_weight,
    feed_down_weight,
):
    rows = tokens.shape[1]
    span = 2 * rows
    count = 2 * span
    pairs, spans = lax.axis_size("dp") // 2, lax.axis_size("ctx") // 2
    devices = 4 * pairs * spans
    dp_at, ctx_at = lax.axis_index("dp"), lax.axis_index("ctx")
    side, span_at = ctx_at % 2, ctx_at // 2
    rank = (dp_at % 2) * 2 + side
    part = D // devices
    conv_part = CONV // devices
    gain_part = DSSM // devices
    groups = [
        [(y * 2 + c) * 2 * spans + z * 2 + x for y in range(pairs) for z in range(spans)]
        for c in range(2)
        for x in range(2)
    ]

    def order(value):
        lead = value.shape[:-1]
        value = value.reshape(*lead, pairs, 2, spans, 2 * part)
        return jnp.swapaxes(value, -3, -2).reshape(*lead, D)

    def disorder(value):
        lead = value.shape[:-1]
        value = value.reshape(*lead, pairs, spans, 2, 2 * part)
        return jnp.swapaxes(value, -3, -2).reshape(*lead, D)

    def gather(value):
        return lax.all_gather(value, BOTH, axis=0, tiled=True, axis_index_groups=groups)

    def scatter(value):
        return lax.psum_scatter(
            value, BOTH, scatter_dimension=0, tiled=True, axis_index_groups=groups
        )

    vector = jnp.concatenate(
        [
            input_gain,
            ffn_gain,
            conv_kernel.reshape(-1),
            conv_offset,
            mamba_norm_gain,
        ]
    )
    vector = jnp.pad(vector, (0, part * VEC - vector.shape[0])).reshape(part, VEC)

    def mixer_part(s):
        kv = s // 2
        return jnp.concatenate(
            [
                mamba_mix_weight[:, SW * s : SW * (s + 1)],
                mamba_mix_weight[:, DSSM:],
                query_weight[:, QW * s : QW * (s + 1)],
                key_weight[:, HD * kv : HD * (kv + 1)],
                value_weight[:, HD * kv : HD * (kv + 1)],
                mamba_step_weight[:, SH * s : SH * (s + 1)],
                vector,
                jnp.zeros((part, WIDE - STEP_AT - SH - VEC), bf16),
            ],
            1,
        )

    mamba_out_turned = mamba_out_weight.T
    attention_out_turned = attention_out_weight.T
    feed_down_turned = feed_down_weight.T

    def feed_part(s):
        return jnp.concatenate(
            [
                mamba_gate_weight[:, SW * s : SW * (s + 1)],
                mamba_out_turned[:, SW * s : SW * (s + 1)],
                attention_out_turned[:, QW * s : QW * (s + 1)],
                feed_gate_weight[:, FW * s : FW * (s + 1)],
                feed_up_weight[:, FW * s : FW * (s + 1)],
                feed_down_turned[:, FW * s : FW * (s + 1)],
            ],
            1,
        )

    mixer_own = group_swap(jnp.stack([mixer_part(s) for s in range(TP)]), rank)
    mixer = gather(mixer_own.reshape(TP * part, WIDE))
    feed_own = group_swap(jnp.stack([feed_part(s) for s in range(TP)]), rank)
    own_low = order(tokens[0])
    own_hidden = own_low.astype(f32)
    own_scale_one = lax.rsqrt(jnp.mean(own_hidden * own_hidden, -1, keepdims=True) + EPSILON)
    hidden = group_gather(own_low, side)
    own_cotangent = order(out_cotangent[0])
    upstream = group_gather(own_cotangent, side)
    cosine, sine = rope_tables(span_at * span + jnp.arange(span, dtype=jnp.int32))
    feed_own, mixer, hidden, upstream, cosine, sine = lax.optimization_barrier(
        (feed_own, mixer, hidden, upstream, cosine, sine)
    )
    feed_own = feed_own.reshape(TP * part, feed_own.shape[-1])
    branch = gather(feed_own[:, : 2 * SW + QW])
    feed = gather(feed_own[:, 2 * SW + QW :])
    full_gate = branch[:, :SW]
    full_out = branch[:, SW:]
    full_gate_up = feed[:, : 2 * FW]
    full_down = feed[:, 2 * FW :]

    vectors = mixer[:, STEP_AT + SH : STEP_AT + SH + VEC].reshape(devices, part * VEC)
    full_gain = vectors[:, :part].reshape(D).astype(f32)
    full_gain_two = vectors[:, part : 2 * part].reshape(D).astype(f32)
    natural = vectors.reshape(pairs, spans, 2, 2, part * VEC)
    natural = natural.transpose(0, 2, 1, 3, 4).reshape(devices, part * VEC)
    at = 2 * part
    all_kernel = natural[:, at : at + KW * conv_part].reshape(devices, KW, conv_part)
    all_kernel = all_kernel.transpose(1, 0, 2).reshape(KW, CONV)
    at += KW * conv_part
    all_offset = natural[:, at : at + conv_part].reshape(1, CONV)
    at += conv_part
    all_mamba_gain = natural[:, at : at + gain_part].reshape(DSSM)
    taps = jnp.concatenate([all_kernel, all_offset], 0)
    taps = jnp.concatenate(
        [lax.dynamic_slice_in_dim(taps, rank * SW, SW, 1), taps[:, DSSM:]], 1
    ).astype(f32)
    kernel, offset = taps[:KW], taps[KW]
    mamba_gain = lax.dynamic_slice_in_dim(all_mamba_gain, rank * SW, SW, 0).astype(f32)
    own_step_offset = lax.dynamic_slice_in_dim(step_offset, rank * SH, SH, 0)
    own_decay_log = lax.dynamic_slice_in_dim(decay_log, rank * SH, SH, 0)
    own_skip = lax.dynamic_slice_in_dim(skip_scale, rank * SH, SH, 0)

    at = jnp.reshape(span_at, (1,)).astype(jnp.int32)
    taps = jnp.pad(taps, ((0, 8 - taps.shape[0]), (0, 0)))
    heads = jnp.stack([own_step_offset, own_decay_log])
    heads = jnp.pad(heads, ((0, 6), (0, 128 - SH)))
    skip = jnp.repeat(own_skip, MP)[None]

    low_normed, mix_rows, query, key_value, step_rows = project(
        hidden, full_gain[None], mixer, cosine, sine
    )
    rim = mix_rows.reshape(2, span, MIXW)[:, span - LEAD :]
    rim = move_spans(rim, 1)
    key_value = key_value.reshape(2, span, 2 * HD)
    reached = [key_value] + [move_spans(key_value, s) for s in range(1, spans)]
    key_values = jnp.concatenate(reached, 1)
    conv, prepared, turned, message = prep(rim, mix_rows, step_rows, taps, heads)
    messages = [move_spans(message, s) for s in range(1, spans)]
    attended, log_total = attend(at, query, key_values)
    gate_rows, mixed, state_in, square = scan(
        low_normed, branch, conv, prepared, turned, skip, messages
    )
    square = group_sum(square[:, 0])
    mamba_scale = lax.rsqrt(square / DSSM + EPSILON)[:, None]
    gate_sigmoid = jax.nn.sigmoid(gate_rows)
    gate_silu = gate_rows * gate_sigmoid
    gated = mixed * gate_silu
    mamba_rows = (gated * mamba_scale * mamba_gain).astype(bf16)
    branches = jnp.concatenate([mamba_rows, attended], 1)
    middle = own_hidden + group_scatter(input_product(branches, full_out), side)

    scale_two = lax.rsqrt(jnp.mean(middle * middle, -1, keepdims=True) + EPSILON)
    low_two = group_gather((middle * scale_two * full_gain_two).astype(bf16), side)
    pre = forward_product(low_two, full_gate_up)
    gate_pre, up_pre = pre[:, :FW], pre[:, FW:]
    sigmoid = jax.nn.sigmoid(gate_pre)
    silu = gate_pre * sigmoid
    activation = (silu * up_pre).astype(bf16)

    back_activation = forward_product(upstream, full_down)
    back_gate = (back_activation * up_pre * sigmoid * (1.0 + gate_pre * (1.0 - sigmoid))).astype(
        bf16
    )
    back_up = (back_activation * silu).astype(bf16)
    back_feed = jnp.concatenate([back_gate, back_up], 1)
    feed_sums = weight_sums(low_two, back_feed, upstream, activation)
    back_feed, feed_sums = lax.optimization_barrier((back_feed, feed_sums))
    gradient_feed = scatter(feed_sums)
    back_normed_two = group_scatter(input_product(back_feed, full_gate_up), side)
    weighted = back_normed_two * full_gain_two
    gradient_gain_two = jnp.sum(back_normed_two * middle * scale_two, 0)
    back_middle = (
        own_cotangent.astype(f32)
        + scale_two * weighted
        - middle * scale_two**3 * jnp.mean(weighted * middle, -1, keepdims=True)
    )
    low_middle = group_gather(back_middle.astype(bf16), side)

    layer_out = middle + group_scatter(input_product(activation, full_down), side)

    back_branches = forward_product(low_middle, full_out)
    back_attended = back_branches[:, SW:].astype(bf16)
    back_rows = back_branches[:, :SW]
    weighted = back_rows * mamba_gain
    gradient_mamba_gain = jnp.sum(back_rows * gated * mamba_scale, 0)
    mean = group_sum(jnp.sum(weighted * gated, -1))[:, None] / DSSM
    back_gated = mamba_scale * weighted - gated * mamba_scale**3 * mean
    back_mixed = back_gated * gate_silu
    low_gate = (
        back_gated * mixed * gate_sigmoid * (1.0 + gate_rows * (1.0 - gate_sigmoid))
    ).astype(bf16)
    back_conv, back_prep, back_skip, *sent = scan_back(
        back_mixed, conv, prepared, turned, skip, state_in, messages
    )
    received = [move_spans(piece, -s) for s, piece in zip(range(1, spans), sent)]
    back_query, own_back, other_back = attend_back(
        at, query, key_values, attended, log_total, back_attended, cosine, sine
    )
    other_back = other_back.reshape(2, spans - 1, span, 2 * HD)
    pieces = [move_spans(other_back[:, s - 1], -s) for s in range(1, spans)]
    back_mix, back_step, back_rim, tap_sums, head_sums = prep_back(
        rim,
        mix_rows,
        step_rows,
        taps,
        heads,
        conv,
        prepared,
        state_in,
        back_conv,
        back_prep,
        back_skip,
        received,
    )
    back_rim = move_spans(back_rim, -1)
    back_all = assemble(
        low_gate, back_mix, back_rim, back_step, back_query, own_back, pieces, cosine, sine
    )
    back_all, gradient_feed = lax.optimization_barrier((back_all, gradient_feed))
    gradient_mixer = scatter(weight_sums(low_normed, back_all, low_middle, branches))
    back_normed = group_scatter(
        input_product(back_all[:, :SW], full_gate) + input_product(back_all[:, SW:], mixer), side
    )
    weighted = back_normed * full_gain
    gradient_gain_one = jnp.sum(back_normed * own_hidden * own_scale_one, 0)
    input_gradient = (
        back_middle
        + own_scale_one * weighted
        - own_hidden * own_scale_one**3 * jnp.mean(weighted * own_hidden, -1, keepdims=True)
    )

    def placed(value, width):
        wide = jnp.zeros(value.shape[:-1] + (width,), f32)
        return lax.dynamic_update_slice_in_dim(
            wide, value, rank * value.shape[-1], value.ndim - 1
        )

    tap_grads = jnp.sum(tap_sums, 0)[: KW + 1]
    tap_grads = jnp.concatenate([placed(tap_grads[:, :SW], DSSM), tap_grads[:, SW:]], 1)
    head_grads = jnp.sum(head_sums, 0)[:3, :SH]
    gain_grads, tap_grads, mamba_gain_grad, head_grads = lax.psum(
        (
            jnp.stack([gradient_gain_one, gradient_gain_two]),
            tap_grads,
            placed(gradient_mamba_gain, DSSM),
            placed(head_grads, MH),
        ),
        BOTH,
    )
    feature_at = ((dp_at // 2 * spans + span_at) * TP + rank) * part
    own_gains = lax.dynamic_slice_in_dim(gain_grads, feature_at, part, 1)
    device_at = dp_at * 2 * spans + ctx_at
    own_taps = lax.dynamic_slice_in_dim(tap_grads, device_at * conv_part, conv_part, 1)
    own_mamba_gain = lax.dynamic_slice_in_dim(
        mamba_gain_grad, device_at * gain_part, gain_part, 0
    )

    feed_parts = group_swap(gradient_feed.reshape(TP, part, 3 * FW), rank).astype(f32)
    mixer_parts = group_swap(gradient_mixer.reshape(TP, part, -1), rank).astype(f32)

    def columns(parts, start, width):
        piece = parts[:, :, start : start + width]
        return piece.transpose(1, 0, 2).reshape(part, TP * width)

    def shared(start):
        piece = mixer_parts[:, :, start : start + HD].reshape(KVH, TP // KVH, part, HD)
        return jnp.sum(piece, 1).transpose(1, 0, 2).reshape(part, KVH * HD)

    at = SW + MIXW
    step_at = SW + STEP_AT
    mix_gradient = jnp.concatenate(
        [
            columns(mixer_parts, SW, SW),
            jnp.sum(mixer_parts[:, :, 2 * SW : SW + MIXW], 0),
        ],
        1,
    )
    return (
        disorder(layer_out.astype(bf16))[None],
        disorder(input_gradient)[None],
        own_gains[0],
        columns(mixer_parts, 0, SW),
        mix_gradient,
        columns(mixer_parts, step_at, SH),
        own_taps[:KW],
        own_taps[KW],
        head_grads[0],
        head_grads[1],
        head_grads[2],
        own_mamba_gain,
        columns(mixer_parts, SW + WIDE, SW).T,
        columns(mixer_parts, at, QW),
        shared(at + QW),
        shared(at + QW + HD),
        columns(mixer_parts, 2 * SW + WIDE, QW).T,
        own_gains[1],
        columns(feed_parts, 0, FW),
        columns(feed_parts, FW, FW),
        columns(feed_parts, 2 * FW, FW).T,
    )


def solution(mesh):
    both = BOTH
    tokens = P("dp", "ctx", None)
    first = P(both, None)
    second = P(None, both)
    vector = P(both)
    whole = P()
    weights = (
        vector,
        first,
        first,
        first,
        second,
        vector,
        whole,
        whole,
        whole,
        vector,
        second,
        first,
        first,
        first,
        second,
        vector,
        first,
        first,
        second,
    )
    return jax.shard_map(
        local,
        mesh=mesh,
        in_specs=(tokens, tokens) + weights,
        out_specs=(tokens, tokens) + weights,
        check_vma=False,
    )
```

```python
import jax
import jax.numpy as jnp
from jax import lax
from jax.experimental import pallas as pl
from jax.experimental.pallas import tpu as pltpu
from jax.sharding import PartitionSpec as P

D = 1024
DSSM = 1536
MH = 24
MP = 64
NS = 128
KW = 4
AH = 8
KVH = 2
HD = 64
FF = 2048
CONV = DSSM + 2 * NS

TP = 4
SW = DSSM // TP
SH = MH // TP
QW = AH * HD // TP
FEED = 8
FW = FF // FEED
MIXW = SW + 2 * NS
STEP_AT = MIXW + QW + 2 * HD
VEC = 16
WIDE = 1024
FULL = WIDE + SW

EPSILON = 1e-05
ROPE_BASE = 100000000000.0
HIGHEST = lax.Precision.HIGHEST
NEGATIVE = -1e30
BOTH = ("dp", "ctx")
bf16 = jnp.bfloat16
f32 = jnp.float32


def forward_product(left, right):
    return jnp.dot(left, right, preferred_element_type=f32)


def input_product(upstream, weight):
    return lax.dot_general(
        upstream, weight, (((1,), (1,)), ((), ())), preferred_element_type=f32
    )


def swap_core(value):
    pairs = [(i, i ^ 1) for i in range(lax.axis_size("dp"))]
    return lax.ppermute(value, "dp", pairs)


def swap_side(value):
    pairs = [(i, i ^ 1) for i in range(lax.axis_size("ctx"))]
    return lax.ppermute(value, "ctx", pairs)


def swap_pair(value):
    pairs = [(i, i ^ 2) for i in range(lax.axis_size("dp"))]
    return lax.ppermute(value, "dp", pairs)


def move_spans(value, by):
    blocks = lax.axis_size("ctx")
    pairs = [(i, i + 2 * by) for i in range(blocks) if 0 <= i + 2 * by < blocks]
    return lax.ppermute(value, "ctx", pairs)


def group_gather(value, side):
    other = swap_side(value)
    first = side == 0
    mine = jnp.concatenate([jnp.where(first, value, other), jnp.where(first, other, value)], 0)
    return jnp.concatenate([mine, swap_core(mine)], 0)


def group_scatter(partial, side):
    span = partial.shape[0] // 2
    rows = span // 2
    mine = partial[:span] + swap_core(partial[span:])
    first = side == 0
    keep = jnp.where(first, mine[:rows], mine[rows:])
    send = jnp.where(first, mine[rows:], mine[:rows]).astype(bf16)
    return keep + swap_side(send).astype(f32)


def group_sum(value):
    span = value.shape[0] // 2
    other = swap_core(value)
    value = value + jnp.concatenate([other[span:], other[:span]], 0)
    return value + swap_side(value)


def exchange(parts, axis, bit, swap):
    first = lax.index_in_dim(parts, 0, axis, keepdims=False)
    second = lax.index_in_dim(parts, 1, axis, keepdims=False)
    low = bit == 0
    keep = jnp.where(low, first, second)
    other = swap(jnp.where(low, second, first))
    return jnp.stack([jnp.where(low, keep, other), jnp.where(low, other, keep)], axis)


def group_swap(parts, core, side):
    split = parts.reshape(2, 2, *parts.shape[1:])
    split = exchange(exchange(split, 0, core, swap_core), 1, side, swap_side)
    return split.reshape(parts.shape)


def feed_swap(parts, pair, core, side):
    split = parts.reshape(2, 2, 2, *parts.shape[1:])
    split = exchange(exchange(split, 1, core, swap_core), 2, side, swap_side)
    return exchange(split, 0, pair, swap_pair).reshape(parts.shape)


def both(first, second):
    return lax.optimization_barrier((first, second))


def feed_gather(value):
    half = value.shape[0] // 2
    first, second = value[:half], value[half:]
    first_other, second_other = both(swap_side(first), swap_pair(second))
    first_pair = jnp.concatenate([first, first_other], 0)
    second_pair = jnp.concatenate([second, second_other], 0)
    first_other, second_other = both(swap_pair(first_pair), swap_side(second_pair))
    mine = jnp.concatenate([first_pair, first_other, second_pair, second_other], 0)
    return jnp.concatenate([mine, swap_core(mine)], 0)


def feed_gather_slow(value):
    half = value.shape[0] // 2
    row = jnp.stack([value, swap_side(value)])
    square = jnp.stack([row, swap_pair(row)])
    first = square[:, :, :half].reshape(4 * half, -1)
    second = square[:, :, half:].swapaxes(0, 1).reshape(4 * half, -1)
    mine = jnp.concatenate([first, second], 0)
    return jnp.concatenate([mine, swap_core(mine)], 0)


def feed_scatter(own, other):
    part = own.shape[0] // 4

    def meet(first, second, first_swap, second_swap):
        rows = first.shape[0] // 2
        first_other, second_other = both(
            first_swap(first[rows:].astype(bf16)), second_swap(second[rows:].astype(bf16))
        )
        return (
            first[:rows] + first_other.astype(f32),
            second[:rows] + second_other.astype(f32),
        )

    mine = own.astype(f32) + swap_core(other).astype(f32)
    first, second = meet(mine[: 2 * part], mine[2 * part :], swap_pair, swap_side)
    return jnp.concatenate(meet(first, second, swap_side, swap_pair), 0)


def call(body, grid, in_specs, out_specs, out_shape, scratch=()):
    return pl.pallas_call(
        body,
        grid=grid,
        in_specs=in_specs,
        out_specs=out_specs,
        out_shape=out_shape,
        scratch_shapes=list(scratch),
        compiler_params=pltpu.CompilerParams(vmem_limit_bytes=48 * 1024 * 1024),
    )


def shape(*dims, dtype=f32):
    return jax.ShapeDtypeStruct(dims, dtype)


def row_block(rows, width):
    return pl.BlockSpec((rows, width), lambda b: (b, 0))


def seq_block(*dims):
    return pl.BlockSpec((1,) + dims, lambda b: (b,) + (0,) * len(dims))


def fixed(*dims):
    return pl.BlockSpec(dims, lambda b: (0,) * len(dims))


SCALAR = pl.BlockSpec(memory_space=pltpu.SMEM)


def product(left, right, left_dim=1, right_dim=0):
    return lax.dot_general(
        left, right, (((left_dim,), (right_dim,)), ((), ())), preferred_element_type=f32
    )


def halves(value):
    high = value.astype(bf16)
    return high, (value - high.astype(f32)).astype(bf16)


def fine_product(left, right, left_dim=1, right_dim=0):
    left_high, left_low = halves(left)
    right_high, right_low = halves(right)
    return (
        product(left_high, right_high, left_dim, right_dim)
        + product(left_high, right_low, left_dim, right_dim)
        + product(left_low, right_high, left_dim, right_dim)
    )


def head_mask():
    row = lax.broadcasted_iota(jnp.int32, (128, SW), 0)
    column = lax.broadcasted_iota(jnp.int32, (128, SW), 1)
    return jnp.where(column // MP == row, 1.0, 0.0).astype(bf16)


def spread_heads(value, mask):
    high, low = halves(value)
    return product(high, mask) + product(low, mask)


def sum_heads(value, mask):
    high, low = halves(value)
    return product(high, mask, 1, 1) + product(low, mask, 1, 1)


def rope_tables(positions):
    ladder = jnp.arange(HD // 2, dtype=f32)
    rates = ROPE_BASE ** (-2.0 * ladder / HD)
    angles = positions.astype(f32)[:, None] * rates[None, :]
    cosine, sine = jnp.cos(angles), jnp.sin(angles)
    return (
        jnp.concatenate([cosine] * 4, 1),
        jnp.concatenate([-sine, sine, -sine, sine], 1),
    )


def turn(value, cosine, sine):
    lane = lax.broadcasted_iota(jnp.int32, value.shape, 1)
    half = HD // 2
    other = jnp.where(
        lane % HD < half, pltpu.roll(value, 128 - half, 1), pltpu.roll(value, half, 1)
    )
    return value * cosine + other * sine


def turn_first(value, cosine, sine):
    lane = lax.broadcasted_iota(jnp.int32, value.shape, 1)
    return jnp.where(lane < HD, turn(value, cosine, sine), value)


def project_kernel(
    hidden,
    weight,
    cosine,
    sine,
    normed_out,
    mix_out,
    query_out,
    key_value_out,
    step_out,
    gate_out,
    gain_out,
):
    wide = hidden[...].astype(f32)
    scale = lax.rsqrt(jnp.mean(wide * wide, -1, keepdims=True) + EPSILON)
    gains = weight[:, STEP_AT:WIDE].astype(f32).T
    gain_out[...] = gains[SH : SH + 2]
    normed = (wide * scale * gains[SH : SH + 1]).astype(bf16)
    normed_out[...] = normed
    rows = product(normed, weight[...])
    mix_out[...] = rows[:, :MIXW].astype(bf16)
    at = MIXW
    query_out[...] = turn(rows[:, at : at + QW], cosine[...], sine[...]).astype(bf16)
    at += QW
    pair = turn_first(rows[:, at : at + 2 * HD], cosine[...], sine[...])
    key_value_out[...] = pair.astype(bf16)
    tail = rows[:, STEP_AT:WIDE]
    lane = lax.broadcasted_iota(jnp.int32, tail.shape, 1)
    step_out[...] = jnp.where(lane < SH, tail, 0.0)
    gate_out[...] = rows[:, WIDE:]


def project(hidden, weight, cosine, sine):
    count = hidden.shape[0]
    span = count // 2
    return call(
        project_kernel,
        (2,),
        [row_block(span, D), fixed(*weight.shape), fixed(span, 128), fixed(span, 128)],
        [
            row_block(span, D),
            row_block(span, MIXW),
            row_block(span, QW),
            row_block(span, 128),
            row_block(span, 128),
            row_block(span, SW),
            fixed(2, D),
        ],
        [
            shape(count, D, dtype=bf16),
            shape(count, MIXW, dtype=bf16),
            shape(count, QW, dtype=bf16),
            shape(count, 128, dtype=bf16),
            shape(count, 128),
            shape(count, SW),
            shape(2, D),
        ],
    )(hidden, weight, cosine, sine)


def feed_kernel(
    normed, upstream, gate_up, down, back_out, activation_out, own_out, other_out, layer_out
):
    pre = product(normed[...], gate_up[...])
    gate, up = pre[:, :FW], pre[:, FW:]
    sigmoid = 1.0 / (1.0 + jnp.exp(-gate))
    silu = gate * sigmoid
    activation = (silu * up).astype(bf16)
    activation_out[...] = activation
    back = product(upstream[...], down[...])
    back_gate = back * up * sigmoid * (1.0 + gate * (1.0 - sigmoid))
    back_feed = jnp.concatenate([back_gate.astype(bf16), (back * silu).astype(bf16)], 1)
    back_out[...] = back_feed
    partial = product(back_feed, gate_up[...], 1, 1)
    mine = pl.program_id(0) < pl.num_programs(0) // 2

    @pl.when(mine)
    def _():
        own_out[...] = partial

    @pl.when(jnp.logical_not(mine))
    def _():
        other_out[...] = partial.astype(bf16)

    layer_out[...] = product(activation, down[...], 1, 1).astype(bf16)


def feed_pass(normed, upstream, feed):
    count = normed.shape[0]
    rows = count // 4
    return call(
        feed_kernel,
        (4,),
        [
            row_block(rows, D),
            row_block(rows, D),
            fixed(D, 2 * FW),
            pl.BlockSpec((D, FW), lambda b: (0, 2)),
        ],
        [
            row_block(rows, 2 * FW),
            row_block(rows, FW),
            pl.BlockSpec((rows, D), lambda b: (jnp.minimum(b, 1), 0)),
            pl.BlockSpec((rows, D), lambda b: (jnp.maximum(b - 2, 0), 0)),
            row_block(rows, D),
        ],
        [
            shape(count, 2 * FW, dtype=bf16),
            shape(count, FW, dtype=bf16),
            shape(count // 2, D),
            shape(count // 2, D, dtype=bf16),
            shape(count, D, dtype=bf16),
        ],
    )(normed, upstream, feed, feed)


def visible_keys(span, keys, at):
    query = lax.broadcasted_iota(jnp.int32, (span, keys), 0)
    key = lax.broadcasted_iota(jnp.int32, (span, keys), 1)
    return (key < span) & (key <= query) | (key >= span) & (key < (at + 1) * span)


def attend_kernel(at, query, key_value, attended_out, total_out):
    span, keys = query.shape[0], key_value.shape[1]
    visible = visible_keys(span, keys, at[0])
    pair = key_value[0]
    for h in range(QW // HD):
        part = slice(h * HD, (h + 1) * HD)
        scores = product(query[:, part], pair[:, :HD], 1, 1) * HD ** (-0.5)
        scores = jnp.where(visible, scores, NEGATIVE)
        peak = jnp.max(scores, -1, keepdims=True)
        weights = jnp.exp(scores - peak)
        total = jnp.sum(weights, -1, keepdims=True)
        summed = product(weights.astype(bf16), pair[:, HD:])
        attended_out[:, part] = (summed / total).astype(bf16)
        total_out[:, part] = jnp.broadcast_to(peak + jnp.log(total), (span, HD))


def attend(at, query, key_values):
    count = query.shape[0]
    span = count // 2
    return call(
        attend_kernel,
        (2,),
        [SCALAR, row_block(span, QW), seq_block(*key_values.shape[1:])],
        [row_block(span, QW), row_block(span, QW)],
        [shape(count, QW, dtype=bf16), shape(count, QW)],
    )(at, query, key_values)


def attend_back_kernel(
    at, query, key_value, attended, log_total, back, cosine, sine, query_out, own_out, other_out
):
    span, keys = query.shape[0], key_value.shape[1]
    scale = HD ** (-0.5)
    visible = visible_keys(span, keys, at[0])
    pair = key_value[0]
    back_pair = jnp.zeros((keys, 2 * HD), f32)
    turned = []
    for h in range(QW // HD):
        part = slice(h * HD, (h + 1) * HD)
        head = query[:, part]
        upstream = back[:, part]
        delta = jnp.sum(
            upstream.astype(f32) * attended[:, part].astype(f32), -1, keepdims=True
        )
        scores = product(head, pair[:, :HD], 1, 1) * scale
        chance = jnp.where(visible, jnp.exp(scores - log_total[:, part][:, :1]), 0.0)
        back_chance = product(upstream, pair[:, HD:], 1, 1)
        back_scores = (chance * (back_chance - delta) * scale).astype(bf16)
        turned.append(product(back_scores, pair[:, :HD]))
        back_pair = back_pair + jnp.concatenate(
            [product(back_scores, head, 0, 0), product(chance.astype(bf16), upstream, 0, 0)], 1
        )
    query_out[...] = turn(jnp.concatenate(turned, 1), cosine[...], -sine[...]).astype(bf16)
    own_out[0] = back_pair[:span]
    other_out[0] = back_pair[span:].astype(bf16)


def attend_back(at, query, key_values, attended, log_total, back, cosine, sine):
    count = query.shape[0]
    span = count // 2
    keys = key_values.shape[1]
    return call(
        attend_back_kernel,
        (2,),
        [SCALAR, row_block(span, QW), seq_block(keys, 2 * HD)]
        + [row_block(span, QW)] * 3
        + [fixed(span, 128)] * 2,
        [row_block(span, QW), seq_block(span, 2 * HD), seq_block(keys - span, 2 * HD)],
        [
            shape(count, QW, dtype=bf16),
            shape(2, span, 2 * HD),
            shape(2, keys - span, 2 * HD, dtype=bf16),
        ],
    )(at, query, key_values, attended, log_total, back, cosine, sine)


LEAD = 8


def extend(scratch, rim, mix):
    scratch[0:LEAD] = rim[0].astype(f32)
    scratch[LEAD:] = mix[...].astype(f32)


def prep_kernel(rim, mix, step, taps, heads, conv_out, prep_out, turned_out, message_out, ext):
    rows = mix.shape[0]
    extend(ext, rim, mix)
    conv = taps[KW : KW + 1] + taps[0:1] * ext[pl.ds(LEAD - KW + 1, rows)]
    for tap in range(1, KW):
        conv = conv + taps[tap : tap + 1] * ext[pl.ds(LEAD - KW + 1 + tap, rows)]
    conv = conv / (1.0 + jnp.exp(-conv))
    conv_out[...] = conv
    lane = lax.broadcasted_iota(jnp.int32, step.shape, 1)
    raw = step[...] + heads[0:1]
    steps = jnp.maximum(raw, 0.0) + jnp.log1p(jnp.exp(-jnp.abs(raw)))
    steps = jnp.where(lane < SH, steps, 0.0)
    rate = -jnp.exp(heads[1:2]) * steps
    below = lax.broadcasted_iota(jnp.int32, (rows, rows), 0)
    along = lax.broadcasted_iota(jnp.int32, (rows, rows), 1)
    lower = jnp.where(below >= along, 1.0, 0.0)
    curve = lax.dot_general(
        lower, rate, (((1,), (0,)), ((), ())), precision=HIGHEST, preferred_element_type=f32
    )
    prep_out[:, :128] = steps
    prep_out[:, 128:] = curve
    turned_out[0, :8] = steps.T[:8]
    turned_out[0, 8:] = curve.T[:8]
    last = curve[rows - 1 : rows]
    weights = jnp.exp(last - curve) * steps
    mask = head_mask()
    scaled = spread_heads(weights, mask) * conv[:, :SW]
    state = fine_product(scaled, conv[:, SW : SW + NS], 0, 0)
    message_out[0, :SW] = state.astype(bf16)
    high = last.astype(bf16)
    low = (last - high.astype(f32)).astype(bf16)
    row = lax.broadcasted_iota(jnp.int32, (16, 128), 0)
    tail = jnp.where(row == 0, high.astype(f32), jnp.where(row == 1, low.astype(f32), 0.0))
    message_out[0, SW:] = tail.astype(bf16)


def prep(rim, mix, step, taps, heads):
    count = mix.shape[0]
    rows = count // 2
    return call(
        prep_kernel,
        (2,),
        [
            seq_block(LEAD, MIXW),
            row_block(rows, MIXW),
            row_block(rows, 128),
            fixed(8, MIXW),
            fixed(8, 128),
        ],
        [
            row_block(rows, MIXW),
            row_block(rows, 256),
            seq_block(16, rows),
            seq_block(SW + 16, NS),
        ],
        [
            shape(count, MIXW),
            shape(count, 256),
            shape(2, 16, rows),
            shape(2, SW + 16, NS, dtype=bf16),
        ],
        [pltpu.VMEM((LEAD + rows, MIXW), f32)],
    )(rim, mix, step, taps, heads)


def head_column(tail):
    row = lax.broadcasted_iota(jnp.int32, (SW, 128), 0)
    lane = lax.broadcasted_iota(jnp.int32, (SW, 128), 1)
    return jnp.sum(jnp.where(row // MP == lane, tail, 0.0), 1, keepdims=True)


def decay_of(message, at):
    return message[0, at : at + 1].astype(f32) + message[0, at + 1 : at + 2].astype(f32)


def scan_kernel(
    parts, gate, conv, prep, turned, skip, *refs
):
    messages = refs[:parts]
    mixed_out, state_out, square_out = refs[parts:]
    rows = conv.shape[0]
    between = jnp.zeros((1, 128), f32)
    state = jnp.zeros((SW, NS), f32)
    for message in messages:
        state = state + jnp.exp(head_column(between)) * message[0, :SW].astype(f32)
        between = between + decay_of(message, SW)
    state_out[0] = state
    entry = conv[:, SW : SW + NS]
    readout = conv[:, SW + NS :]
    meeting = fine_product(readout, entry, 1, 1)
    below = lax.broadcasted_iota(jnp.int32, (rows, rows), 0)
    along = lax.broadcasted_iota(jnp.int32, (rows, rows), 1)
    causal = below >= along
    meeting = jnp.where(causal, meeting, 0.0)
    parts_out = []
    for h in range(SH):
        spread = prep[:, 128 + h : 129 + h] - turned[0, 8 + h : 9 + h]
        mixing = jnp.exp(jnp.where(causal, spread, 0.0)) * meeting * turned[0, h : h + 1]
        signal = conv[:, MP * h : MP * (h + 1)].astype(bf16)
        parts_out.append(product(mixing.astype(bf16), signal))
    signal = conv[:, :SW]
    carried = fine_product(readout, state, 1, 1)
    grown = spread_heads(jnp.exp(prep[:, 128:]), head_mask())
    mixed = jnp.concatenate(parts_out, 1) + carried * grown + skip[...] * signal
    mixed_out[...] = mixed
    gated = mixed * gate[...] / (1.0 + jnp.exp(-gate[...]))
    square_out[...] = jnp.broadcast_to(jnp.sum(gated * gated, 1, keepdims=True), (rows, 128))


def scan(gate, conv, prepared, turned, skip, messages):
    count = conv.shape[0]
    rows = count // 2
    return call(
        lambda *refs: scan_kernel(len(messages), *refs),
        (2,),
        [
            row_block(rows, SW),
            row_block(rows, MIXW),
            row_block(rows, 256),
            seq_block(16, rows),
            fixed(1, SW),
        ]
        + [seq_block(SW + 16, NS)] * len(messages),
        [
            row_block(rows, SW),
            seq_block(SW, NS),
            row_block(rows, 128),
        ],
        [shape(count, SW), shape(2, SW, NS), shape(count, 128)],
    )(gate, conv, prepared, turned, skip, *messages)


def scan_back_kernel(parts, back, conv, prep, turned, skip, state, *refs):
    tails = refs[:parts]
    conv_out, prep_out, skip_out = refs[parts : parts + 3]
    sent_out = refs[parts + 3 :]
    rows = conv.shape[0]
    mask = head_mask()
    entry = conv[:, SW : SW + NS]
    readout = conv[:, SW + NS :]
    signal = conv[:, :SW]
    upstream = back[...]
    meeting = fine_product(readout, entry, 1, 1)
    below = lax.broadcasted_iota(jnp.int32, (rows, rows), 0)
    along = lax.broadcasted_iota(jnp.int32, (rows, rows), 1)
    causal = below >= along
    back_meeting = jnp.zeros((rows, rows), f32)
    lane = lax.broadcasted_iota(jnp.int32, (rows, 128), 1)
    place = lax.broadcasted_iota(jnp.int32, (8, rows), 0)
    back_steps = jnp.zeros((8, rows), f32)
    curve_along = jnp.zeros((8, rows), f32)
    back_curve = jnp.zeros((rows, 128), f32)
    back_signal = []
    for h in range(SH):
        part = slice(MP * h, MP * (h + 1))
        spread = prep[:, 128 + h : 129 + h] - turned[0, 8 + h : 9 + h]
        decay = jnp.where(causal, jnp.exp(jnp.where(causal, spread, 0.0)), 0.0)
        step = turned[0, h : h + 1]
        head_back = upstream[:, part].astype(bf16)
        back_mixing = product(head_back, signal[:, part].astype(bf16), 1, 1) * decay
        back_meeting = back_meeting + back_mixing * step
        scaled = back_mixing * meeting
        down = jnp.sum(scaled, 0, keepdims=True)
        across = jnp.sum(scaled * step, 1, keepdims=True)
        back_steps = jnp.where(place == h, down, back_steps)
        curve_along = jnp.where(place == h, -down * step, curve_along)
        back_curve = jnp.where(lane == h, across, back_curve)
        mixing = (decay * meeting * step).astype(bf16)
        back_signal.append(product(mixing, head_back, 0, 0))
    fold = jnp.concatenate([back_steps, curve_along, jnp.zeros((112, rows), f32)], 0).T
    grown = spread_heads(jnp.exp(prep[:, 128:]), mask)
    back_carried = upstream * grown
    carried = fine_product(readout, state[0], 1, 1)
    back_curve = back_curve + sum_heads(back_carried * carried, mask)
    back_curve = back_curve + jnp.where(lane < SH, pltpu.roll(fold, 120, 1), 0.0)
    conv_out[:, :SW] = jnp.concatenate(back_signal, 1) + skip[...] * upstream
    conv_out[:, SW : SW + NS] = fine_product(back_meeting, readout, 0, 0)
    conv_out[:, SW + NS :] = fine_product(back_meeting, entry) + fine_product(
        back_carried, state[0]
    )
    prep_out[:, :128] = jnp.where(lane < SH, fold, 0.0)
    prep_out[:, 128:] = back_curve
    back_skip = jnp.sum(upstream * signal, 0, keepdims=True)
    skip_out[0] = jnp.broadcast_to(sum_heads(jnp.broadcast_to(back_skip, (8, SW)), mask), (8, 128))
    back_state = fine_product(back_carried, readout, 0, 0)
    between = jnp.zeros((1, 128), f32)
    for tail, sent in zip(tails, sent_out):
        sent[0] = (jnp.exp(head_column(between)) * back_state).astype(bf16)
        between = between + decay_of(tail, 0)


def scan_back(back, conv, prepared, turned, skip, state, messages):
    count = conv.shape[0]
    rows = count // 2
    tail = pl.BlockSpec((1, 16, NS), lambda b: (b, SW // 16, 0))
    return call(
        lambda *refs: scan_back_kernel(len(messages), *refs),
        (2,),
        [
            row_block(rows, SW),
            row_block(rows, MIXW),
            row_block(rows, 256),
            seq_block(16, rows),
            fixed(1, SW),
            seq_block(SW, NS),
        ]
        + [tail] * len(messages),
        [row_block(rows, MIXW), row_block(rows, 256), seq_block(8, 128)]
        + [seq_block(SW, NS)] * len(messages),
        [shape(count, MIXW), shape(count, 256), shape(2, 8, 128)]
        + [shape(2, SW, NS, dtype=bf16)] * len(messages),
    )(back, conv, prepared, turned, skip, state, *messages)


def prep_back_kernel(
    parts,
    rim,
    mix,
    step,
    taps,
    heads,
    conv,
    prep,
    state,
    back_conv,
    back_prep,
    back_skip,
    *refs,
):
    received = refs[:parts]
    mix_out, step_out, rim_out, tap_out, head_out, ext, padded = refs[parts:]
    rows = mix.shape[0]
    mask = head_mask()
    next_back = jnp.zeros((SW, NS), f32)
    for piece in received:
        next_back = next_back + piece[0].astype(f32)
    steps, curve = prep[:, :128], prep[:, 128:]
    last = curve[rows - 1 : rows]
    decay = jnp.exp(last - curve)
    wide = spread_heads(decay * steps, mask)
    signal = conv[:, :SW]
    entry = conv[:, SW : SW + NS]
    back_scaled = fine_product(entry, next_back, 1, 1)
    back_weights = sum_heads(back_scaled * signal, mask)
    both = back_weights * decay
    back_steps = back_prep[:, :128] + both
    weighed = both * steps
    whole = jnp.sum(next_back * state[0], 1, keepdims=True)
    row = lax.broadcasted_iota(jnp.int32, (SW, 128), 0)
    lane = lax.broadcasted_iota(jnp.int32, (SW, 128), 1)
    whole = jnp.sum(jnp.where(row // MP == lane, whole, 0.0), 0, keepdims=True) * jnp.exp(last)
    at_last = lax.broadcasted_iota(jnp.int32, (rows, 128), 0) == rows - 1
    back_curve = back_prep[:, 128:] - weighed
    back_curve = back_curve + jnp.where(
        at_last, jnp.sum(weighed, 0, keepdims=True) + whole, 0.0
    )
    below = lax.broadcasted_iota(jnp.int32, (rows, rows), 0)
    along = lax.broadcasted_iota(jnp.int32, (rows, rows), 1)
    upper = jnp.where(below <= along, 1.0, 0.0)
    back_rate = lax.dot_general(
        upper, back_curve, (((1,), (0,)), ((), ())), precision=HIGHEST, preferred_element_type=f32
    )
    pace = -jnp.exp(heads[1:2])
    back_decay = jnp.sum(back_rate * pace * steps, 0, keepdims=True)
    raw = step[...] + heads[0:1]
    back_steps = (back_steps + back_rate * pace) / (1.0 + jnp.exp(-raw))
    wide_lane = lax.broadcasted_iota(jnp.int32, (rows, 128), 1)
    back_steps = jnp.where(wide_lane < SH, back_steps, 0.0)
    step_out[...] = back_steps
    place = lax.broadcasted_iota(jnp.int32, (8, 128), 0)
    total = jnp.where(place == 0, jnp.sum(back_steps, 0, keepdims=True), 0.0)
    total = jnp.where(place == 1, back_decay, total)
    head_out[0] = jnp.where(place == 2, back_skip[0], total)

    extend(ext, rim, mix)
    before = taps[KW : KW + 1] + taps[0:1] * ext[pl.ds(LEAD - KW + 1, rows)]
    for tap in range(1, KW):
        before = before + taps[tap : tap + 1] * ext[pl.ds(LEAD - KW + 1 + tap, rows)]
    sigmoid = 1.0 / (1.0 + jnp.exp(-before))
    slope = sigmoid * (1.0 + before * (1.0 - sigmoid))
    scaled = wide * signal
    upstream = jnp.concatenate(
        [
            back_conv[:, :SW] + back_scaled * wide,
            back_conv[:, SW : SW + NS] + fine_product(scaled, next_back),
            back_conv[:, SW + NS :],
        ],
        1,
    )
    back = upstream * slope
    place = lax.broadcasted_iota(jnp.int32, (8, MIXW), 0)
    sums = jnp.where(place == KW, jnp.sum(back, 0, keepdims=True), 0.0)
    for tap in range(KW):
        moved = jnp.sum(back * ext[pl.ds(LEAD - KW + 1 + tap, rows)], 0, keepdims=True)
        sums = jnp.where(place == tap, moved, sums)
    tap_out[0] = sums
    padded[0:LEAD] = jnp.zeros((LEAD, MIXW), f32)
    padded[LEAD : LEAD + rows] = back
    padded[LEAD + rows :] = jnp.zeros((LEAD, MIXW), f32)
    result = taps[KW - 1 : KW] * back
    first = jnp.zeros((LEAD, MIXW), f32)
    for tap in range(KW):
        if tap < KW - 1:
            result = result + taps[tap : tap + 1] * padded[pl.ds(LEAD + KW - 1 - tap, rows)]
        first = first + taps[tap : tap + 1] * padded[pl.ds(LEAD - tap, LEAD)]
    mix_out[...] = result
    rim_out[0] = jnp.where(place < KW - 1, first, 0.0)


def prep_back(rim, mix, step, taps, heads, conv, prepared, state, back_conv, back_prep, back_skip, received):
    count = mix.shape[0]
    rows = count // 2
    return call(
        lambda *refs: prep_back_kernel(len(received), *refs),
        (2,),
        [
            seq_block(LEAD, MIXW),
            row_block(rows, MIXW),
            row_block(rows, 128),
            fixed(8, MIXW),
            fixed(8, 128),
            row_block(rows, MIXW),
            row_block(rows, 256),
            seq_block(SW, NS),
            row_block(rows, MIXW),
            row_block(rows, 256),
            seq_block(8, 128),
        ]
        + [seq_block(SW, NS)] * len(received),
        [
            row_block(rows, MIXW),
            row_block(rows, 128),
            seq_block(LEAD, MIXW),
            seq_block(8, MIXW),
            seq_block(8, 128),
        ],
        [
            shape(count, MIXW),
            shape(count, 128),
            shape(2, LEAD, MIXW),
            shape(2, 8, MIXW),
            shape(2, 8, 128),
        ],
        [
            pltpu.VMEM((LEAD + rows, MIXW), f32),
            pltpu.VMEM((rows + 2 * LEAD, MIXW), f32),
        ],
    )(
        rim,
        mix,
        step,
        taps,
        heads,
        conv,
        prepared,
        state,
        back_conv,
        back_prep,
        back_skip,
        *received,
    )


def assemble_kernel(parts, side, gate, mix, rim, step, query, own, cosine, sine, *refs):
    received, out = refs[:parts], refs[parts]
    rows = mix.shape[0]
    out[:, WIDE:] = gate[...]
    mixed = slice(0, MIXW)
    out[:, mixed] = mix[...].astype(bf16)
    tail = mix[rows - 16 :]
    returned = jnp.concatenate([jnp.zeros((16 - LEAD, MIXW), f32), rim[0]], 0)
    tail = tail + pltpu.roll(returned, LEAD - KW + 1, 0)
    out[rows - 16 :, mixed] = tail.astype(bf16)
    at = MIXW
    out[:, at : at + QW] = query[...]
    half = jnp.zeros((rows // 2, 2 * HD), f32)
    for piece in received:
        half = half + piece[0].astype(f32)
    row = lax.broadcasted_iota(jnp.int32, (rows, 2 * HD), 0)
    pair = own[0] + jnp.where(row // (rows // 2) == side[0], jnp.concatenate([half, half], 0), 0.0)
    at += QW
    out[:, at : at + 2 * HD] = turn_first(pair, cosine[...], -sine[...]).astype(bf16)
    out[:, STEP_AT:WIDE] = step[...].astype(bf16)


def assemble(side, gate, mix, rim, step, query, own, received, cosine, sine):
    count = mix.shape[0]
    rows = count // 2
    return call(
        lambda *refs: assemble_kernel(len(received), *refs),
        (2,),
        [
            SCALAR,
            row_block(rows, SW),
            row_block(rows, MIXW),
            seq_block(LEAD, MIXW),
            row_block(rows, 128),
            row_block(rows, QW),
            seq_block(rows, 2 * HD),
            fixed(rows, 128),
            fixed(rows, 128),
        ]
        + [seq_block(rows // 2, 2 * HD)] * len(received),
        row_block(rows, FULL),
        shape(count, FULL, dtype=bf16),
    )(side, gate, mix, rim, step, query, own, cosine, sine, *received)


def sums_kernel(first_left, first_right, second_left, second_right, out):
    width = first_right.shape[1]
    out[:, :width] = product(first_left[...], first_right[...], 0, 0).astype(bf16)
    out[:, width:] = product(second_left[...], second_right[...], 0, 0).astype(bf16)


def weight_sums(first_left, first_right, second_left, second_right):
    count = first_left.shape[0]
    wide, more = first_right.shape[1], second_right.shape[1]
    rows = 256
    left = pl.BlockSpec((count, rows), lambda b: (0, b))
    return call(
        sums_kernel,
        (D // rows,),
        [left, fixed(count, wide), left, fixed(count, more)],
        row_block(rows, wide + more),
        shape(D, wide + more, dtype=bf16),
    )(first_left, first_right, second_left, second_right)


def local(
    tokens,
    out_cotangent,
    input_gain,
    mamba_gate_weight,
    mamba_mix_weight,
    mamba_step_weight,
    conv_kernel,
    conv_offset,
    step_offset,
    decay_log,
    skip_scale,
    mamba_norm_gain,
    mamba_out_weight,
    query_weight,
    key_weight,
    value_weight,
    attention_out_weight,
    ffn_gain,
    feed_gate_weight,
    feed_up_weight,
    feed_down_weight,
):
    rows = tokens.shape[1]
    span = 2 * rows
    count = 2 * span
    quads, spans = lax.axis_size("dp") // 4, lax.axis_size("ctx") // 2
    devices = 8 * quads * spans
    dp_at, ctx_at = lax.axis_index("dp"), lax.axis_index("ctx")
    side, span_at = ctx_at % 2, ctx_at // 2
    core, pair = dp_at % 2, dp_at // 2 % 2
    rank = core * 2 + side
    part = D // devices
    conv_part = CONV // devices
    gain_part = DSSM // devices
    groups = [
        [
            ((quad * 2 + y) * 2 + c) * 2 * spans + z * 2 + x
            for quad in range(quads)
            for z in range(spans)
            for y in range(2)
        ]
        for c in range(2)
        for x in range(2)
    ]
    feed_groups = [
        [(quad * 4 + d) * 2 * spans + z * 2 + x for quad in range(quads) for z in range(spans)]
        for d in range(4)
        for x in range(2)
    ]

    def order(value):
        lead = value.shape[:-1]
        value = value.reshape(*lead, quads, 4, spans, 2 * part)
        return jnp.swapaxes(value, -3, -2).reshape(*lead, D)

    def disorder(value):
        lead = value.shape[:-1]
        value = value.reshape(*lead, quads, spans, 4, 2 * part)
        return jnp.swapaxes(value, -3, -2).reshape(*lead, D)

    def gather(value, groups):
        return lax.all_gather(value, BOTH, axis=0, tiled=True, axis_index_groups=groups)

    def scatter(value, groups):
        return lax.psum_scatter(
            value, BOTH, scatter_dimension=0, tiled=True, axis_index_groups=groups
        )

    vector = jnp.concatenate([conv_kernel.reshape(-1), conv_offset, mamba_norm_gain])
    vector = jnp.pad(vector, (0, part * (VEC - 2) - vector.shape[0])).reshape(part, VEC - 2)
    tail = jnp.concatenate(
        [
            input_gain[:, None],
            ffn_gain[:, None],
            vector,
            jnp.zeros((part, WIDE - STEP_AT - SH - VEC), bf16),
        ],
        1,
    )
    def mixer_part(s):
        kv = s // 2
        return jnp.concatenate(
            [
                mamba_mix_weight[:, SW * s : SW * (s + 1)],
                mamba_mix_weight[:, DSSM:],
                query_weight[:, QW * s : QW * (s + 1)],
                key_weight[:, HD * kv : HD * (kv + 1)],
                value_weight[:, HD * kv : HD * (kv + 1)],
                mamba_step_weight[:, SH * s : SH * (s + 1)],
                tail,
                mamba_gate_weight[:, SW * s : SW * (s + 1)],
            ],
            1,
        )

    mixer_own = group_swap(jnp.stack([mixer_part(s) for s in range(TP)]), core, side)
    later = (
        mamba_out_weight,
        attention_out_weight,
        feed_gate_weight,
        feed_up_weight,
        feed_down_weight,
        tokens,
        out_cotangent,
    )
    mixer_own, later = lax.optimization_barrier((mixer_own, later))
    mamba_out_weight, attention_out_weight = later[:2]
    feed_gate_weight, feed_up_weight, feed_down_weight, tokens, out_cotangent = later[2:]
    mixer = gather(mixer_own.reshape(TP * part, -1), groups)
    mamba_out_turned = mamba_out_weight.T
    attention_out_turned = attention_out_weight.T
    feed_down_turned = feed_down_weight.T

    def branch_part(s):
        return jnp.concatenate(
            [
                mamba_out_turned[:, SW * s : SW * (s + 1)],
                attention_out_turned[:, QW * s : QW * (s + 1)],
            ],
            1,
        )

    branch_own = group_swap(jnp.stack([branch_part(s) for s in range(TP)]), core, side)
    branch_own = branch_own.reshape(TP * part, -1)
    def feed_part(s):
        return jnp.concatenate(
            [
                feed_gate_weight[:, FW * s : FW * (s + 1)],
                feed_up_weight[:, FW * s : FW * (s + 1)],
                feed_down_turned[:, FW * s : FW * (s + 1)],
            ],
            1,
        )

    feed_own = feed_swap(jnp.stack([feed_part(s) for s in range(FEED)]), pair, core, side)
    feed_own = feed_own.reshape(FEED * part, -1)
    own_low = order(tokens[0])
    own_hidden = own_low.astype(f32)
    own_scale_one = lax.rsqrt(jnp.mean(own_hidden * own_hidden, -1, keepdims=True) + EPSILON)
    hidden = group_gather(own_low, side)
    own_cotangent = order(out_cotangent[0])
    cosine, sine = rope_tables(span_at * span + jnp.arange(span, dtype=jnp.int32))
    upstream = feed_gather_slow(own_cotangent)
    branch_own, feed_own, mixer, hidden, upstream, cosine, sine = lax.optimization_barrier(
        (branch_own, feed_own, mixer, hidden, upstream, cosine, sine)
    )
    full_out = gather(branch_own, groups)
    feed = gather(feed_own, feed_groups)

    at = STEP_AT + SH + 2
    vectors = mixer[:, at : at + VEC - 2]
    natural = vectors.reshape(quads, spans, 4, 2, part * (VEC - 2))
    natural = natural.transpose(0, 2, 1, 3, 4).reshape(devices, part * (VEC - 2))
    at = 0
    all_kernel = natural[:, at : at + KW * conv_part].reshape(devices, KW, conv_part)
    all_kernel = all_kernel.transpose(1, 0, 2).reshape(KW, CONV)
    at += KW * conv_part
    all_offset = natural[:, at : at + conv_part].reshape(1, CONV)
    at += conv_part
    all_mamba_gain = natural[:, at : at + gain_part].reshape(DSSM)
    taps = jnp.concatenate([all_kernel, all_offset], 0)
    taps = jnp.concatenate(
        [lax.dynamic_slice_in_dim(taps, rank * SW, SW, 1), taps[:, DSSM:]], 1
    ).astype(f32)
    kernel, offset = taps[:KW], taps[KW]
    mamba_gain = lax.dynamic_slice_in_dim(all_mamba_gain, rank * SW, SW, 0).astype(f32)
    own_step_offset = lax.dynamic_slice_in_dim(step_offset, rank * SH, SH, 0)
    own_decay_log = lax.dynamic_slice_in_dim(decay_log, rank * SH, SH, 0)
    own_skip = lax.dynamic_slice_in_dim(skip_scale, rank * SH, SH, 0)

    at = jnp.reshape(span_at, (1,)).astype(jnp.int32)
    taps = jnp.pad(taps, ((0, 8 - taps.shape[0]), (0, 0)))
    heads = jnp.stack([own_step_offset, own_decay_log])
    heads = jnp.pad(heads, ((0, 6), (0, 128 - SH)))
    skip = jnp.repeat(own_skip, MP)[None]

    low_normed, mix_rows, query, key_value, step_rows, gate_rows, gains = project(
        hidden, mixer, cosine, sine
    )
    full_gain, full_gain_two = gains[0], gains[1]
    rim = mix_rows.reshape(2, span, MIXW)[:, span - LEAD :]
    rim = move_spans(rim, 1)
    key_value = key_value.reshape(2, span, 2 * HD)
    reached = [key_value] + [move_spans(key_value, s) for s in range(1, spans)]
    key_values = jnp.concatenate(reached, 1)
    conv, prepared, turned, message = prep(rim, mix_rows, step_rows, taps, heads)
    messages = [move_spans(message, s) for s in range(1, spans)]
    attended, log_total = attend(at, query, key_values)
    mixed, state_in, square = scan(gate_rows, conv, prepared, turned, skip, messages)
    square = group_sum(square[:, 0])
    mamba_scale = lax.rsqrt(square / DSSM + EPSILON)[:, None]
    gate_sigmoid = jax.nn.sigmoid(gate_rows)
    gate_silu = gate_rows * gate_sigmoid
    gated = mixed * gate_silu
    mamba_rows = (gated * mamba_scale * mamba_gain).astype(bf16)
    branches = jnp.concatenate([mamba_rows, attended], 1)
    middle = own_hidden + group_scatter(input_product(branches, full_out), side)
    middle, feed = lax.optimization_barrier((middle, feed))

    scale_two = lax.rsqrt(jnp.mean(middle * middle, -1, keepdims=True) + EPSILON)
    low_two = feed_gather((middle * scale_two * full_gain_two).astype(bf16))
    back_feed, activation, own_partial, other_partial, layer_partial = feed_pass(
        low_two, upstream, feed
    )
    gradient_feed = scatter(weight_sums(low_two, back_feed, upstream, activation), feed_groups)
    back_normed_two = feed_scatter(own_partial, other_partial)
    weighted = back_normed_two * full_gain_two
    gradient_gain_two = jnp.sum(back_normed_two * middle * scale_two, 0)
    back_middle = (
        own_cotangent.astype(f32)
        + scale_two * weighted
        - middle * scale_two**3 * jnp.mean(weighted * middle, -1, keepdims=True)
    )
    low_middle = group_gather(back_middle.astype(bf16), side)

    back_branches = forward_product(low_middle, full_out)
    back_attended = back_branches[:, SW:].astype(bf16)
    back_rows = back_branches[:, :SW]
    weighted = back_rows * mamba_gain
    gradient_mamba_gain = jnp.sum(back_rows * gated * mamba_scale, 0)
    mean = group_sum(jnp.sum(weighted * gated, -1))[:, None] / DSSM
    back_gated = mamba_scale * weighted - gated * mamba_scale**3 * mean
    back_mixed = back_gated * gate_silu
    low_gate = (
        back_gated * mixed * gate_sigmoid * (1.0 + gate_rows * (1.0 - gate_sigmoid))
    ).astype(bf16)
    back_attended, gradient_feed = lax.optimization_barrier((back_attended, gradient_feed))
    back_query, own_back, other_back = attend_back(
        at, query, key_values, attended, log_total, back_attended, cosine, sine
    )
    other_back = other_back.reshape(2, spans - 1, 2, rows, 2 * HD)
    low_half, high_half = other_back[:, :, 0], other_back[:, :, 1]
    half_back = jnp.where(side == 0, low_half, high_half).astype(f32)
    half_back = half_back + swap_side(jnp.where(side == 0, high_half, low_half)).astype(f32)
    half_back = half_back.astype(bf16)
    back_conv, back_prep, back_skip, *sent = scan_back(
        back_mixed, conv, prepared, turned, skip, state_in, messages
    )
    received = [move_spans(piece, -s) for s, piece in zip(range(1, spans), sent)]
    pieces = [move_spans(half_back[:, s - 1], -s) for s in range(1, spans)]
    back_mix, back_step, back_rim, tap_sums, head_sums = prep_back(
        rim,
        mix_rows,
        step_rows,
        taps,
        heads,
        conv,
        prepared,
        state_in,
        back_conv,
        back_prep,
        back_skip,
        received,
    )
    back_rim = move_spans(back_rim, -1)
    back_all = assemble(
        jnp.reshape(side, (1,)).astype(jnp.int32),
        low_gate,
        back_mix,
        back_rim,
        back_step,
        back_query,
        own_back,
        pieces,
        cosine,
        sine,
    )
    back_all, layer_partial = lax.optimization_barrier((back_all, layer_partial))
    layer_half = layer_partial.shape[0] // 2
    layer_out = middle + feed_scatter(layer_partial[:layer_half], layer_partial[layer_half:])
    gradient_mixer = scatter(
        weight_sums(low_normed, back_all, low_middle, branches), groups
    )
    back_normed = group_scatter(input_product(back_all, mixer), side)
    weighted = back_normed * full_gain
    gradient_gain_one = jnp.sum(back_normed * own_hidden * own_scale_one, 0)
    input_gradient = (
        back_middle
        + own_scale_one * weighted
        - own_hidden * own_scale_one**3 * jnp.mean(weighted * own_hidden, -1, keepdims=True)
    )

    def placed(value, width):
        wide = jnp.zeros(value.shape[:-1] + (width,), f32)
        return lax.dynamic_update_slice_in_dim(
            wide, value, rank * value.shape[-1], value.ndim - 1
        )

    tap_grads = jnp.sum(tap_sums, 0)[: KW + 1]
    tap_grads = jnp.concatenate([placed(tap_grads[:, :SW], DSSM), tap_grads[:, SW:]], 1)
    head_grads = jnp.sum(head_sums, 0)[:3, :SH]
    gain_grads, tap_grads, mamba_gain_grad, head_grads = lax.psum(
        (
            jnp.stack([gradient_gain_one, gradient_gain_two]),
            tap_grads,
            placed(gradient_mamba_gain, DSSM),
            placed(head_grads, MH),
        ),
        BOTH,
    )
    feature_at = (((dp_at // 4 * spans + span_at) * 2 + pair) * TP + rank) * part
    own_gains = lax.dynamic_slice_in_dim(gain_grads, feature_at, part, 1)
    device_at = dp_at * 2 * spans + ctx_at
    own_taps = lax.dynamic_slice_in_dim(tap_grads, device_at * conv_part, conv_part, 1)
    own_mamba_gain = lax.dynamic_slice_in_dim(
        mamba_gain_grad, device_at * gain_part, gain_part, 0
    )

    feed_parts = feed_swap(gradient_feed.reshape(FEED, part, -1), pair, core, side).astype(f32)
    mixer_parts = group_swap(gradient_mixer.reshape(TP, part, -1), core, side).astype(f32)

    def columns(parts, start, width):
        piece = parts[:, :, start : start + width]
        return piece.transpose(1, 0, 2).reshape(part, parts.shape[0] * width)

    def shared(start):
        piece = mixer_parts[:, :, start : start + HD].reshape(KVH, TP // KVH, part, HD)
        return jnp.sum(piece, 1).transpose(1, 0, 2).reshape(part, KVH * HD)

    at = MIXW
    mix_gradient = jnp.concatenate(
        [
            columns(mixer_parts, 0, SW),
            jnp.sum(mixer_parts[:, :, SW:MIXW], 0),
        ],
        1,
    )
    return (
        disorder(layer_out.astype(bf16))[None],
        disorder(input_gradient)[None],
        own_gains[0],
        columns(mixer_parts, WIDE, SW),
        mix_gradient,
        columns(mixer_parts, STEP_AT, SH),
        own_taps[:KW],
        own_taps[KW],
        head_grads[0],
        head_grads[1],
        head_grads[2],
        own_mamba_gain,
        columns(mixer_parts, FULL, SW).T,
        columns(mixer_parts, at, QW),
        shared(at + QW),
        shared(at + QW + HD),
        columns(mixer_parts, FULL + SW, QW).T,
        own_gains[1],
        columns(feed_parts, 0, FW),
        columns(feed_parts, FW, FW),
        columns(feed_parts, 2 * FW, FW).T,
    )


def solution(mesh):
    both = BOTH
    tokens = P("dp", "ctx", None)
    first = P(both, None)
    second = P(None, both)
    vector = P(both)
    whole = P()
    weights = (
        vector,
        first,
        first,
        first,
        second,
        vector,
        whole,
        whole,
        whole,
        vector,
        second,
        first,
        first,
        first,
        second,
        vector,
        first,
        first,
        second,
    )
    return jax.shard_map(
        local,
        mesh=mesh,
        in_specs=(tokens, tokens) + weights,
        out_specs=(tokens, tokens) + weights,
        check_vma=False,
    )
```

```python
import jax
import jax.numpy as jnp
from jax import lax
from jax.experimental import pallas as pl
from jax.experimental.pallas import tpu as pltpu
from jax.sharding import PartitionSpec as P

D = 1024
DSSM = 1536
MH = 24
MP = 64
NS = 128
KW = 4
AH = 8
KVH = 2
HD = 64
FF = 2048
CONV = DSSM + 2 * NS

TP = 4
SW = DSSM // TP
SH = MH // TP
QW = AH * HD // TP
FEED = 8
FW = FF // FEED
LEAD = 8
MIXW = SW + 2 * NS
STEP_AT = MIXW + QW + 2 * HD
VEC = 16
WIDE = 1024
FULL = WIDE + SW

EPSILON = 1e-05
ROPE_BASE = 100000000000.0
HIGHEST = lax.Precision.HIGHEST
NEGATIVE = -1e30
BOTH = ("dp", "ctx")
bf16 = jnp.bfloat16
f32 = jnp.float32


def forward_product(left, right):
    return jnp.dot(left, right, preferred_element_type=f32)


def input_product(upstream, weight):
    return lax.dot_general(
        upstream, weight, (((1,), (1,)), ((), ())), preferred_element_type=f32
    )


def swap_core(value):
    pairs = [(i, i ^ 1) for i in range(lax.axis_size("dp"))]
    return lax.ppermute(value, "dp", pairs)


def swap_side(value):
    pairs = [(i, i ^ 1) for i in range(lax.axis_size("ctx"))]
    return lax.ppermute(value, "ctx", pairs)


def swap_pair(value):
    pairs = [(i, i ^ 2) for i in range(lax.axis_size("dp"))]
    return lax.ppermute(value, "dp", pairs)


def move_spans(value, by):
    blocks = lax.axis_size("ctx")
    pairs = [(i, i + 2 * by) for i in range(blocks) if 0 <= i + 2 * by < blocks]
    return lax.ppermute(value, "ctx", pairs)


def group_gather(value, side):
    other = swap_side(value)
    first = side == 0
    mine = jnp.concatenate([jnp.where(first, value, other), jnp.where(first, other, value)], 0)
    return jnp.concatenate([mine, swap_core(mine)], 0)


def group_scatter(partial, side):
    span = partial.shape[0] // 2
    rows = span // 2
    mine = partial[:span] + swap_core(partial[span:])
    first = side == 0
    keep = jnp.where(first, mine[:rows], mine[rows:])
    send = jnp.where(first, mine[rows:], mine[:rows]).astype(bf16)
    return keep + swap_side(send).astype(f32)


def group_sum(value):
    span = value.shape[0] // 2
    other = swap_core(value)
    value = value + jnp.concatenate([other[span:], other[:span]], 0)
    return value + swap_side(value)


def exchange(parts, axis, bit, swap):
    first = lax.index_in_dim(parts, 0, axis, keepdims=False)
    second = lax.index_in_dim(parts, 1, axis, keepdims=False)
    low = bit == 0
    keep = jnp.where(low, first, second)
    other = swap(jnp.where(low, second, first))
    return jnp.stack([jnp.where(low, keep, other), jnp.where(low, other, keep)], axis)


def group_swap(parts, core, side):
    split = parts.reshape(2, 2, *parts.shape[1:])
    split = exchange(exchange(split, 0, core, swap_core), 1, side, swap_side)
    return split.reshape(parts.shape)


def feed_swap(parts, pair, core, side):
    split = parts.reshape(2, 2, 2, *parts.shape[1:])
    split = exchange(exchange(split, 1, core, swap_core), 2, side, swap_side)
    return exchange(split, 0, pair, swap_pair).reshape(parts.shape)


def both(first, second):
    return lax.optimization_barrier((first, second))


def feed_gather(value):
    half = value.shape[0] // 2
    first, second = value[:half], value[half:]
    first_other, second_other = both(swap_side(first), swap_pair(second))
    first_pair = jnp.concatenate([first, first_other], 0)
    second_pair = jnp.concatenate([second, second_other], 0)
    first_other, second_other = both(swap_pair(first_pair), swap_side(second_pair))
    mine = jnp.concatenate([first_pair, first_other, second_pair, second_other], 0)
    return jnp.concatenate([mine, swap_core(mine)], 0)


def feed_gather_slow(value):
    half = value.shape[0] // 2
    row = jnp.stack([value, swap_side(value)])
    square = jnp.stack([row, swap_pair(row)])
    first = square[:, :, :half].reshape(4 * half, -1)
    second = square[:, :, half:].swapaxes(0, 1).reshape(4 * half, -1)
    mine = jnp.concatenate([first, second], 0)
    return jnp.concatenate([mine, swap_core(mine)], 0)


def feed_scatter(own, other, beside=None):
    part = own.shape[0] // 4

    def meet(first, second, first_swap, second_swap):
        rows = first.shape[0] // 2
        first_other, second_other = both(
            first_swap(first[rows:].astype(bf16)), second_swap(second[rows:].astype(bf16))
        )
        return (
            first[:rows] + first_other.astype(f32),
            second[:rows] + second_other.astype(f32),
        )

    mine = own.astype(f32) + swap_core(other).astype(f32)
    first, second = meet(mine[: 2 * part], mine[2 * part :], swap_pair, swap_side)
    if beside is not None:
        first, second, beside = lax.optimization_barrier((first, second, beside))
    return (jnp.concatenate(meet(first, second, swap_side, swap_pair), 0), beside)


def call(body, grid, in_specs, out_specs, out_shape, scratch=()):
    return pl.pallas_call(
        body,
        grid=grid,
        in_specs=in_specs,
        out_specs=out_specs,
        out_shape=out_shape,
        scratch_shapes=list(scratch),
        compiler_params=pltpu.CompilerParams(vmem_limit_bytes=48 * 1024 * 1024),
    )


def shape(*dims, dtype=f32):
    return jax.ShapeDtypeStruct(dims, dtype)


def row_block(rows, width):
    return pl.BlockSpec((rows, width), lambda b: (b, 0))


def seq_block(*dims):
    return pl.BlockSpec((1,) + dims, lambda b: (b,) + (0,) * len(dims))


def fixed(*dims):
    return pl.BlockSpec(dims, lambda b: (0,) * len(dims))


SCALAR = pl.BlockSpec(memory_space=pltpu.SMEM)


def product(left, right, left_dim=1, right_dim=0):
    return lax.dot_general(
        left, right, (((left_dim,), (right_dim,)), ((), ())), preferred_element_type=f32
    )


def halves(value):
    high = value.astype(bf16)
    return high, (value - high.astype(f32)).astype(bf16)


def fine_product(left, right, left_dim=1, right_dim=0):
    left_high, left_low = halves(left)
    right_high, right_low = halves(right)
    return (
        product(left_high, right_high, left_dim, right_dim)
        + product(left_high, right_low, left_dim, right_dim)
        + product(left_low, right_high, left_dim, right_dim)
    )


def head_mask():
    row = lax.broadcasted_iota(jnp.int32, (128, SW), 0)
    column = lax.broadcasted_iota(jnp.int32, (128, SW), 1)
    return jnp.where(column // MP == row, 1.0, 0.0).astype(bf16)


def spread_heads(value, mask):
    high, low = halves(value)
    return product(high, mask) + product(low, mask)


def sum_heads(value, mask):
    high, low = halves(value)
    return product(high, mask, 1, 1) + product(low, mask, 1, 1)


def rope_tables(positions):
    ladder = jnp.arange(HD // 2, dtype=f32)
    rates = ROPE_BASE ** (-2.0 * ladder / HD)
    angles = positions.astype(f32)[:, None] * rates[None, :]
    cosine, sine = jnp.cos(angles), jnp.sin(angles)
    return (
        jnp.concatenate([cosine] * 4, 1),
        jnp.concatenate([-sine, sine, -sine, sine], 1),
    )


def turn(value, cosine, sine):
    lane = lax.broadcasted_iota(jnp.int32, value.shape, 1)
    half = HD // 2
    other = jnp.where(
        lane % HD < half, pltpu.roll(value, 128 - half, 1), pltpu.roll(value, half, 1)
    )
    return value * cosine + other * sine


def turn_first(value, cosine, sine):
    lane = lax.broadcasted_iota(jnp.int32, value.shape, 1)
    return jnp.where(lane < HD, turn(value, cosine, sine), value)


def project_kernel(
    hidden,
    rim_hidden,
    weight,
    cosine,
    sine,
    normed_out,
    mix_out,
    query_out,
    key_value_out,
    step_out,
    gate_out,
    gain_out,
    rim_out,
):
    def norm(value):
        wide = value.astype(f32)
        scale = lax.rsqrt(jnp.mean(wide * wide, -1, keepdims=True) + EPSILON)
        return (wide * scale * gains[SH : SH + 1]).astype(bf16)

    gains = weight[:, STEP_AT:WIDE].astype(f32).T
    gain_out[...] = gains[SH : SH + 2]
    rim_out[0] = product(norm(rim_hidden[0]), weight[:, :MIXW])[16 - LEAD :].astype(bf16)
    normed = norm(hidden[...])
    normed_out[...] = normed
    rows = product(normed, weight[...])
    mix_out[...] = rows[:, :MIXW].astype(bf16)
    at = MIXW
    query_out[...] = turn(rows[:, at : at + QW], cosine[...], sine[...]).astype(bf16)
    at += QW
    pair = turn_first(rows[:, at : at + 2 * HD], cosine[...], sine[...])
    key_value_out[...] = pair.astype(bf16)
    tail = rows[:, STEP_AT:WIDE]
    lane = lax.broadcasted_iota(jnp.int32, tail.shape, 1)
    step_out[...] = jnp.where(lane < SH, tail, 0.0)
    gate_out[...] = rows[:, WIDE:]


def project(hidden, rim_hidden, weight, cosine, sine):
    count = hidden.shape[0]
    span = count // 2
    return call(
        project_kernel,
        (2,),
        [
            row_block(span, D),
            seq_block(16, D),
            fixed(*weight.shape),
            fixed(span, 128),
            fixed(span, 128),
        ],
        [
            row_block(span, D),
            row_block(span, MIXW),
            row_block(span, QW),
            row_block(span, 128),
            row_block(span, 128),
            row_block(span, SW),
            fixed(2, D),
            seq_block(LEAD, MIXW),
        ],
        [
            shape(count, D, dtype=bf16),
            shape(count, MIXW, dtype=bf16),
            shape(count, QW, dtype=bf16),
            shape(count, 128, dtype=bf16),
            shape(count, 128),
            shape(count, SW),
            shape(2, D),
            shape(2, LEAD, MIXW, dtype=bf16),
        ],
    )(hidden, rim_hidden, weight, cosine, sine)


def feed_kernel(
    normed, upstream, gate_up, down, back_out, activation_out, own_out, other_out, layer_out
):
    pre = product(normed[...], gate_up[...])
    gate, up = pre[:, :FW], pre[:, FW:]
    sigmoid = 1.0 / (1.0 + jnp.exp(-gate))
    silu = gate * sigmoid
    activation = (silu * up).astype(bf16)
    activation_out[...] = activation
    back = product(upstream[...], down[...])
    back_gate = back * up * sigmoid * (1.0 + gate * (1.0 - sigmoid))
    back_feed = jnp.concatenate([back_gate.astype(bf16), (back * silu).astype(bf16)], 1)
    back_out[...] = back_feed
    partial = product(back_feed, gate_up[...], 1, 1)
    mine = pl.program_id(0) < pl.num_programs(0) // 2

    @pl.when(mine)
    def _():
        own_out[...] = partial

    @pl.when(jnp.logical_not(mine))
    def _():
        other_out[...] = partial.astype(bf16)

    layer_out[...] = product(activation, down[...], 1, 1).astype(bf16)


def feed_pass(normed, upstream, feed):
    count = normed.shape[0]
    rows = count // 4
    return call(
        feed_kernel,
        (4,),
        [
            row_block(rows, D),
            row_block(rows, D),
            fixed(D, 2 * FW),
            pl.BlockSpec((D, FW), lambda b: (0, 2)),
        ],
        [
            row_block(rows, 2 * FW),
            row_block(rows, FW),
            pl.BlockSpec((rows, D), lambda b: (jnp.minimum(b, 1), 0)),
            pl.BlockSpec((rows, D), lambda b: (jnp.maximum(b - 2, 0), 0)),
            row_block(rows, D),
        ],
        [
            shape(count, 2 * FW, dtype=bf16),
            shape(count, FW, dtype=bf16),
            shape(count // 2, D),
            shape(count // 2, D, dtype=bf16),
            shape(count, D, dtype=bf16),
        ],
    )(normed, upstream, feed, feed)


def visible_keys(span, keys, at):
    query = lax.broadcasted_iota(jnp.int32, (span, keys), 0)
    key = lax.broadcasted_iota(jnp.int32, (span, keys), 1)
    return (key < span) & (key <= query) | (key >= span) & (key < (at + 1) * span)


def attend_kernel(at, query, key_value, attended_out, total_out):
    span, keys = query.shape[0], key_value.shape[1]
    visible = visible_keys(span, keys, at[0])
    pair = key_value[0]
    for h in range(QW // HD):
        part = slice(h * HD, (h + 1) * HD)
        scores = product(query[:, part], pair[:, :HD], 1, 1) * HD ** (-0.5)
        scores = jnp.where(visible, scores, NEGATIVE)
        peak = jnp.max(scores, -1, keepdims=True)
        weights = jnp.exp(scores - peak)
        total = jnp.sum(weights, -1, keepdims=True)
        summed = product(weights.astype(bf16), pair[:, HD:])
        attended_out[:, part] = (summed / total).astype(bf16)
        total_out[:, part] = jnp.broadcast_to(peak + jnp.log(total), (span, HD))


def attend(at, query, key_values):
    count = query.shape[0]
    span = count // 2
    return call(
        attend_kernel,
        (2,),
        [SCALAR, row_block(span, QW), seq_block(*key_values.shape[1:])],
        [row_block(span, QW), row_block(span, QW)],
        [shape(count, QW, dtype=bf16), shape(count, QW)],
    )(at, query, key_values)


def attend_back_kernel(
    at, query, key_value, attended, log_total, back, cosine, sine, query_out, own_out, other_out
):
    span, keys = query.shape[0], key_value.shape[1]
    scale = HD ** (-0.5)
    visible = visible_keys(span, keys, at[0])
    pair = key_value[0]
    back_pair = jnp.zeros((keys, 2 * HD), f32)
    turned = []
    for h in range(QW // HD):
        part = slice(h * HD, (h + 1) * HD)
        head = query[:, part]
        upstream = back[:, part]
        delta = jnp.sum(
            upstream.astype(f32) * attended[:, part].astype(f32), -1, keepdims=True
        )
        scores = product(head, pair[:, :HD], 1, 1) * scale
        chance = jnp.where(visible, jnp.exp(scores - log_total[:, part][:, :1]), 0.0)
        back_chance = product(upstream, pair[:, HD:], 1, 1)
        back_scores = (chance * (back_chance - delta) * scale).astype(bf16)
        turned.append(product(back_scores, pair[:, :HD]))
        back_pair = back_pair + jnp.concatenate(
            [product(back_scores, head, 0, 0), product(chance.astype(bf16), upstream, 0, 0)], 1
        )
    query_out[...] = turn(jnp.concatenate(turned, 1), cosine[...], -sine[...]).astype(bf16)
    own_out[0] = back_pair[:span]
    other_out[0] = back_pair[span:].astype(bf16)


def attend_back(at, query, key_values, attended, log_total, back, cosine, sine):
    count = query.shape[0]
    span = count // 2
    keys = key_values.shape[1]
    return call(
        attend_back_kernel,
        (2,),
        [SCALAR, row_block(span, QW), seq_block(keys, 2 * HD)]
        + [row_block(span, QW)] * 3
        + [fixed(span, 128)] * 2,
        [row_block(span, QW), seq_block(span, 2 * HD), seq_block(keys - span, 2 * HD)],
        [
            shape(count, QW, dtype=bf16),
            shape(2, span, 2 * HD),
            shape(2, keys - span, 2 * HD, dtype=bf16),
        ],
    )(at, query, key_values, attended, log_total, back, cosine, sine)


def extend(scratch, rim, mix):
    scratch[0:LEAD] = rim[0].astype(f32)
    scratch[LEAD:] = mix[...].astype(f32)


def prep_kernel(rim, mix, step, taps, heads, conv_out, prep_out, turned_out, message_out, ext):
    rows = mix.shape[0]
    extend(ext, rim, mix)
    conv = taps[KW : KW + 1] + taps[0:1] * ext[pl.ds(LEAD - KW + 1, rows)]
    for tap in range(1, KW):
        conv = conv + taps[tap : tap + 1] * ext[pl.ds(LEAD - KW + 1 + tap, rows)]
    conv = conv / (1.0 + jnp.exp(-conv))
    conv_out[...] = conv
    lane = lax.broadcasted_iota(jnp.int32, step.shape, 1)
    raw = step[...] + heads[0:1]
    steps = jnp.maximum(raw, 0.0) + jnp.log1p(jnp.exp(-jnp.abs(raw)))
    steps = jnp.where(lane < SH, steps, 0.0)
    rate = -jnp.exp(heads[1:2]) * steps
    below = lax.broadcasted_iota(jnp.int32, (rows, rows), 0)
    along = lax.broadcasted_iota(jnp.int32, (rows, rows), 1)
    lower = jnp.where(below >= along, 1.0, 0.0)
    curve = lax.dot_general(
        lower, rate, (((1,), (0,)), ((), ())), precision=HIGHEST, preferred_element_type=f32
    )
    prep_out[:, :128] = steps
    prep_out[:, 128:] = curve
    turned_out[0, :8] = steps.T[:8]
    turned_out[0, 8:] = curve.T[:8]
    last = curve[rows - 1 : rows]
    weights = jnp.exp(last - curve) * steps
    mask = head_mask()
    scaled = spread_heads(weights, mask) * conv[:, :SW]
    state = fine_product(scaled, conv[:, SW : SW + NS], 0, 0)
    message_out[0, :SW] = state.astype(bf16)
    high = last.astype(bf16)
    low = (last - high.astype(f32)).astype(bf16)
    row = lax.broadcasted_iota(jnp.int32, (16, 128), 0)
    tail = jnp.where(row == 0, high.astype(f32), jnp.where(row == 1, low.astype(f32), 0.0))
    message_out[0, SW:] = tail.astype(bf16)


def prep(rim, mix, step, taps, heads):
    count = mix.shape[0]
    rows = count // 2
    return call(
        prep_kernel,
        (2,),
        [
            seq_block(LEAD, MIXW),
            row_block(rows, MIXW),
            row_block(rows, 128),
            fixed(8, MIXW),
            fixed(8, 128),
        ],
        [
            row_block(rows, MIXW),
            row_block(rows, 256),
            seq_block(16, rows),
            seq_block(SW + 16, NS),
        ],
        [
            shape(count, MIXW),
            shape(count, 256),
            shape(2, 16, rows),
            shape(2, SW + 16, NS, dtype=bf16),
        ],
        [pltpu.VMEM((LEAD + rows, MIXW), f32)],
    )(rim, mix, step, taps, heads)


def head_column(tail):
    row = lax.broadcasted_iota(jnp.int32, (SW, 128), 0)
    lane = lax.broadcasted_iota(jnp.int32, (SW, 128), 1)
    return jnp.sum(jnp.where(row // MP == lane, tail, 0.0), 1, keepdims=True)


def decay_of(message, at):
    return message[0, at : at + 1].astype(f32) + message[0, at + 1 : at + 2].astype(f32)


def scan_kernel(
    parts, gate, conv, prep, turned, skip, *refs
):
    messages = refs[:parts]
    mixed_out, state_out, square_out = refs[parts:]
    rows = conv.shape[0]
    between = jnp.zeros((1, 128), f32)
    state = jnp.zeros((SW, NS), f32)
    for message in messages:
        state = state + jnp.exp(head_column(between)) * message[0, :SW].astype(f32)
        between = between + decay_of(message, SW)
    state_out[0] = state
    entry = conv[:, SW : SW + NS]
    readout = conv[:, SW + NS :]
    meeting = fine_product(readout, entry, 1, 1)
    below = lax.broadcasted_iota(jnp.int32, (rows, rows), 0)
    along = lax.broadcasted_iota(jnp.int32, (rows, rows), 1)
    causal = below >= along
    meeting = jnp.where(causal, meeting, 0.0)
    parts_out = []
    for h in range(SH):
        spread = prep[:, 128 + h : 129 + h] - turned[0, 8 + h : 9 + h]
        mixing = jnp.exp(jnp.where(causal, spread, 0.0)) * meeting * turned[0, h : h + 1]
        signal = conv[:, MP * h : MP * (h + 1)].astype(bf16)
        parts_out.append(product(mixing.astype(bf16), signal))
    signal = conv[:, :SW]
    carried = fine_product(readout, state, 1, 1)
    grown = spread_heads(jnp.exp(prep[:, 128:]), head_mask())
    mixed = jnp.concatenate(parts_out, 1) + carried * grown + skip[...] * signal
    mixed_out[...] = mixed
    gated = mixed * gate[...] / (1.0 + jnp.exp(-gate[...]))
    square_out[...] = jnp.broadcast_to(jnp.sum(gated * gated, 1, keepdims=True), (rows, 128))


def scan(gate, conv, prepared, turned, skip, messages):
    count = conv.shape[0]
    rows = count // 2
    return call(
        lambda *refs: scan_kernel(len(messages), *refs),
        (2,),
        [
            row_block(rows, SW),
            row_block(rows, MIXW),
            row_block(rows, 256),
            seq_block(16, rows),
            fixed(1, SW),
        ]
        + [seq_block(SW + 16, NS)] * len(messages),
        [
            row_block(rows, SW),
            seq_block(SW, NS),
            row_block(rows, 128),
        ],
        [shape(count, SW), shape(2, SW, NS), shape(count, 128)],
    )(gate, conv, prepared, turned, skip, *messages)


def scan_back_kernel(parts, back, conv, prep, turned, skip, state, *refs):
    tails = refs[:parts]
    conv_out, prep_out, skip_out = refs[parts : parts + 3]
    sent_out = refs[parts + 3 :]
    rows = conv.shape[0]
    mask = head_mask()
    entry = conv[:, SW : SW + NS]
    readout = conv[:, SW + NS :]
    signal = conv[:, :SW]
    upstream = back[...]
    meeting = fine_product(readout, entry, 1, 1)
    below = lax.broadcasted_iota(jnp.int32, (rows, rows), 0)
    along = lax.broadcasted_iota(jnp.int32, (rows, rows), 1)
    causal = below >= along
    back_meeting = jnp.zeros((rows, rows), f32)
    lane = lax.broadcasted_iota(jnp.int32, (rows, 128), 1)
    place = lax.broadcasted_iota(jnp.int32, (8, rows), 0)
    back_steps = jnp.zeros((8, rows), f32)
    curve_along = jnp.zeros((8, rows), f32)
    back_curve = jnp.zeros((rows, 128), f32)
    back_signal = []
    for h in range(SH):
        part = slice(MP * h, MP * (h + 1))
        spread = prep[:, 128 + h : 129 + h] - turned[0, 8 + h : 9 + h]
        decay = jnp.where(causal, jnp.exp(jnp.where(causal, spread, 0.0)), 0.0)
        step = turned[0, h : h + 1]
        head_back = upstream[:, part].astype(bf16)
        back_mixing = product(head_back, signal[:, part].astype(bf16), 1, 1) * decay
        back_meeting = back_meeting + back_mixing * step
        scaled = back_mixing * meeting
        down = jnp.sum(scaled, 0, keepdims=True)
        across = jnp.sum(scaled * step, 1, keepdims=True)
        back_steps = jnp.where(place == h, down, back_steps)
        curve_along = jnp.where(place == h, -down * step, curve_along)
        back_curve = jnp.where(lane == h, across, back_curve)
        mixing = (decay * meeting * step).astype(bf16)
        back_signal.append(product(mixing, head_back, 0, 0))
    fold = jnp.concatenate([back_steps, curve_along, jnp.zeros((112, rows), f32)], 0).T
    grown = spread_heads(jnp.exp(prep[:, 128:]), mask)
    back_carried = upstream * grown
    carried = fine_product(readout, state[0], 1, 1)
    back_curve = back_curve + sum_heads(back_carried * carried, mask)
    back_curve = back_curve + jnp.where(lane < SH, pltpu.roll(fold, 120, 1), 0.0)
    conv_out[:, :SW] = jnp.concatenate(back_signal, 1) + skip[...] * upstream
    conv_out[:, SW : SW + NS] = fine_product(back_meeting, readout, 0, 0)
    conv_out[:, SW + NS :] = fine_product(back_meeting, entry) + fine_product(
        back_carried, state[0]
    )
    prep_out[:, :128] = jnp.where(lane < SH, fold, 0.0)
    prep_out[:, 128:] = back_curve
    back_skip = jnp.sum(upstream * signal, 0, keepdims=True)
    skip_out[0] = jnp.broadcast_to(sum_heads(jnp.broadcast_to(back_skip, (8, SW)), mask), (8, 128))
    back_state = fine_product(back_carried, readout, 0, 0)
    between = jnp.zeros((1, 128), f32)
    for tail, sent in zip(tails, sent_out):
        sent[0] = (jnp.exp(head_column(between)) * back_state).astype(bf16)
        between = between + decay_of(tail, 0)


def scan_back(back, conv, prepared, turned, skip, state, messages):
    count = conv.shape[0]
    rows = count // 2
    tail = pl.BlockSpec((1, 16, NS), lambda b: (b, SW // 16, 0))
    return call(
        lambda *refs: scan_back_kernel(len(messages), *refs),
        (2,),
        [
            row_block(rows, SW),
            row_block(rows, MIXW),
            row_block(rows, 256),
            seq_block(16, rows),
            fixed(1, SW),
            seq_block(SW, NS),
        ]
        + [tail] * len(messages),
        [row_block(rows, MIXW), row_block(rows, 256), seq_block(8, 128)]
        + [seq_block(SW, NS)] * len(messages),
        [shape(count, MIXW), shape(count, 256), shape(2, 8, 128)]
        + [shape(2, SW, NS, dtype=bf16)] * len(messages),
    )(back, conv, prepared, turned, skip, state, *messages)


def prep_back_kernel(
    parts,
    rim,
    mix,
    step,
    taps,
    heads,
    conv,
    prep,
    state,
    back_conv,
    back_prep,
    back_skip,
    *refs,
):
    received = refs[:parts]
    mix_out, step_out, rim_out, tap_out, head_out, ext, padded = refs[parts:]
    rows = mix.shape[0]
    mask = head_mask()
    next_back = jnp.zeros((SW, NS), f32)
    for piece in received:
        next_back = next_back + piece[0].astype(f32)
    steps, curve = prep[:, :128], prep[:, 128:]
    last = curve[rows - 1 : rows]
    decay = jnp.exp(last - curve)
    wide = spread_heads(decay * steps, mask)
    signal = conv[:, :SW]
    entry = conv[:, SW : SW + NS]
    back_scaled = fine_product(entry, next_back, 1, 1)
    back_weights = sum_heads(back_scaled * signal, mask)
    both = back_weights * decay
    back_steps = back_prep[:, :128] + both
    weighed = both * steps
    whole = jnp.sum(next_back * state[0], 1, keepdims=True)
    row = lax.broadcasted_iota(jnp.int32, (SW, 128), 0)
    lane = lax.broadcasted_iota(jnp.int32, (SW, 128), 1)
    whole = jnp.sum(jnp.where(row // MP == lane, whole, 0.0), 0, keepdims=True) * jnp.exp(last)
    at_last = lax.broadcasted_iota(jnp.int32, (rows, 128), 0) == rows - 1
    back_curve = back_prep[:, 128:] - weighed
    back_curve = back_curve + jnp.where(
        at_last, jnp.sum(weighed, 0, keepdims=True) + whole, 0.0
    )
    below = lax.broadcasted_iota(jnp.int32, (rows, rows), 0)
    along = lax.broadcasted_iota(jnp.int32, (rows, rows), 1)
    upper = jnp.where(below <= along, 1.0, 0.0)
    back_rate = lax.dot_general(
        upper, back_curve, (((1,), (0,)), ((), ())), precision=HIGHEST, preferred_element_type=f32
    )
    pace = -jnp.exp(heads[1:2])
    back_decay = jnp.sum(back_rate * pace * steps, 0, keepdims=True)
    raw = step[...] + heads[0:1]
    back_steps = (back_steps + back_rate * pace) / (1.0 + jnp.exp(-raw))
    wide_lane = lax.broadcasted_iota(jnp.int32, (rows, 128), 1)
    back_steps = jnp.where(wide_lane < SH, back_steps, 0.0)
    step_out[...] = back_steps
    place = lax.broadcasted_iota(jnp.int32, (8, 128), 0)
    total = jnp.where(place == 0, jnp.sum(back_steps, 0, keepdims=True), 0.0)
    total = jnp.where(place == 1, back_decay, total)
    head_out[0] = jnp.where(place == 2, back_skip[0], total)

    extend(ext, rim, mix)
    before = taps[KW : KW + 1] + taps[0:1] * ext[pl.ds(LEAD - KW + 1, rows)]
    for tap in range(1, KW):
        before = before + taps[tap : tap + 1] * ext[pl.ds(LEAD - KW + 1 + tap, rows)]
    sigmoid = 1.0 / (1.0 + jnp.exp(-before))
    slope = sigmoid * (1.0 + before * (1.0 - sigmoid))
    scaled = wide * signal
    upstream = jnp.concatenate(
        [
            back_conv[:, :SW] + back_scaled * wide,
            back_conv[:, SW : SW + NS] + fine_product(scaled, next_back),
            back_conv[:, SW + NS :],
        ],
        1,
    )
    back = upstream * slope
    place = lax.broadcasted_iota(jnp.int32, (8, MIXW), 0)
    sums = jnp.where(place == KW, jnp.sum(back, 0, keepdims=True), 0.0)
    for tap in range(KW):
        moved = jnp.sum(back * ext[pl.ds(LEAD - KW + 1 + tap, rows)], 0, keepdims=True)
        sums = jnp.where(place == tap, moved, sums)
    tap_out[0] = sums
    padded[0:LEAD] = jnp.zeros((LEAD, MIXW), f32)
    padded[LEAD : LEAD + rows] = back
    padded[LEAD + rows :] = jnp.zeros((LEAD, MIXW), f32)
    result = taps[KW - 1 : KW] * back
    first = jnp.zeros((LEAD, MIXW), f32)
    for tap in range(KW):
        if tap < KW - 1:
            result = result + taps[tap : tap + 1] * padded[pl.ds(LEAD + KW - 1 - tap, rows)]
        first = first + taps[tap : tap + 1] * padded[pl.ds(LEAD - tap, LEAD)]
    mix_out[...] = result
    rim_out[0] = jnp.where(place < KW - 1, first, 0.0)


def prep_back(rim, mix, step, taps, heads, conv, prepared, state, back_conv, back_prep, back_skip, received):
    count = mix.shape[0]
    rows = count // 2
    return call(
        lambda *refs: prep_back_kernel(len(received), *refs),
        (2,),
        [
            seq_block(LEAD, MIXW),
            row_block(rows, MIXW),
            row_block(rows, 128),
            fixed(8, MIXW),
            fixed(8, 128),
            row_block(rows, MIXW),
            row_block(rows, 256),
            seq_block(SW, NS),
            row_block(rows, MIXW),
            row_block(rows, 256),
            seq_block(8, 128),
        ]
        + [seq_block(SW, NS)] * len(received),
        [
            row_block(rows, MIXW),
            row_block(rows, 128),
            seq_block(LEAD, MIXW),
            seq_block(8, MIXW),
            seq_block(8, 128),
        ],
        [
            shape(count, MIXW),
            shape(count, 128),
            shape(2, LEAD, MIXW),
            shape(2, 8, MIXW),
            shape(2, 8, 128),
        ],
        [
            pltpu.VMEM((LEAD + rows, MIXW), f32),
            pltpu.VMEM((rows + 2 * LEAD, MIXW), f32),
        ],
    )(
        rim,
        mix,
        step,
        taps,
        heads,
        conv,
        prepared,
        state,
        back_conv,
        back_prep,
        back_skip,
        *received,
    )


def assemble_kernel(parts, side, gate, mix, rim, step, query, own, cosine, sine, *refs):
    received, out = refs[:parts], refs[parts]
    rows = mix.shape[0]
    out[:, WIDE:] = gate[...]
    mixed = slice(0, MIXW)
    out[:, mixed] = mix[...].astype(bf16)
    tail = mix[rows - 16 :]
    returned = jnp.concatenate([jnp.zeros((16 - LEAD, MIXW), f32), rim[0]], 0)
    tail = tail + pltpu.roll(returned, LEAD - KW + 1, 0)
    out[rows - 16 :, mixed] = tail.astype(bf16)
    at = MIXW
    out[:, at : at + QW] = query[...]
    half = jnp.zeros((rows // 2, 2 * HD), f32)
    for piece in received:
        half = half + piece[0].astype(f32)
    row = lax.broadcasted_iota(jnp.int32, (rows, 2 * HD), 0)
    pair = own[0] + jnp.where(row // (rows // 2) == side[0], jnp.concatenate([half, half], 0), 0.0)
    at += QW
    out[:, at : at + 2 * HD] = turn_first(pair, cosine[...], -sine[...]).astype(bf16)
    out[:, STEP_AT:WIDE] = step[...].astype(bf16)


def assemble(side, gate, mix, rim, step, query, own, received, cosine, sine):
    count = mix.shape[0]
    rows = count // 2
    return call(
        lambda *refs: assemble_kernel(len(received), *refs),
        (2,),
        [
            SCALAR,
            row_block(rows, SW),
            row_block(rows, MIXW),
            seq_block(LEAD, MIXW),
            row_block(rows, 128),
            row_block(rows, QW),
            seq_block(rows, 2 * HD),
            fixed(rows, 128),
            fixed(rows, 128),
        ]
        + [seq_block(rows // 2, 2 * HD)] * len(received),
        row_block(rows, FULL),
        shape(count, FULL, dtype=bf16),
    )(side, gate, mix, rim, step, query, own, cosine, sine, *received)


def sums_kernel(first_left, first_right, second_left, second_right, out):
    width = first_right.shape[1]
    out[:, :width] = product(first_left[...], first_right[...], 0, 0).astype(bf16)
    out[:, width:] = product(second_left[...], second_right[...], 0, 0).astype(bf16)


def weight_sums(first_left, first_right, second_left, second_right):
    count = first_left.shape[0]
    wide, more = first_right.shape[1], second_right.shape[1]
    rows = 256
    left = pl.BlockSpec((count, rows), lambda b: (0, b))
    return call(
        sums_kernel,
        (D // rows,),
        [left, fixed(count, wide), left, fixed(count, more)],
        row_block(rows, wide + more),
        shape(D, wide + more, dtype=bf16),
    )(first_left, first_right, second_left, second_right)


def local(
    tokens,
    out_cotangent,
    input_gain,
    mamba_gate_weight,
    mamba_mix_weight,
    mamba_step_weight,
    conv_kernel,
    conv_offset,
    step_offset,
    decay_log,
    skip_scale,
    mamba_norm_gain,
    mamba_out_weight,
    query_weight,
    key_weight,
    value_weight,
    attention_out_weight,
    ffn_gain,
    feed_gate_weight,
    feed_up_weight,
    feed_down_weight,
):
    rows = tokens.shape[1]
    span = 2 * rows
    count = 2 * span
    quads, spans = lax.axis_size("dp") // 4, lax.axis_size("ctx") // 2
    devices = 8 * quads * spans
    dp_at, ctx_at = lax.axis_index("dp"), lax.axis_index("ctx")
    side, span_at = ctx_at % 2, ctx_at // 2
    core, pair = dp_at % 2, dp_at // 2 % 2
    rank = core * 2 + side
    part = D // devices
    conv_part = CONV // devices
    gain_part = DSSM // devices
    groups = [
        [
            ((quad * 2 + y) * 2 + c) * 2 * spans + z * 2 + x
            for quad in range(quads)
            for z in range(spans)
            for y in range(2)
        ]
        for c in range(2)
        for x in range(2)
    ]
    feed_groups = [
        [(quad * 4 + d) * 2 * spans + z * 2 + x for quad in range(quads) for z in range(spans)]
        for d in range(4)
        for x in range(2)
    ]

    def order(value):
        lead = value.shape[:-1]
        value = value.reshape(*lead, quads, 4, spans, 2 * part)
        return jnp.swapaxes(value, -3, -2).reshape(*lead, D)

    def disorder(value):
        lead = value.shape[:-1]
        value = value.reshape(*lead, quads, spans, 4, 2 * part)
        return jnp.swapaxes(value, -3, -2).reshape(*lead, D)

    def gather(value, groups):
        return lax.all_gather(value, BOTH, axis=0, tiled=True, axis_index_groups=groups)

    def scatter(value, groups):
        return lax.psum_scatter(
            value, BOTH, scatter_dimension=0, tiled=True, axis_index_groups=groups
        )

    vector = jnp.concatenate([conv_kernel.reshape(-1), conv_offset, mamba_norm_gain])
    vector = jnp.pad(vector, (0, part * (VEC - 2) - vector.shape[0])).reshape(part, VEC - 2)
    tail = jnp.concatenate(
        [
            input_gain[:, None],
            ffn_gain[:, None],
            vector,
            jnp.zeros((part, WIDE - STEP_AT - SH - VEC), bf16),
        ],
        1,
    )
    def mixer_part(s):
        kv = s // 2
        return jnp.concatenate(
            [
                mamba_mix_weight[:, SW * s : SW * (s + 1)],
                mamba_mix_weight[:, DSSM:],
                query_weight[:, QW * s : QW * (s + 1)],
                key_weight[:, HD * kv : HD * (kv + 1)],
                value_weight[:, HD * kv : HD * (kv + 1)],
                mamba_step_weight[:, SH * s : SH * (s + 1)],
                tail,
                mamba_gate_weight[:, SW * s : SW * (s + 1)],
            ],
            1,
        )

    mixer_own = group_swap(jnp.stack([mixer_part(s) for s in range(TP)]), core, side)
    later = (
        mamba_out_weight,
        attention_out_weight,
        feed_gate_weight,
        feed_up_weight,
        feed_down_weight,
        tokens,
        out_cotangent,
    )
    mixer_own, later = lax.optimization_barrier((mixer_own, later))
    mamba_out_weight, attention_out_weight = later[:2]
    feed_gate_weight, feed_up_weight, feed_down_weight, tokens, out_cotangent = later[2:]
    mixer = gather(mixer_own.reshape(TP * part, -1), groups)
    mamba_out_turned = mamba_out_weight.T
    attention_out_turned = attention_out_weight.T
    feed_down_turned = feed_down_weight.T

    def branch_part(s):
        return jnp.concatenate(
            [
                mamba_out_turned[:, SW * s : SW * (s + 1)],
                attention_out_turned[:, QW * s : QW * (s + 1)],
            ],
            1,
        )

    branch_own = group_swap(jnp.stack([branch_part(s) for s in range(TP)]), core, side)
    branch_own = branch_own.reshape(TP * part, -1)
    def feed_part(s):
        return jnp.concatenate(
            [
                feed_gate_weight[:, FW * s : FW * (s + 1)],
                feed_up_weight[:, FW * s : FW * (s + 1)],
                feed_down_turned[:, FW * s : FW * (s + 1)],
            ],
            1,
        )

    feed_own = feed_swap(jnp.stack([feed_part(s) for s in range(FEED)]), pair, core, side)
    feed_own = feed_own.reshape(FEED * part, -1)
    own_low = order(tokens[0])
    own_hidden = own_low.astype(f32)
    own_scale_one = lax.rsqrt(jnp.mean(own_hidden * own_hidden, -1, keepdims=True) + EPSILON)
    hidden = group_gather(own_low, side)
    own_cotangent = order(out_cotangent[0])
    cosine, sine = rope_tables(span_at * span + jnp.arange(span, dtype=jnp.int32))
    upstream = feed_gather_slow(own_cotangent)
    rim_hidden = move_spans(hidden.reshape(2, span, D)[:, span - 16 :], 1)
    branch_own, feed_own, mixer, hidden, rim_hidden, upstream, cosine, sine = (
        lax.optimization_barrier(
            (branch_own, feed_own, mixer, hidden, rim_hidden, upstream, cosine, sine)
        )
    )
    full_out = gather(branch_own, groups)
    feed = gather(feed_own, feed_groups)

    at = STEP_AT + SH + 2
    vectors = mixer[:, at : at + VEC - 2]
    natural = vectors.reshape(quads, spans, 4, 2, part * (VEC - 2))
    natural = natural.transpose(0, 2, 1, 3, 4).reshape(devices, part * (VEC - 2))
    at = 0
    all_kernel = natural[:, at : at + KW * conv_part].reshape(devices, KW, conv_part)
    all_kernel = all_kernel.transpose(1, 0, 2).reshape(KW, CONV)
    at += KW * conv_part
    all_offset = natural[:, at : at + conv_part].reshape(1, CONV)
    at += conv_part
    all_mamba_gain = natural[:, at : at + gain_part].reshape(DSSM)
    taps = jnp.concatenate([all_kernel, all_offset], 0)
    taps = jnp.concatenate(
        [lax.dynamic_slice_in_dim(taps, rank * SW, SW, 1), taps[:, DSSM:]], 1
    ).astype(f32)
    kernel, offset = taps[:KW], taps[KW]
    mamba_gain = lax.dynamic_slice_in_dim(all_mamba_gain, rank * SW, SW, 0).astype(f32)
    own_step_offset = lax.dynamic_slice_in_dim(step_offset, rank * SH, SH, 0)
    own_decay_log = lax.dynamic_slice_in_dim(decay_log, rank * SH, SH, 0)
    own_skip = lax.dynamic_slice_in_dim(skip_scale, rank * SH, SH, 0)

    at = jnp.reshape(span_at, (1,)).astype(jnp.int32)
    taps = jnp.pad(taps, ((0, 8 - taps.shape[0]), (0, 0)))
    heads = jnp.stack([own_step_offset, own_decay_log])
    heads = jnp.pad(heads, ((0, 6), (0, 128 - SH)))
    skip = jnp.repeat(own_skip, MP)[None]

    low_normed, mix_rows, query, key_value, step_rows, gate_rows, gains, rim = project(
        hidden, rim_hidden, mixer, cosine, sine
    )
    full_gain, full_gain_two = gains[0], gains[1]
    key_value = key_value.reshape(2, span, 2 * HD)
    half = jnp.where(side == 0, key_value[:, :rows], key_value[:, rows:])
    halves_in = jnp.stack([move_spans(half, s) for s in range(1, spans)], 1)
    halves_other = swap_side(halves_in)
    reached = jnp.stack(
        [
            jnp.where(side == 0, halves_in, halves_other),
            jnp.where(side == 0, halves_other, halves_in),
        ],
        2,
    ).reshape(2, (spans - 1) * span, 2 * HD)
    key_values = jnp.concatenate([key_value, reached], 1)
    conv, prepared, turned, message = prep(rim, mix_rows, step_rows, taps, heads)
    messages = [move_spans(message, s) for s in range(1, spans)]
    attended, log_total = attend(at, query, key_values)
    mixed, state_in, square = scan(gate_rows, conv, prepared, turned, skip, messages)
    square = group_sum(square[:, 0])
    mamba_scale = lax.rsqrt(square / DSSM + EPSILON)[:, None]
    gate_sigmoid = jax.nn.sigmoid(gate_rows)
    gate_silu = gate_rows * gate_sigmoid
    gated = mixed * gate_silu
    mamba_rows = (gated * mamba_scale * mamba_gain).astype(bf16)
    branches = jnp.concatenate([mamba_rows, attended], 1)
    middle = own_hidden + group_scatter(input_product(branches, full_out), side)
    middle, feed = lax.optimization_barrier((middle, feed))

    scale_two = lax.rsqrt(jnp.mean(middle * middle, -1, keepdims=True) + EPSILON)
    low_two = feed_gather((middle * scale_two * full_gain_two).astype(bf16))
    back_feed, activation, own_partial, other_partial, layer_partial = feed_pass(
        low_two, upstream, feed
    )
    back_normed_two, feed_sums = feed_scatter(
        own_partial, other_partial, weight_sums(low_two, back_feed, upstream, activation)
    )
    gradient_feed = scatter(feed_sums, feed_groups)
    weighted = back_normed_two * full_gain_two
    gradient_gain_two = jnp.sum(back_normed_two * middle * scale_two, 0)
    back_middle = (
        own_cotangent.astype(f32)
        + scale_two * weighted
        - middle * scale_two**3 * jnp.mean(weighted * middle, -1, keepdims=True)
    )
    low_middle = group_gather(back_middle.astype(bf16), side)

    back_branches = forward_product(low_middle, full_out)
    back_attended = back_branches[:, SW:].astype(bf16)
    back_rows = back_branches[:, :SW]
    weighted = back_rows * mamba_gain
    gradient_mamba_gain = jnp.sum(back_rows * gated * mamba_scale, 0)
    mean = group_sum(jnp.sum(weighted * gated, -1))[:, None] / DSSM
    back_gated = mamba_scale * weighted - gated * mamba_scale**3 * mean
    back_mixed = back_gated * gate_silu
    low_gate = (
        back_gated * mixed * gate_sigmoid * (1.0 + gate_rows * (1.0 - gate_sigmoid))
    ).astype(bf16)
    back_attended, gradient_feed = lax.optimization_barrier((back_attended, gradient_feed))
    back_query, own_back, other_back = attend_back(
        at, query, key_values, attended, log_total, back_attended, cosine, sine
    )
    other_back = other_back.reshape(2, spans - 1, 2, rows, 2 * HD)
    low_half, high_half = other_back[:, :, 0], other_back[:, :, 1]
    half_back = jnp.where(side == 0, low_half, high_half).astype(f32)
    half_back = half_back + swap_side(jnp.where(side == 0, high_half, low_half)).astype(f32)
    half_back = half_back.astype(bf16)
    back_conv, back_prep, back_skip, *sent = scan_back(
        back_mixed, conv, prepared, turned, skip, state_in, messages
    )
    received = [move_spans(piece, -s) for s, piece in zip(range(1, spans), sent)]
    pieces = [move_spans(half_back[:, s - 1], -s) for s in range(1, spans)]
    back_mix, back_step, back_rim, tap_sums, head_sums = prep_back(
        rim,
        mix_rows,
        step_rows,
        taps,
        heads,
        conv,
        prepared,
        state_in,
        back_conv,
        back_prep,
        back_skip,
        received,
    )
    back_rim = move_spans(back_rim, -1)
    back_all = assemble(
        jnp.reshape(side, (1,)).astype(jnp.int32),
        low_gate,
        back_mix,
        back_rim,
        back_step,
        back_query,
        own_back,
        pieces,
        cosine,
        sine,
    )
    back_all, layer_partial = lax.optimization_barrier((back_all, layer_partial))
    layer_half = layer_partial.shape[0] // 2
    layer_out = middle + feed_scatter(layer_partial[:layer_half], layer_partial[layer_half:])[0]
    gradient_mixer = scatter(
        weight_sums(low_normed, back_all, low_middle, branches), groups
    )
    back_normed = group_scatter(input_product(back_all, mixer), side)
    weighted = back_normed * full_gain
    gradient_gain_one = jnp.sum(back_normed * own_hidden * own_scale_one, 0)
    input_gradient = (
        back_middle
        + own_scale_one * weighted
        - own_hidden * own_scale_one**3 * jnp.mean(weighted * own_hidden, -1, keepdims=True)
    )

    def placed(value, width):
        wide = jnp.zeros(value.shape[:-1] + (width,), f32)
        return lax.dynamic_update_slice_in_dim(
            wide, value, rank * value.shape[-1], value.ndim - 1
        )

    tap_grads = jnp.sum(tap_sums, 0)[: KW + 1]
    tap_grads = jnp.concatenate([placed(tap_grads[:, :SW], DSSM), tap_grads[:, SW:]], 1)
    head_grads = jnp.sum(head_sums, 0)[:3, :SH]
    gain_grads, tap_grads, mamba_gain_grad, head_grads = lax.psum(
        (
            jnp.stack([gradient_gain_one, gradient_gain_two]),
            tap_grads,
            placed(gradient_mamba_gain, DSSM),
            placed(head_grads, MH),
        ),
        BOTH,
    )
    feature_at = (((dp_at // 4 * spans + span_at) * 2 + pair) * TP + rank) * part
    own_gains = lax.dynamic_slice_in_dim(gain_grads, feature_at, part, 1)
    device_at = dp_at * 2 * spans + ctx_at
    own_taps = lax.dynamic_slice_in_dim(tap_grads, device_at * conv_part, conv_part, 1)
    own_mamba_gain = lax.dynamic_slice_in_dim(
        mamba_gain_grad, device_at * gain_part, gain_part, 0
    )

    feed_parts = feed_swap(gradient_feed.reshape(FEED, part, -1), pair, core, side).astype(f32)
    mixer_parts = group_swap(gradient_mixer.reshape(TP, part, -1), core, side).astype(f32)

    def columns(parts, start, width):
        piece = parts[:, :, start : start + width]
        return piece.transpose(1, 0, 2).reshape(part, parts.shape[0] * width)

    def shared(start):
        piece = mixer_parts[:, :, start : start + HD].reshape(KVH, TP // KVH, part, HD)
        return jnp.sum(piece, 1).transpose(1, 0, 2).reshape(part, KVH * HD)

    at = MIXW
    mix_gradient = jnp.concatenate(
        [
            columns(mixer_parts, 0, SW),
            jnp.sum(mixer_parts[:, :, SW:MIXW], 0),
        ],
        1,
    )
    return (
        disorder(layer_out.astype(bf16))[None],
        disorder(input_gradient)[None],
        own_gains[0],
        columns(mixer_parts, WIDE, SW),
        mix_gradient,
        columns(mixer_parts, STEP_AT, SH),
        own_taps[:KW],
        own_taps[KW],
        head_grads[0],
        head_grads[1],
        head_grads[2],
        own_mamba_gain,
        columns(mixer_parts, FULL, SW).T,
        columns(mixer_parts, at, QW),
        shared(at + QW),
        shared(at + QW + HD),
        columns(mixer_parts, FULL + SW, QW).T,
        own_gains[1],
        columns(feed_parts, 0, FW),
        columns(feed_parts, FW, FW),
        columns(feed_parts, 2 * FW, FW).T,
    )


def solution(mesh):
    both = BOTH
    tokens = P("dp", "ctx", None)
    first = P(both, None)
    second = P(None, both)
    vector = P(both)
    whole = P()
    weights = (
        vector,
        first,
        first,
        first,
        second,
        vector,
        whole,
        whole,
        whole,
        vector,
        second,
        first,
        first,
        first,
        second,
        vector,
        first,
        first,
        second,
    )
    return jax.shard_map(
        local,
        mesh=mesh,
        in_specs=(tokens, tokens) + weights,
        out_specs=(tokens, tokens) + weights,
        check_vma=False,
    )
```

```python
import jax
import jax.numpy as jnp
from jax import lax
from jax.experimental import pallas as pl
from jax.experimental.pallas import tpu as pltpu
from jax.sharding import PartitionSpec as P

D = 1024
DSSM = 1536
MH = 24
MP = 64
NS = 128
KW = 4
AH = 8
KVH = 2
HD = 64
FF = 2048
CONV = DSSM + 2 * NS

TP = 4
SW = DSSM // TP
SH = MH // TP
QW = AH * HD // TP
FEED = 8
FW = FF // FEED
LEAD = 8
MIXW = SW + 2 * NS
STEP_AT = MIXW + QW + 2 * HD
VEC = 16
WIDE = 1024
FULL = WIDE + SW

EPSILON = 1e-05
ROPE_BASE = 100000000000.0
HIGHEST = lax.Precision.HIGHEST
NEGATIVE = -1e30
BOTH = ("dp", "ctx")
bf16 = jnp.bfloat16
f32 = jnp.float32


def forward_product(left, right):
    return jnp.dot(left, right, preferred_element_type=f32)


def input_product(upstream, weight):
    return lax.dot_general(
        upstream, weight, (((1,), (1,)), ((), ())), preferred_element_type=f32
    )


def swap_core(value):
    pairs = [(i, i ^ 1) for i in range(lax.axis_size("dp"))]
    return lax.ppermute(value, "dp", pairs)


def swap_side(value):
    pairs = [(i, i ^ 1) for i in range(lax.axis_size("ctx"))]
    return lax.ppermute(value, "ctx", pairs)


def swap_pair(value):
    pairs = [(i, i ^ 2) for i in range(lax.axis_size("dp"))]
    return lax.ppermute(value, "dp", pairs)


def move_spans(value, by):
    blocks = lax.axis_size("ctx")
    pairs = [(i, i + 2 * by) for i in range(blocks) if 0 <= i + 2 * by < blocks]
    return lax.ppermute(value, "ctx", pairs)


def group_gather(value, side):
    other = swap_side(value)
    first = side == 0
    mine = jnp.concatenate([jnp.where(first, value, other), jnp.where(first, other, value)], 0)
    return jnp.concatenate([mine, swap_core(mine)], 0)


def group_scatter(partial, side):
    span = partial.shape[0] // 2
    rows = span // 2
    mine = partial[:span] + swap_core(partial[span:])
    first = side == 0
    keep = jnp.where(first, mine[:rows], mine[rows:])
    send = jnp.where(first, mine[rows:], mine[:rows]).astype(bf16)
    return keep + swap_side(send).astype(f32)


def group_sum(value):
    span = value.shape[0] // 2
    other = swap_core(value)
    value = value + jnp.concatenate([other[span:], other[:span]], 0)
    return value + swap_side(value)


def exchange(parts, axis, bit, swap):
    first = lax.index_in_dim(parts, 0, axis, keepdims=False)
    second = lax.index_in_dim(parts, 1, axis, keepdims=False)
    low = bit == 0
    keep = jnp.where(low, first, second)
    other = swap(jnp.where(low, second, first))
    return jnp.stack([jnp.where(low, keep, other), jnp.where(low, other, keep)], axis)


def group_swap(parts, core, side):
    split = parts.reshape(2, 2, *parts.shape[1:])
    split = exchange(exchange(split, 0, core, swap_core), 1, side, swap_side)
    return split.reshape(parts.shape)


def feed_swap(parts, pair, core, side):
    split = parts.reshape(2, 2, 2, *parts.shape[1:])
    split = exchange(exchange(split, 1, core, swap_core), 2, side, swap_side)
    return exchange(split, 0, pair, swap_pair).reshape(parts.shape)


def both(first, second):
    return lax.optimization_barrier((first, second))


def feed_gather(value):
    half = value.shape[0] // 2
    first, second = value[:half], value[half:]
    first_other, second_other = both(swap_side(first), swap_pair(second))
    first_pair = jnp.concatenate([first, first_other], 0)
    second_pair = jnp.concatenate([second, second_other], 0)
    first_other, second_other = both(swap_pair(first_pair), swap_side(second_pair))
    mine = jnp.concatenate([first_pair, first_other, second_pair, second_other], 0)
    return jnp.concatenate([mine, swap_core(mine)], 0)


def feed_gather_slow(value):
    half = value.shape[0] // 2
    row = jnp.stack([value, swap_side(value)])
    square = jnp.stack([row, swap_pair(row)])
    first = square[:, :, :half].reshape(4 * half, -1)
    second = square[:, :, half:].swapaxes(0, 1).reshape(4 * half, -1)
    mine = jnp.concatenate([first, second], 0)
    return jnp.concatenate([mine, swap_core(mine)], 0)


def feed_scatter(own, other, beside=None):
    part = own.shape[0] // 4

    def meet(first, second, first_swap, second_swap):
        rows = first.shape[0] // 2
        first_other, second_other = both(
            first_swap(first[rows:].astype(bf16)), second_swap(second[rows:].astype(bf16))
        )
        return (
            first[:rows] + first_other.astype(f32),
            second[:rows] + second_other.astype(f32),
        )

    mine = own.astype(f32) + swap_core(other).astype(f32)
    first, second = meet(mine[: 2 * part], mine[2 * part :], swap_pair, swap_side)
    if beside is not None:
        first, second, beside = lax.optimization_barrier((first, second, beside))
    return (jnp.concatenate(meet(first, second, swap_side, swap_pair), 0), beside)


def call(body, grid, in_specs, out_specs, out_shape, scratch=()):
    return pl.pallas_call(
        body,
        grid=grid,
        in_specs=in_specs,
        out_specs=out_specs,
        out_shape=out_shape,
        scratch_shapes=list(scratch),
        compiler_params=pltpu.CompilerParams(vmem_limit_bytes=48 * 1024 * 1024),
    )


def shape(*dims, dtype=f32):
    return jax.ShapeDtypeStruct(dims, dtype)


def row_block(rows, width):
    return pl.BlockSpec((rows, width), lambda b: (b, 0))


def seq_block(*dims):
    return pl.BlockSpec((1,) + dims, lambda b: (b,) + (0,) * len(dims))


def fixed(*dims):
    return pl.BlockSpec(dims, lambda b: (0,) * len(dims))


SCALAR = pl.BlockSpec(memory_space=pltpu.SMEM)


def product(left, right, left_dim=1, right_dim=0):
    return lax.dot_general(
        left, right, (((left_dim,), (right_dim,)), ((), ())), preferred_element_type=f32
    )


def halves(value):
    high = value.astype(bf16)
    return high, (value - high.astype(f32)).astype(bf16)


def fine_product(left, right, left_dim=1, right_dim=0):
    left_high, left_low = halves(left)
    right_high, right_low = halves(right)
    return (
        product(left_high, right_high, left_dim, right_dim)
        + product(left_high, right_low, left_dim, right_dim)
        + product(left_low, right_high, left_dim, right_dim)
    )


def head_mask():
    row = lax.broadcasted_iota(jnp.int32, (128, SW), 0)
    column = lax.broadcasted_iota(jnp.int32, (128, SW), 1)
    return jnp.where(column // MP == row, 1.0, 0.0).astype(bf16)


def spread_heads(value, mask):
    high, low = halves(value)
    return product(high, mask) + product(low, mask)


def sum_heads(value, mask):
    high, low = halves(value)
    return product(high, mask, 1, 1) + product(low, mask, 1, 1)


def rope_tables(positions):
    ladder = jnp.arange(HD // 2, dtype=f32)
    rates = ROPE_BASE ** (-2.0 * ladder / HD)
    angles = positions.astype(f32)[:, None] * rates[None, :]
    cosine, sine = jnp.cos(angles), jnp.sin(angles)
    return (
        jnp.concatenate([cosine] * 4, 1),
        jnp.concatenate([-sine, sine, -sine, sine], 1),
    )


def turn(value, cosine, sine):
    lane = lax.broadcasted_iota(jnp.int32, value.shape, 1)
    half = HD // 2
    other = jnp.where(
        lane % HD < half, pltpu.roll(value, 128 - half, 1), pltpu.roll(value, half, 1)
    )
    return value * cosine + other * sine


def turn_first(value, cosine, sine):
    lane = lax.broadcasted_iota(jnp.int32, value.shape, 1)
    return jnp.where(lane < HD, turn(value, cosine, sine), value)


def project_kernel(
    hidden,
    rim_hidden,
    weight,
    cosine,
    sine,
    normed_out,
    mix_out,
    query_out,
    key_value_out,
    step_out,
    gain_out,
    rim_out,
):
    def norm(value):
        wide = value.astype(f32)
        scale = lax.rsqrt(jnp.mean(wide * wide, -1, keepdims=True) + EPSILON)
        return (wide * scale * gains[SH : SH + 1]).astype(bf16)

    gains = weight[:, STEP_AT:WIDE].astype(f32).T
    gain_out[...] = gains[SH : SH + 2]
    rim_out[0] = product(norm(rim_hidden[0]), weight[:, :MIXW])[16 - LEAD :].astype(bf16)
    normed = norm(hidden[...])
    normed_out[...] = normed
    rows = product(normed, weight[...])
    mix_out[...] = rows[:, :MIXW].astype(bf16)
    at = MIXW
    query_out[...] = turn(rows[:, at : at + QW], cosine[...], sine[...]).astype(bf16)
    at += QW
    pair = turn_first(rows[:, at : at + 2 * HD], cosine[...], sine[...])
    key_value_out[...] = pair.astype(bf16)
    tail = rows[:, STEP_AT:WIDE]
    lane = lax.broadcasted_iota(jnp.int32, tail.shape, 1)
    step_out[...] = jnp.where(lane < SH, tail, 0.0)


def project(hidden, rim_hidden, weight, cosine, sine):
    count = hidden.shape[0]
    span = count // 2
    return call(
        project_kernel,
        (2,),
        [
            row_block(span, D),
            seq_block(16, D),
            fixed(*weight.shape),
            fixed(span, 128),
            fixed(span, 128),
        ],
        [
            row_block(span, D),
            row_block(span, MIXW),
            row_block(span, QW),
            row_block(span, 128),
            row_block(span, 128),
            fixed(2, D),
            seq_block(LEAD, MIXW),
        ],
        [
            shape(count, D, dtype=bf16),
            shape(count, MIXW, dtype=bf16),
            shape(count, QW, dtype=bf16),
            shape(count, 128, dtype=bf16),
            shape(count, 128),
            shape(2, D),
            shape(2, LEAD, MIXW, dtype=bf16),
        ],
    )(hidden, rim_hidden, weight, cosine, sine)


def feed_kernel(
    normed, upstream, gate_up, down, back_out, activation_out, own_out, other_out, layer_out
):
    pre = product(normed[...], gate_up[...])
    gate, up = pre[:, :FW], pre[:, FW:]
    sigmoid = 1.0 / (1.0 + jnp.exp(-gate))
    silu = gate * sigmoid
    activation = (silu * up).astype(bf16)
    activation_out[...] = activation
    back = product(upstream[...], down[...])
    back_gate = back * up * sigmoid * (1.0 + gate * (1.0 - sigmoid))
    back_feed = jnp.concatenate([back_gate.astype(bf16), (back * silu).astype(bf16)], 1)
    back_out[...] = back_feed
    partial = product(back_feed, gate_up[...], 1, 1)
    mine = pl.program_id(0) < pl.num_programs(0) // 2

    @pl.when(mine)
    def _():
        own_out[...] = partial

    @pl.when(jnp.logical_not(mine))
    def _():
        other_out[...] = partial.astype(bf16)

    layer_out[...] = product(activation, down[...], 1, 1).astype(bf16)


def feed_pass(normed, upstream, feed):
    count = normed.shape[0]
    rows = count // 2
    return call(
        feed_kernel,
        (2,),
        [
            row_block(rows, D),
            row_block(rows, D),
            fixed(D, 2 * FW),
            pl.BlockSpec((D, FW), lambda b: (0, 2)),
        ],
        [
            row_block(rows, 2 * FW),
            row_block(rows, FW),
            pl.BlockSpec((rows, D), lambda b: (0, 0)),
            pl.BlockSpec((rows, D), lambda b: (0, 0)),
            row_block(rows, D),
        ],
        [
            shape(count, 2 * FW, dtype=bf16),
            shape(count, FW, dtype=bf16),
            shape(count // 2, D),
            shape(count // 2, D, dtype=bf16),
            shape(count, D, dtype=bf16),
        ],
    )(normed, upstream, feed, feed)


def visible_keys(span, keys, at):
    query = lax.broadcasted_iota(jnp.int32, (span, keys), 0)
    key = lax.broadcasted_iota(jnp.int32, (span, keys), 1)
    return (key < span) & (key <= query) | (key >= span) & (key < (at + 1) * span)


def attend_kernel(at, query, key_value, attended_out, total_out):
    span, keys = query.shape[0], key_value.shape[1]
    visible = visible_keys(span, keys, at[0])
    pair = key_value[0]
    for h in range(QW // HD):
        part = slice(h * HD, (h + 1) * HD)
        scores = product(query[:, part], pair[:, :HD], 1, 1) * HD ** (-0.5)
        scores = jnp.where(visible, scores, NEGATIVE)
        peak = jnp.max(scores, -1, keepdims=True)
        weights = jnp.exp(scores - peak)
        total = jnp.sum(weights, -1, keepdims=True)
        summed = product(weights.astype(bf16), pair[:, HD:])
        attended_out[:, part] = (summed / total).astype(bf16)
        total_out[:, part] = jnp.broadcast_to(peak + jnp.log(total), (span, HD))


def attend(at, query, key_values):
    count = query.shape[0]
    span = count // 2
    return call(
        attend_kernel,
        (2,),
        [SCALAR, row_block(span, QW), seq_block(*key_values.shape[1:])],
        [row_block(span, QW), row_block(span, QW)],
        [shape(count, QW, dtype=bf16), shape(count, QW)],
    )(at, query, key_values)


def attend_back_kernel(
    at, query, key_value, attended, log_total, back, cosine, sine, query_out, own_out, other_out
):
    span, keys = query.shape[0], key_value.shape[1]
    scale = HD ** (-0.5)
    visible = visible_keys(span, keys, at[0])
    pair = key_value[0]
    back_pair = jnp.zeros((keys, 2 * HD), f32)
    turned = []
    for h in range(QW // HD):
        part = slice(h * HD, (h + 1) * HD)
        head = query[:, part]
        upstream = back[:, part]
        delta = jnp.sum(
            upstream.astype(f32) * attended[:, part].astype(f32), -1, keepdims=True
        )
        scores = product(head, pair[:, :HD], 1, 1) * scale
        chance = jnp.where(visible, jnp.exp(scores - log_total[:, part][:, :1]), 0.0)
        back_chance = product(upstream, pair[:, HD:], 1, 1)
        back_scores = (chance * (back_chance - delta) * scale).astype(bf16)
        turned.append(product(back_scores, pair[:, :HD]))
        back_pair = back_pair + jnp.concatenate(
            [product(back_scores, head, 0, 0), product(chance.astype(bf16), upstream, 0, 0)], 1
        )
    query_out[...] = turn(jnp.concatenate(turned, 1), cosine[...], -sine[...]).astype(bf16)
    own_out[0] = back_pair[:span]
    other_out[0] = back_pair[span:].astype(bf16)


def attend_back(at, query, key_values, attended, log_total, back, cosine, sine):
    count = query.shape[0]
    span = count // 2
    keys = key_values.shape[1]
    return call(
        attend_back_kernel,
        (2,),
        [SCALAR, row_block(span, QW), seq_block(keys, 2 * HD)]
        + [row_block(span, QW)] * 3
        + [fixed(span, 128)] * 2,
        [row_block(span, QW), seq_block(span, 2 * HD), seq_block(keys - span, 2 * HD)],
        [
            shape(count, QW, dtype=bf16),
            shape(2, span, 2 * HD),
            shape(2, keys - span, 2 * HD, dtype=bf16),
        ],
    )(at, query, key_values, attended, log_total, back, cosine, sine)


def extend(scratch, rim, mix):
    scratch[0:LEAD] = rim[0].astype(f32)
    scratch[LEAD:] = mix[...].astype(f32)


def prep_kernel(rim, mix, step, taps, heads, conv_out, prep_out, turned_out, message_out, ext):
    rows = mix.shape[0]
    extend(ext, rim, mix)
    conv = taps[KW : KW + 1] + taps[0:1] * ext[pl.ds(LEAD - KW + 1, rows)]
    for tap in range(1, KW):
        conv = conv + taps[tap : tap + 1] * ext[pl.ds(LEAD - KW + 1 + tap, rows)]
    conv = conv / (1.0 + jnp.exp(-conv))
    conv_out[...] = conv
    lane = lax.broadcasted_iota(jnp.int32, step.shape, 1)
    raw = step[...] + heads[0:1]
    steps = jnp.maximum(raw, 0.0) + jnp.log1p(jnp.exp(-jnp.abs(raw)))
    steps = jnp.where(lane < SH, steps, 0.0)
    rate = -jnp.exp(heads[1:2]) * steps
    below = lax.broadcasted_iota(jnp.int32, (rows, rows), 0)
    along = lax.broadcasted_iota(jnp.int32, (rows, rows), 1)
    lower = jnp.where(below >= along, 1.0, 0.0)
    curve = lax.dot_general(
        lower, rate, (((1,), (0,)), ((), ())), precision=HIGHEST, preferred_element_type=f32
    )
    prep_out[:, :128] = steps
    prep_out[:, 128:] = curve
    turned_out[0, :8] = steps.T[:8]
    turned_out[0, 8:] = curve.T[:8]
    last = curve[rows - 1 : rows]
    weights = jnp.exp(last - curve) * steps
    mask = head_mask()
    scaled = spread_heads(weights, mask) * conv[:, :SW]
    state = fine_product(scaled, conv[:, SW : SW + NS], 0, 0)
    message_out[0, :SW] = state.astype(bf16)
    high = last.astype(bf16)
    low = (last - high.astype(f32)).astype(bf16)
    row = lax.broadcasted_iota(jnp.int32, (16, 128), 0)
    tail = jnp.where(row == 0, high.astype(f32), jnp.where(row == 1, low.astype(f32), 0.0))
    message_out[0, SW:] = tail.astype(bf16)


def prep(rim, mix, step, taps, heads):
    count = mix.shape[0]
    rows = count // 2
    return call(
        prep_kernel,
        (2,),
        [
            seq_block(LEAD, MIXW),
            row_block(rows, MIXW),
            row_block(rows, 128),
            fixed(8, MIXW),
            fixed(8, 128),
        ],
        [
            row_block(rows, MIXW),
            row_block(rows, 256),
            seq_block(16, rows),
            seq_block(SW + 16, NS),
        ],
        [
            shape(count, MIXW),
            shape(count, 256),
            shape(2, 16, rows),
            shape(2, SW + 16, NS, dtype=bf16),
        ],
        [pltpu.VMEM((LEAD + rows, MIXW), f32)],
    )(rim, mix, step, taps, heads)


def head_column(tail):
    row = lax.broadcasted_iota(jnp.int32, (SW, 128), 0)
    lane = lax.broadcasted_iota(jnp.int32, (SW, 128), 1)
    return jnp.sum(jnp.where(row // MP == lane, tail, 0.0), 1, keepdims=True)


def decay_of(message, at):
    return message[0, at : at + 1].astype(f32) + message[0, at + 1 : at + 2].astype(f32)


def scan_kernel(
    parts, conv, prep, turned, skip, *refs
):
    messages = refs[:parts]
    mixed_out, state_out = refs[parts:]
    rows = conv.shape[0]
    between = jnp.zeros((1, 128), f32)
    state = jnp.zeros((SW, NS), f32)
    for message in messages:
        state = state + jnp.exp(head_column(between)) * message[0, :SW].astype(f32)
        between = between + decay_of(message, SW)
    state_out[0] = state
    entry = conv[:, SW : SW + NS]
    readout = conv[:, SW + NS :]
    meeting = fine_product(readout, entry, 1, 1)
    below = lax.broadcasted_iota(jnp.int32, (rows, rows), 0)
    along = lax.broadcasted_iota(jnp.int32, (rows, rows), 1)
    causal = below >= along
    meeting = jnp.where(causal, meeting, 0.0)
    parts_out = []
    for h in range(SH):
        spread = prep[:, 128 + h : 129 + h] - turned[0, 8 + h : 9 + h]
        mixing = jnp.exp(jnp.where(causal, spread, 0.0)) * meeting * turned[0, h : h + 1]
        signal = conv[:, MP * h : MP * (h + 1)].astype(bf16)
        parts_out.append(product(mixing.astype(bf16), signal))
    signal = conv[:, :SW]
    carried = fine_product(readout, state, 1, 1)
    grown = spread_heads(jnp.exp(prep[:, 128:]), head_mask())
    mixed = jnp.concatenate(parts_out, 1) + carried * grown + skip[...] * signal
    mixed_out[...] = mixed


def scan(conv, prepared, turned, skip, messages):
    count = conv.shape[0]
    rows = count // 2
    return call(
        lambda *refs: scan_kernel(len(messages), *refs),
        (2,),
        [
            row_block(rows, MIXW),
            row_block(rows, 256),
            seq_block(16, rows),
            fixed(1, SW),
        ]
        + [seq_block(SW + 16, NS)] * len(messages),
        [row_block(rows, SW), seq_block(SW, NS)],
        [shape(count, SW), shape(2, SW, NS)],
    )(conv, prepared, turned, skip, *messages)


def scan_back_kernel(parts, back, conv, prep, turned, skip, state, *refs):
    tails = refs[:parts]
    conv_out, prep_out, skip_out = refs[parts : parts + 3]
    sent_out = refs[parts + 3 :]
    rows = conv.shape[0]
    mask = head_mask()
    entry = conv[:, SW : SW + NS]
    readout = conv[:, SW + NS :]
    signal = conv[:, :SW]
    upstream = back[...]
    meeting = fine_product(readout, entry, 1, 1)
    below = lax.broadcasted_iota(jnp.int32, (rows, rows), 0)
    along = lax.broadcasted_iota(jnp.int32, (rows, rows), 1)
    causal = below >= along
    back_meeting = jnp.zeros((rows, rows), f32)
    lane = lax.broadcasted_iota(jnp.int32, (rows, 128), 1)
    place = lax.broadcasted_iota(jnp.int32, (8, rows), 0)
    back_steps = jnp.zeros((8, rows), f32)
    curve_along = jnp.zeros((8, rows), f32)
    back_curve = jnp.zeros((rows, 128), f32)
    back_signal = []
    for h in range(SH):
        part = slice(MP * h, MP * (h + 1))
        spread = prep[:, 128 + h : 129 + h] - turned[0, 8 + h : 9 + h]
        decay = jnp.where(causal, jnp.exp(jnp.where(causal, spread, 0.0)), 0.0)
        step = turned[0, h : h + 1]
        head_back = upstream[:, part].astype(bf16)
        back_mixing = product(head_back, signal[:, part].astype(bf16), 1, 1) * decay
        back_meeting = back_meeting + back_mixing * step
        scaled = back_mixing * meeting
        down = jnp.sum(scaled, 0, keepdims=True)
        across = jnp.sum(scaled * step, 1, keepdims=True)
        back_steps = jnp.where(place == h, down, back_steps)
        curve_along = jnp.where(place == h, -down * step, curve_along)
        back_curve = jnp.where(lane == h, across, back_curve)
        mixing = (decay * meeting * step).astype(bf16)
        back_signal.append(product(mixing, head_back, 0, 0))
    fold = jnp.concatenate([back_steps, curve_along, jnp.zeros((112, rows), f32)], 0).T
    grown = spread_heads(jnp.exp(prep[:, 128:]), mask)
    back_carried = upstream * grown
    carried = fine_product(readout, state[0], 1, 1)
    back_curve = back_curve + sum_heads(back_carried * carried, mask)
    back_curve = back_curve + jnp.where(lane < SH, pltpu.roll(fold, 120, 1), 0.0)
    conv_out[:, :SW] = jnp.concatenate(back_signal, 1) + skip[...] * upstream
    conv_out[:, SW : SW + NS] = fine_product(back_meeting, readout, 0, 0)
    conv_out[:, SW + NS :] = fine_product(back_meeting, entry) + fine_product(
        back_carried, state[0]
    )
    prep_out[:, :128] = jnp.where(lane < SH, fold, 0.0)
    prep_out[:, 128:] = back_curve
    back_skip = jnp.sum(upstream * signal, 0, keepdims=True)
    skip_out[0] = jnp.broadcast_to(sum_heads(jnp.broadcast_to(back_skip, (8, SW)), mask), (8, 128))
    back_state = fine_product(back_carried, readout, 0, 0)
    between = jnp.zeros((1, 128), f32)
    for tail, sent in zip(tails, sent_out):
        sent[0] = (jnp.exp(head_column(between)) * back_state).astype(bf16)
        between = between + decay_of(tail, 0)


def scan_back(back, conv, prepared, turned, skip, state, messages):
    count = conv.shape[0]
    rows = count // 2
    tail = pl.BlockSpec((1, 16, NS), lambda b: (b, SW // 16, 0))
    return call(
        lambda *refs: scan_back_kernel(len(messages), *refs),
        (2,),
        [
            row_block(rows, SW),
            row_block(rows, MIXW),
            row_block(rows, 256),
            seq_block(16, rows),
            fixed(1, SW),
            seq_block(SW, NS),
        ]
        + [tail] * len(messages),
        [row_block(rows, MIXW), row_block(rows, 256), seq_block(8, 128)]
        + [seq_block(SW, NS)] * len(messages),
        [shape(count, MIXW), shape(count, 256), shape(2, 8, 128)]
        + [shape(2, SW, NS, dtype=bf16)] * len(messages),
    )(back, conv, prepared, turned, skip, state, *messages)


def prep_back_kernel(
    parts,
    rim,
    mix,
    step,
    taps,
    heads,
    conv,
    prep,
    state,
    back_conv,
    back_prep,
    back_skip,
    *refs,
):
    received = refs[:parts]
    mix_out, step_out, rim_out, tap_out, head_out, ext, padded = refs[parts:]
    rows = mix.shape[0]
    mask = head_mask()
    next_back = jnp.zeros((SW, NS), f32)
    for piece in received:
        next_back = next_back + piece[0].astype(f32)
    steps, curve = prep[:, :128], prep[:, 128:]
    last = curve[rows - 1 : rows]
    decay = jnp.exp(last - curve)
    wide = spread_heads(decay * steps, mask)
    signal = conv[:, :SW]
    entry = conv[:, SW : SW + NS]
    back_scaled = fine_product(entry, next_back, 1, 1)
    back_weights = sum_heads(back_scaled * signal, mask)
    both = back_weights * decay
    back_steps = back_prep[:, :128] + both
    weighed = both * steps
    whole = jnp.sum(next_back * state[0], 1, keepdims=True)
    row = lax.broadcasted_iota(jnp.int32, (SW, 128), 0)
    lane = lax.broadcasted_iota(jnp.int32, (SW, 128), 1)
    whole = jnp.sum(jnp.where(row // MP == lane, whole, 0.0), 0, keepdims=True) * jnp.exp(last)
    at_last = lax.broadcasted_iota(jnp.int32, (rows, 128), 0) == rows - 1
    back_curve = back_prep[:, 128:] - weighed
    back_curve = back_curve + jnp.where(
        at_last, jnp.sum(weighed, 0, keepdims=True) + whole, 0.0
    )
    below = lax.broadcasted_iota(jnp.int32, (rows, rows), 0)
    along = lax.broadcasted_iota(jnp.int32, (rows, rows), 1)
    upper = jnp.where(below <= along, 1.0, 0.0)
    back_rate = lax.dot_general(
        upper, back_curve, (((1,), (0,)), ((), ())), precision=HIGHEST, preferred_element_type=f32
    )
    pace = -jnp.exp(heads[1:2])
    back_decay = jnp.sum(back_rate * pace * steps, 0, keepdims=True)
    raw = step[...] + heads[0:1]
    back_steps = (back_steps + back_rate * pace) / (1.0 + jnp.exp(-raw))
    wide_lane = lax.broadcasted_iota(jnp.int32, (rows, 128), 1)
    back_steps = jnp.where(wide_lane < SH, back_steps, 0.0)
    step_out[...] = back_steps
    place = lax.broadcasted_iota(jnp.int32, (8, 128), 0)
    total = jnp.where(place == 0, jnp.sum(back_steps, 0, keepdims=True), 0.0)
    total = jnp.where(place == 1, back_decay, total)
    head_out[0] = jnp.where(place == 2, back_skip[0], total)

    extend(ext, rim, mix)
    before = taps[KW : KW + 1] + taps[0:1] * ext[pl.ds(LEAD - KW + 1, rows)]
    for tap in range(1, KW):
        before = before + taps[tap : tap + 1] * ext[pl.ds(LEAD - KW + 1 + tap, rows)]
    sigmoid = 1.0 / (1.0 + jnp.exp(-before))
    slope = sigmoid * (1.0 + before * (1.0 - sigmoid))
    scaled = wide * signal
    upstream = jnp.concatenate(
        [
            back_conv[:, :SW] + back_scaled * wide,
            back_conv[:, SW : SW + NS] + fine_product(scaled, next_back),
            back_conv[:, SW + NS :],
        ],
        1,
    )
    back = upstream * slope
    place = lax.broadcasted_iota(jnp.int32, (8, MIXW), 0)
    sums = jnp.where(place == KW, jnp.sum(back, 0, keepdims=True), 0.0)
    for tap in range(KW):
        moved = jnp.sum(back * ext[pl.ds(LEAD - KW + 1 + tap, rows)], 0, keepdims=True)
        sums = jnp.where(place == tap, moved, sums)
    tap_out[0] = sums
    padded[0:LEAD] = jnp.zeros((LEAD, MIXW), f32)
    padded[LEAD : LEAD + rows] = back
    padded[LEAD + rows :] = jnp.zeros((LEAD, MIXW), f32)
    result = taps[KW - 1 : KW] * back
    first = jnp.zeros((LEAD, MIXW), f32)
    for tap in range(KW):
        if tap < KW - 1:
            result = result + taps[tap : tap + 1] * padded[pl.ds(LEAD + KW - 1 - tap, rows)]
        first = first + taps[tap : tap + 1] * padded[pl.ds(LEAD - tap, LEAD)]
    mix_out[...] = result
    rim_out[0] = jnp.where(place < KW - 1, first, 0.0)


def prep_back(rim, mix, step, taps, heads, conv, prepared, state, back_conv, back_prep, back_skip, received):
    count = mix.shape[0]
    rows = count // 2
    return call(
        lambda *refs: prep_back_kernel(len(received), *refs),
        (2,),
        [
            seq_block(LEAD, MIXW),
            row_block(rows, MIXW),
            row_block(rows, 128),
            fixed(8, MIXW),
            fixed(8, 128),
            row_block(rows, MIXW),
            row_block(rows, 256),
            seq_block(SW, NS),
            row_block(rows, MIXW),
            row_block(rows, 256),
            seq_block(8, 128),
        ]
        + [seq_block(SW, NS)] * len(received),
        [
            row_block(rows, MIXW),
            row_block(rows, 128),
            seq_block(LEAD, MIXW),
            seq_block(8, MIXW),
            seq_block(8, 128),
        ],
        [
            shape(count, MIXW),
            shape(count, 128),
            shape(2, LEAD, MIXW),
            shape(2, 8, MIXW),
            shape(2, 8, 128),
        ],
        [
            pltpu.VMEM((LEAD + rows, MIXW), f32),
            pltpu.VMEM((rows + 2 * LEAD, MIXW), f32),
        ],
    )(
        rim,
        mix,
        step,
        taps,
        heads,
        conv,
        prepared,
        state,
        back_conv,
        back_prep,
        back_skip,
        *received,
    )


def assemble_kernel(parts, side, gate, mix, rim, step, query, own, cosine, sine, *refs):
    received, out = refs[:parts], refs[parts]
    rows = mix.shape[0]
    out[:, WIDE:] = gate[...]
    mixed = slice(0, MIXW)
    out[:, mixed] = mix[...].astype(bf16)
    tail = mix[rows - 16 :]
    returned = jnp.concatenate([jnp.zeros((16 - LEAD, MIXW), f32), rim[0]], 0)
    tail = tail + pltpu.roll(returned, LEAD - KW + 1, 0)
    out[rows - 16 :, mixed] = tail.astype(bf16)
    at = MIXW
    out[:, at : at + QW] = query[...]
    half = jnp.zeros((rows // 2, 2 * HD), f32)
    for piece in received:
        half = half + piece[0].astype(f32)
    row = lax.broadcasted_iota(jnp.int32, (rows, 2 * HD), 0)
    pair = own[0] + jnp.where(row // (rows // 2) == side[0], jnp.concatenate([half, half], 0), 0.0)
    at += QW
    out[:, at : at + 2 * HD] = turn_first(pair, cosine[...], -sine[...]).astype(bf16)
    out[:, STEP_AT:WIDE] = step[...].astype(bf16)


def assemble(side, gate, mix, rim, step, query, own, received, cosine, sine):
    count = mix.shape[0]
    rows = count // 2
    return call(
        lambda *refs: assemble_kernel(len(received), *refs),
        (2,),
        [
            SCALAR,
            row_block(rows, SW),
            row_block(rows, MIXW),
            seq_block(LEAD, MIXW),
            row_block(rows, 128),
            row_block(rows, QW),
            seq_block(rows, 2 * HD),
            fixed(rows, 128),
            fixed(rows, 128),
        ]
        + [seq_block(rows // 2, 2 * HD)] * len(received),
        row_block(rows, FULL),
        shape(count, FULL, dtype=bf16),
    )(side, gate, mix, rim, step, query, own, cosine, sine, *received)


def sums_kernel(first_left, first_right, second_left, second_right, out):
    width = first_right.shape[1]
    out[:, :width] = product(first_left[...], first_right[...], 0, 0).astype(bf16)
    out[:, width:] = product(second_left[...], second_right[...], 0, 0).astype(bf16)


def weight_sums(first_left, first_right, second_left, second_right):
    count = first_left.shape[0]
    wide, more = first_right.shape[1], second_right.shape[1]
    rows = 512
    left = pl.BlockSpec((count, rows), lambda b: (0, b))
    return call(
        sums_kernel,
        (D // rows,),
        [left, fixed(count, wide), left, fixed(count, more)],
        row_block(rows, wide + more),
        shape(D, wide + more, dtype=bf16),
    )(first_left, first_right, second_left, second_right)


def local(
    tokens,
    out_cotangent,
    input_gain,
    mamba_gate_weight,
    mamba_mix_weight,
    mamba_step_weight,
    conv_kernel,
    conv_offset,
    step_offset,
    decay_log,
    skip_scale,
    mamba_norm_gain,
    mamba_out_weight,
    query_weight,
    key_weight,
    value_weight,
    attention_out_weight,
    ffn_gain,
    feed_gate_weight,
    feed_up_weight,
    feed_down_weight,
):
    rows = tokens.shape[1]
    span = 2 * rows
    count = 2 * span
    quads, spans = lax.axis_size("dp") // 4, lax.axis_size("ctx") // 2
    devices = 8 * quads * spans
    dp_at, ctx_at = lax.axis_index("dp"), lax.axis_index("ctx")
    side, span_at = ctx_at % 2, ctx_at // 2
    core, pair = dp_at % 2, dp_at // 2 % 2
    rank = core * 2 + side
    part = D // devices
    conv_part = CONV // devices
    gain_part = DSSM // devices
    groups = [
        [
            ((quad * 2 + y) * 2 + c) * 2 * spans + z * 2 + x
            for quad in range(quads)
            for z in range(spans)
            for y in range(2)
        ]
        for c in range(2)
        for x in range(2)
    ]
    feed_groups = [
        [(quad * 4 + d) * 2 * spans + z * 2 + x for quad in range(quads) for z in range(spans)]
        for d in range(4)
        for x in range(2)
    ]

    def order(value):
        lead = value.shape[:-1]
        value = value.reshape(*lead, quads, 4, spans, 2 * part)
        return jnp.swapaxes(value, -3, -2).reshape(*lead, D)

    def disorder(value):
        lead = value.shape[:-1]
        value = value.reshape(*lead, quads, spans, 4, 2 * part)
        return jnp.swapaxes(value, -3, -2).reshape(*lead, D)

    def gather(value, groups):
        return lax.all_gather(value, BOTH, axis=0, tiled=True, axis_index_groups=groups)

    def scatter(value, groups):
        return lax.psum_scatter(
            value, BOTH, scatter_dimension=0, tiled=True, axis_index_groups=groups
        )

    vector = jnp.concatenate([conv_kernel.reshape(-1), conv_offset, mamba_norm_gain])
    vector = jnp.pad(vector, (0, part * (VEC - 2) - vector.shape[0])).reshape(part, VEC - 2)
    tail = jnp.concatenate(
        [
            input_gain[:, None],
            ffn_gain[:, None],
            vector,
            jnp.zeros((part, WIDE - STEP_AT - SH - VEC), bf16),
        ],
        1,
    )
    def mixer_part(s):
        kv = s // 2
        return jnp.concatenate(
            [
                mamba_mix_weight[:, SW * s : SW * (s + 1)],
                mamba_mix_weight[:, DSSM:],
                query_weight[:, QW * s : QW * (s + 1)],
                key_weight[:, HD * kv : HD * (kv + 1)],
                value_weight[:, HD * kv : HD * (kv + 1)],
                mamba_step_weight[:, SH * s : SH * (s + 1)],
                tail,
            ],
            1,
        )

    mixer_own = group_swap(jnp.stack([mixer_part(s) for s in range(TP)]), core, side)
    later = (
        mamba_gate_weight,
        mamba_out_weight,
        attention_out_weight,
        feed_gate_weight,
        feed_up_weight,
        feed_down_weight,
        tokens,
        out_cotangent,
    )
    mixer_own, later = lax.optimization_barrier((mixer_own, later))
    mamba_gate_weight, mamba_out_weight, attention_out_weight = later[:3]
    feed_gate_weight, feed_up_weight, feed_down_weight, tokens, out_cotangent = later[3:]
    mixer = gather(mixer_own.reshape(TP * part, -1), groups)
    mamba_out_turned = mamba_out_weight.T
    attention_out_turned = attention_out_weight.T
    feed_down_turned = feed_down_weight.T

    def branch_part(s):
        return jnp.concatenate(
            [
                mamba_gate_weight[:, SW * s : SW * (s + 1)],
                mamba_out_turned[:, SW * s : SW * (s + 1)],
                attention_out_turned[:, QW * s : QW * (s + 1)],
            ],
            1,
        )

    branch_own = group_swap(jnp.stack([branch_part(s) for s in range(TP)]), core, side)
    branch_own = branch_own.reshape(TP * part, -1)
    def feed_part(s):
        return jnp.concatenate(
            [
                feed_gate_weight[:, FW * s : FW * (s + 1)],
                feed_up_weight[:, FW * s : FW * (s + 1)],
                feed_down_turned[:, FW * s : FW * (s + 1)],
            ],
            1,
        )

    feed_own = feed_swap(jnp.stack([feed_part(s) for s in range(FEED)]), pair, core, side)
    feed_own = feed_own.reshape(FEED * part, -1)
    own_low = order(tokens[0])
    own_hidden = own_low.astype(f32)
    own_scale_one = lax.rsqrt(jnp.mean(own_hidden * own_hidden, -1, keepdims=True) + EPSILON)
    hidden = group_gather(own_low, side)
    own_cotangent = order(out_cotangent[0])
    cosine, sine = rope_tables(span_at * span + jnp.arange(span, dtype=jnp.int32))
    upstream = feed_gather_slow(own_cotangent)
    rim_hidden = move_spans(hidden.reshape(2, span, D)[:, span - 16 :], 1)
    branch_own, feed_own, mixer, hidden, rim_hidden, upstream, cosine, sine = (
        lax.optimization_barrier(
            (branch_own, feed_own, mixer, hidden, rim_hidden, upstream, cosine, sine)
        )
    )
    branch = gather(branch_own, groups)
    full_gate, full_out = branch[:, :SW], branch[:, SW:]
    feed = gather(feed_own, feed_groups)

    at = STEP_AT + SH + 2
    vectors = mixer[:, at : at + VEC - 2]
    natural = vectors.reshape(quads, spans, 4, 2, part * (VEC - 2))
    natural = natural.transpose(0, 2, 1, 3, 4).reshape(devices, part * (VEC - 2))
    at = 0
    all_kernel = natural[:, at : at + KW * conv_part].reshape(devices, KW, conv_part)
    all_kernel = all_kernel.transpose(1, 0, 2).reshape(KW, CONV)
    at += KW * conv_part
    all_offset = natural[:, at : at + conv_part].reshape(1, CONV)
    at += conv_part
    all_mamba_gain = natural[:, at : at + gain_part].reshape(DSSM)
    taps = jnp.concatenate([all_kernel, all_offset], 0)
    taps = jnp.concatenate(
        [lax.dynamic_slice_in_dim(taps, rank * SW, SW, 1), taps[:, DSSM:]], 1
    ).astype(f32)
    kernel, offset = taps[:KW], taps[KW]
    mamba_gain = lax.dynamic_slice_in_dim(all_mamba_gain, rank * SW, SW, 0).astype(f32)
    own_step_offset = lax.dynamic_slice_in_dim(step_offset, rank * SH, SH, 0)
    own_decay_log = lax.dynamic_slice_in_dim(decay_log, rank * SH, SH, 0)
    own_skip = lax.dynamic_slice_in_dim(skip_scale, rank * SH, SH, 0)

    at = jnp.reshape(span_at, (1,)).astype(jnp.int32)
    taps = jnp.pad(taps, ((0, 8 - taps.shape[0]), (0, 0)))
    heads = jnp.stack([own_step_offset, own_decay_log])
    heads = jnp.pad(heads, ((0, 6), (0, 128 - SH)))
    skip = jnp.repeat(own_skip, MP)[None]

    low_normed, mix_rows, query, key_value, step_rows, gains, rim = project(
        hidden, rim_hidden, mixer, cosine, sine
    )
    full_gain, full_gain_two = gains[0], gains[1]
    key_value = key_value.reshape(2, span, 2 * HD)
    half = jnp.where(side == 0, key_value[:, :rows], key_value[:, rows:])
    halves_in = jnp.stack([move_spans(half, s) for s in range(1, spans)], 1)
    halves_other = swap_side(halves_in)
    reached = jnp.stack(
        [
            jnp.where(side == 0, halves_in, halves_other),
            jnp.where(side == 0, halves_other, halves_in),
        ],
        2,
    ).reshape(2, (spans - 1) * span, 2 * HD)
    key_values = jnp.concatenate([key_value, reached], 1)
    conv, prepared, turned, message = prep(rim, mix_rows, step_rows, taps, heads)
    messages = [move_spans(message, s) for s in range(1, spans)]
    attended, log_total = attend(at, query, key_values)
    mixed, state_in = scan(conv, prepared, turned, skip, messages)
    gate_rows = forward_product(low_normed, full_gate)
    gate_sigmoid = jax.nn.sigmoid(gate_rows)
    gate_silu = gate_rows * gate_sigmoid
    gated = mixed * gate_silu
    square = group_sum(jnp.sum(gated * gated, -1))
    mamba_scale = lax.rsqrt(square / DSSM + EPSILON)[:, None]
    mamba_rows = (gated * mamba_scale * mamba_gain).astype(bf16)
    branches = jnp.concatenate([mamba_rows, attended], 1)
    middle = own_hidden + group_scatter(input_product(branches, full_out), side)
    middle, feed = lax.optimization_barrier((middle, feed))

    scale_two = lax.rsqrt(jnp.mean(middle * middle, -1, keepdims=True) + EPSILON)
    low_two = feed_gather((middle * scale_two * full_gain_two).astype(bf16))
    back_feed, activation, own_partial, other_partial, layer_partial = feed_pass(
        low_two, upstream, feed
    )
    back_normed_two, feed_sums = feed_scatter(
        own_partial, other_partial, weight_sums(low_two, back_feed, upstream, activation)
    )
    gradient_feed = scatter(feed_sums, feed_groups)
    weighted = back_normed_two * full_gain_two
    gradient_gain_two = jnp.sum(back_normed_two * middle * scale_two, 0)
    back_middle = (
        own_cotangent.astype(f32)
        + scale_two * weighted
        - middle * scale_two**3 * jnp.mean(weighted * middle, -1, keepdims=True)
    )
    low_middle = group_gather(back_middle.astype(bf16), side)

    back_branches = forward_product(low_middle, full_out)
    back_attended = back_branches[:, SW:].astype(bf16)
    back_rows = back_branches[:, :SW]
    weighted = back_rows * mamba_gain
    gradient_mamba_gain = jnp.sum(back_rows * gated * mamba_scale, 0)
    mean = group_sum(jnp.sum(weighted * gated, -1))[:, None] / DSSM
    back_gated = mamba_scale * weighted - gated * mamba_scale**3 * mean
    back_mixed = back_gated * gate_silu
    low_gate = (
        back_gated * mixed * gate_sigmoid * (1.0 + gate_rows * (1.0 - gate_sigmoid))
    ).astype(bf16)
    back_attended, gradient_feed = lax.optimization_barrier((back_attended, gradient_feed))
    back_query, own_back, other_back = attend_back(
        at, query, key_values, attended, log_total, back_attended, cosine, sine
    )
    other_back = other_back.reshape(2, spans - 1, 2, rows, 2 * HD)
    low_half, high_half = other_back[:, :, 0], other_back[:, :, 1]
    half_back = jnp.where(side == 0, low_half, high_half).astype(f32)
    half_back = half_back + swap_side(jnp.where(side == 0, high_half, low_half)).astype(f32)
    half_back = half_back.astype(bf16)
    back_conv, back_prep, back_skip, *sent = scan_back(
        back_mixed, conv, prepared, turned, skip, state_in, messages
    )
    received = [move_spans(piece, -s) for s, piece in zip(range(1, spans), sent)]
    pieces = [move_spans(half_back[:, s - 1], -s) for s in range(1, spans)]
    back_mix, back_step, back_rim, tap_sums, head_sums = prep_back(
        rim,
        mix_rows,
        step_rows,
        taps,
        heads,
        conv,
        prepared,
        state_in,
        back_conv,
        back_prep,
        back_skip,
        received,
    )
    back_rim = move_spans(back_rim, -1)
    back_all = assemble(
        jnp.reshape(side, (1,)).astype(jnp.int32),
        low_gate,
        back_mix,
        back_rim,
        back_step,
        back_query,
        own_back,
        pieces,
        cosine,
        sine,
    )
    back_all, layer_partial = lax.optimization_barrier((back_all, layer_partial))
    layer_half = layer_partial.shape[0] // 2
    layer_out = middle + feed_scatter(layer_partial[:layer_half], layer_partial[layer_half:])[0]
    gradient_mixer = scatter(
        weight_sums(low_normed, back_all, low_middle, branches), groups
    )
    back_normed = group_scatter(
        input_product(back_all[:, :WIDE], mixer) + input_product(back_all[:, WIDE:], full_gate),
        side,
    )
    weighted = back_normed * full_gain
    gradient_gain_one = jnp.sum(back_normed * own_hidden * own_scale_one, 0)
    input_gradient = (
        back_middle
        + own_scale_one * weighted
        - own_hidden * own_scale_one**3 * jnp.mean(weighted * own_hidden, -1, keepdims=True)
    )

    def placed(value, width):
        wide = jnp.zeros(value.shape[:-1] + (width,), f32)
        return lax.dynamic_update_slice_in_dim(
            wide, value, rank * value.shape[-1], value.ndim - 1
        )

    tap_grads = jnp.sum(tap_sums, 0)[: KW + 1]
    tap_grads = jnp.concatenate([placed(tap_grads[:, :SW], DSSM), tap_grads[:, SW:]], 1)
    head_grads = jnp.sum(head_sums, 0)[:3, :SH]
    gain_grads, tap_grads, mamba_gain_grad, head_grads = lax.psum(
        (
            jnp.stack([gradient_gain_one, gradient_gain_two]),
            tap_grads,
            placed(gradient_mamba_gain, DSSM),
            placed(head_grads, MH),
        ),
        BOTH,
    )
    feature_at = (((dp_at // 4 * spans + span_at) * 2 + pair) * TP + rank) * part
    own_gains = lax.dynamic_slice_in_dim(gain_grads, feature_at, part, 1)
    device_at = dp_at * 2 * spans + ctx_at
    own_taps = lax.dynamic_slice_in_dim(tap_grads, device_at * conv_part, conv_part, 1)
    own_mamba_gain = lax.dynamic_slice_in_dim(
        mamba_gain_grad, device_at * gain_part, gain_part, 0
    )

    feed_parts = feed_swap(gradient_feed.reshape(FEED, part, -1), pair, core, side).astype(f32)
    mixer_parts = group_swap(gradient_mixer.reshape(TP, part, -1), core, side).astype(f32)

    def columns(parts, start, width):
        piece = parts[:, :, start : start + width]
        return piece.transpose(1, 0, 2).reshape(part, parts.shape[0] * width)

    def shared(start):
        piece = mixer_parts[:, :, start : start + HD].reshape(KVH, TP // KVH, part, HD)
        return jnp.sum(piece, 1).transpose(1, 0, 2).reshape(part, KVH * HD)

    at = MIXW
    mix_gradient = jnp.concatenate(
        [
            columns(mixer_parts, 0, SW),
            jnp.sum(mixer_parts[:, :, SW:MIXW], 0),
        ],
        1,
    )
    return (
        disorder(layer_out.astype(bf16))[None],
        disorder(input_gradient)[None],
        own_gains[0],
        columns(mixer_parts, WIDE, SW),
        mix_gradient,
        columns(mixer_parts, STEP_AT, SH),
        own_taps[:KW],
        own_taps[KW],
        head_grads[0],
        head_grads[1],
        head_grads[2],
        own_mamba_gain,
        columns(mixer_parts, FULL, SW).T,
        columns(mixer_parts, at, QW),
        shared(at + QW),
        shared(at + QW + HD),
        columns(mixer_parts, FULL + SW, QW).T,
        own_gains[1],
        columns(feed_parts, 0, FW),
        columns(feed_parts, FW, FW),
        columns(feed_parts, 2 * FW, FW).T,
    )


def solution(mesh):
    both = BOTH
    tokens = P("dp", "ctx", None)
    first = P(both, None)
    second = P(None, both)
    vector = P(both)
    whole = P()
    weights = (
        vector,
        first,
        first,
        first,
        second,
        vector,
        whole,
        whole,
        whole,
        vector,
        second,
        first,
        first,
        first,
        second,
        vector,
        first,
        first,
        second,
    )
    return jax.shard_map(
        local,
        mesh=mesh,
        in_specs=(tokens, tokens) + weights,
        out_specs=(tokens, tokens) + weights,
        check_vma=False,
    )
```

```python
import jax
import jax.numpy as jnp
from jax import lax
from jax.experimental import pallas as pl
from jax.experimental.pallas import tpu as pltpu
from jax.sharding import PartitionSpec as P

D = 1024
DSSM = 1536
MH = 24
MP = 64
NS = 128
KW = 4
AH = 8
KVH = 2
HD = 64
FF = 2048
CONV = DSSM + 2 * NS

TP = 4
SW = DSSM // TP
SH = MH // TP
QW = AH * HD // TP
FEED = 8
FW = FF // FEED
LEAD = 8
MIXW = SW + 2 * NS
STEP_AT = MIXW + QW + 2 * HD
VEC = 16
WIDE = 1024
FULL = WIDE + SW

EPSILON = 1e-05
ROPE_BASE = 100000000000.0
HIGHEST = lax.Precision.HIGHEST
NEGATIVE = -1e30
BOTH = ("dp", "ctx")
bf16 = jnp.bfloat16
f32 = jnp.float32


def forward_product(left, right):
    return jnp.dot(left, right, preferred_element_type=f32)


def input_product(upstream, weight):
    return lax.dot_general(
        upstream, weight, (((1,), (1,)), ((), ())), preferred_element_type=f32
    )


def swap_core(value):
    pairs = [(i, i ^ 1) for i in range(lax.axis_size("dp"))]
    return lax.ppermute(value, "dp", pairs)


def swap_side(value):
    pairs = [(i, i ^ 1) for i in range(lax.axis_size("ctx"))]
    return lax.ppermute(value, "ctx", pairs)


def swap_pair(value):
    pairs = [(i, i ^ 2) for i in range(lax.axis_size("dp"))]
    return lax.ppermute(value, "dp", pairs)


def move_spans(value, by):
    blocks = lax.axis_size("ctx")
    pairs = [(i, i + 2 * by) for i in range(blocks) if 0 <= i + 2 * by < blocks]
    return lax.ppermute(value, "ctx", pairs)


def group_gather(value, side):
    other = swap_side(value)
    first = side == 0
    mine = jnp.concatenate([jnp.where(first, value, other), jnp.where(first, other, value)], 0)
    return jnp.concatenate([mine, swap_core(mine)], 0)


def group_scatter(partial, side):
    span = partial.shape[0] // 2
    rows = span // 2
    mine = partial[:span] + swap_core(partial[span:])
    first = side == 0
    keep = jnp.where(first, mine[:rows], mine[rows:])
    send = jnp.where(first, mine[rows:], mine[:rows]).astype(bf16)
    return keep + swap_side(send).astype(f32)


def group_sum(value):
    span = value.shape[0] // 2
    other = swap_core(value)
    value = value + jnp.concatenate([other[span:], other[:span]], 0)
    return value + swap_side(value)


def exchange(parts, axis, bit, swap):
    first = lax.index_in_dim(parts, 0, axis, keepdims=False)
    second = lax.index_in_dim(parts, 1, axis, keepdims=False)
    low = bit == 0
    keep = jnp.where(low, first, second)
    other = swap(jnp.where(low, second, first))
    return jnp.stack([jnp.where(low, keep, other), jnp.where(low, other, keep)], axis)


def group_swap(parts, core, side):
    split = parts.reshape(2, 2, *parts.shape[1:])
    split = exchange(exchange(split, 0, core, swap_core), 1, side, swap_side)
    return split.reshape(parts.shape)


def feed_swap(parts, pair, core, side):
    split = parts.reshape(2, 2, 2, *parts.shape[1:])
    split = exchange(exchange(split, 1, core, swap_core), 2, side, swap_side)
    return exchange(split, 0, pair, swap_pair).reshape(parts.shape)


def both(first, second):
    return lax.optimization_barrier((first, second))


def feed_gather(value):
    half = value.shape[0] // 2
    first, second = value[:half], value[half:]
    first_other, second_other = both(swap_side(first), swap_pair(second))
    first_pair = jnp.concatenate([first, first_other], 0)
    second_pair = jnp.concatenate([second, second_other], 0)
    first_other, second_other = both(swap_pair(first_pair), swap_side(second_pair))
    mine = jnp.concatenate([first_pair, first_other, second_pair, second_other], 0)
    return jnp.concatenate([mine, swap_core(mine)], 0)


def feed_gather_slow(value):
    half = value.shape[0] // 2
    row = jnp.stack([value, swap_side(value)])
    square = jnp.stack([row, swap_pair(row)])
    first = square[:, :, :half].reshape(4 * half, -1)
    second = square[:, :, half:].swapaxes(0, 1).reshape(4 * half, -1)
    mine = jnp.concatenate([first, second], 0)
    return jnp.concatenate([mine, swap_core(mine)], 0)


def feed_scatter(own, other, beside=None):
    part = own.shape[0] // 4

    def meet(first, second, first_swap, second_swap):
        rows = first.shape[0] // 2
        first_other, second_other = both(
            first_swap(first[rows:].astype(bf16)), second_swap(second[rows:].astype(bf16))
        )
        return (
            first[:rows] + first_other.astype(f32),
            second[:rows] + second_other.astype(f32),
        )

    mine = own.astype(f32) + swap_core(other).astype(f32)
    first, second = meet(mine[: 2 * part], mine[2 * part :], swap_pair, swap_side)
    if beside is not None:
        first, second, beside = lax.optimization_barrier((first, second, beside))
    return (jnp.concatenate(meet(first, second, swap_side, swap_pair), 0), beside)


def call(body, grid, in_specs, out_specs, out_shape, scratch=()):
    return pl.pallas_call(
        body,
        grid=grid,
        in_specs=in_specs,
        out_specs=out_specs,
        out_shape=out_shape,
        scratch_shapes=list(scratch),
        compiler_params=pltpu.CompilerParams(vmem_limit_bytes=48 * 1024 * 1024),
    )


def shape(*dims, dtype=f32):
    return jax.ShapeDtypeStruct(dims, dtype)


def row_block(rows, width):
    return pl.BlockSpec((rows, width), lambda b: (b, 0))


def seq_block(*dims):
    return pl.BlockSpec((1,) + dims, lambda b: (b,) + (0,) * len(dims))


def fixed(*dims):
    return pl.BlockSpec(dims, lambda b: (0,) * len(dims))


SCALAR = pl.BlockSpec(memory_space=pltpu.SMEM)


def product(left, right, left_dim=1, right_dim=0):
    return lax.dot_general(
        left, right, (((left_dim,), (right_dim,)), ((), ())), preferred_element_type=f32
    )


def halves(value):
    high = value.astype(bf16)
    return high, (value - high.astype(f32)).astype(bf16)


def fine_product(left, right, left_dim=1, right_dim=0):
    left_high, left_low = halves(left)
    right_high, right_low = halves(right)
    return (
        product(left_high, right_high, left_dim, right_dim)
        + product(left_high, right_low, left_dim, right_dim)
        + product(left_low, right_high, left_dim, right_dim)
    )


def low_product(left, right, left_dim=1, right_dim=0):
    return product(left.astype(bf16), right.astype(bf16), left_dim, right_dim)


def head_mask():
    row = lax.broadcasted_iota(jnp.int32, (128, SW), 0)
    column = lax.broadcasted_iota(jnp.int32, (128, SW), 1)
    return jnp.where(column // MP == row, 1.0, 0.0).astype(bf16)


def spread_heads(value, mask):
    high, low = halves(value)
    return product(high, mask) + product(low, mask)


def sum_heads(value, mask):
    high, low = halves(value)
    return product(high, mask, 1, 1) + product(low, mask, 1, 1)


def rope_tables(positions):
    ladder = jnp.arange(HD // 2, dtype=f32)
    rates = ROPE_BASE ** (-2.0 * ladder / HD)
    angles = positions.astype(f32)[:, None] * rates[None, :]
    cosine, sine = jnp.cos(angles), jnp.sin(angles)
    return (
        jnp.concatenate([cosine] * 4, 1),
        jnp.concatenate([-sine, sine, -sine, sine], 1),
    )


def turn(value, cosine, sine):
    lane = lax.broadcasted_iota(jnp.int32, value.shape, 1)
    half = HD // 2
    other = jnp.where(
        lane % HD < half, pltpu.roll(value, 128 - half, 1), pltpu.roll(value, half, 1)
    )
    return value * cosine + other * sine


def turn_first(value, cosine, sine):
    lane = lax.broadcasted_iota(jnp.int32, value.shape, 1)
    return jnp.where(lane < HD, turn(value, cosine, sine), value)


def project_kernel(
    hidden,
    rim_hidden,
    weight,
    cosine,
    sine,
    normed_out,
    mix_out,
    query_out,
    key_value_out,
    step_out,
    gain_out,
    rim_out,
):
    def norm(value):
        wide = value.astype(f32)
        scale = lax.rsqrt(jnp.mean(wide * wide, -1, keepdims=True) + EPSILON)
        return (wide * scale * gains[SH : SH + 1]).astype(bf16)

    gains = weight[:, STEP_AT:WIDE].astype(f32).T
    gain_out[...] = gains[SH : SH + 2]
    rim_out[0] = product(norm(rim_hidden[0]), weight[:, :MIXW])[16 - LEAD :].astype(bf16)
    normed = norm(hidden[...])
    normed_out[...] = normed
    rows = product(normed, weight[...])
    mix_out[...] = rows[:, :MIXW].astype(bf16)
    at = MIXW
    query_out[...] = turn(rows[:, at : at + QW], cosine[...], sine[...]).astype(bf16)
    at += QW
    pair = turn_first(rows[:, at : at + 2 * HD], cosine[...], sine[...])
    key_value_out[...] = pair.astype(bf16)
    tail = rows[:, STEP_AT:WIDE]
    lane = lax.broadcasted_iota(jnp.int32, tail.shape, 1)
    step_out[...] = jnp.where(lane < SH, tail, 0.0)


def project(hidden, rim_hidden, weight, cosine, sine):
    count = hidden.shape[0]
    span = count // 2
    return call(
        project_kernel,
        (2,),
        [
            row_block(span, D),
            seq_block(16, D),
            fixed(*weight.shape),
            fixed(span, 128),
            fixed(span, 128),
        ],
        [
            row_block(span, D),
            row_block(span, MIXW),
            row_block(span, QW),
            row_block(span, 128),
            row_block(span, 128),
            fixed(2, D),
            seq_block(LEAD, MIXW),
        ],
        [
            shape(count, D, dtype=bf16),
            shape(count, MIXW, dtype=bf16),
            shape(count, QW, dtype=bf16),
            shape(count, 128, dtype=bf16),
            shape(count, 128),
            shape(2, D),
            shape(2, LEAD, MIXW, dtype=bf16),
        ],
    )(hidden, rim_hidden, weight, cosine, sine)


def feed_kernel(
    normed, upstream, gate_up, down, back_out, activation_out, own_out, other_out, layer_out
):
    pre = product(normed[...], gate_up[...])
    gate, up = pre[:, :FW], pre[:, FW:]
    sigmoid = 1.0 / (1.0 + jnp.exp(-gate))
    silu = gate * sigmoid
    activation = (silu * up).astype(bf16)
    activation_out[...] = activation
    back = product(upstream[...], down[...])
    back_gate = back * up * sigmoid * (1.0 + gate * (1.0 - sigmoid))
    back_feed = jnp.concatenate([back_gate.astype(bf16), (back * silu).astype(bf16)], 1)
    back_out[...] = back_feed
    partial = product(back_feed, gate_up[...], 1, 1)
    mine = pl.program_id(0) < pl.num_programs(0) // 2

    @pl.when(mine)
    def _():
        own_out[...] = partial

    @pl.when(jnp.logical_not(mine))
    def _():
        other_out[...] = partial.astype(bf16)

    layer_out[...] = product(activation, down[...], 1, 1).astype(bf16)


def feed_pass(normed, upstream, feed):
    count = normed.shape[0]
    rows = count // 2
    return call(
        feed_kernel,
        (2,),
        [
            row_block(rows, D),
            row_block(rows, D),
            fixed(D, 2 * FW),
            pl.BlockSpec((D, FW), lambda b: (0, 2)),
        ],
        [
            row_block(rows, 2 * FW),
            row_block(rows, FW),
            pl.BlockSpec((rows, D), lambda b: (0, 0)),
            pl.BlockSpec((rows, D), lambda b: (0, 0)),
            row_block(rows, D),
        ],
        [
            shape(count, 2 * FW, dtype=bf16),
            shape(count, FW, dtype=bf16),
            shape(count // 2, D),
            shape(count // 2, D, dtype=bf16),
            shape(count, D, dtype=bf16),
        ],
    )(normed, upstream, feed, feed)


def visible_keys(span, keys, at):
    query = lax.broadcasted_iota(jnp.int32, (span, keys), 0)
    key = lax.broadcasted_iota(jnp.int32, (span, keys), 1)
    return (key < span) & (key <= query) | (key >= span) & (key < (at + 1) * span)


def attend_kernel(at, query, key_value, attended_out, total_out):
    span, keys = query.shape[0], key_value.shape[1]
    visible = visible_keys(span, keys, at[0])
    pair = key_value[0]
    for h in range(QW // HD):
        part = slice(h * HD, (h + 1) * HD)
        scores = product(query[:, part], pair[:, :HD], 1, 1) * HD ** (-0.5)
        scores = jnp.where(visible, scores, NEGATIVE)
        peak = jnp.max(scores, -1, keepdims=True)
        weights = jnp.exp(scores - peak)
        total = jnp.sum(weights, -1, keepdims=True)
        summed = product(weights.astype(bf16), pair[:, HD:])
        attended_out[:, part] = (summed / total).astype(bf16)
        total_out[:, part] = jnp.broadcast_to(peak + jnp.log(total), (span, HD))


def attend(at, query, key_values):
    count = query.shape[0]
    span = count // 2
    return call(
        attend_kernel,
        (2,),
        [SCALAR, row_block(span, QW), seq_block(*key_values.shape[1:])],
        [row_block(span, QW), row_block(span, QW)],
        [shape(count, QW, dtype=bf16), shape(count, QW)],
    )(at, query, key_values)


def attend_back_kernel(
    at, query, key_value, attended, log_total, back, cosine, sine, query_out, own_out, other_out
):
    span, keys = query.shape[0], key_value.shape[1]
    scale = HD ** (-0.5)
    visible = visible_keys(span, keys, at[0])
    pair = key_value[0]
    back_pair = jnp.zeros((keys, 2 * HD), f32)
    turned = []
    for h in range(QW // HD):
        part = slice(h * HD, (h + 1) * HD)
        head = query[:, part]
        upstream = back[:, part]
        delta = jnp.sum(
            upstream.astype(f32) * attended[:, part].astype(f32), -1, keepdims=True
        )
        scores = product(head, pair[:, :HD], 1, 1) * scale
        chance = jnp.where(visible, jnp.exp(scores - log_total[:, part][:, :1]), 0.0)
        back_chance = product(upstream, pair[:, HD:], 1, 1)
        back_scores = (chance * (back_chance - delta) * scale).astype(bf16)
        turned.append(product(back_scores, pair[:, :HD]))
        back_pair = back_pair + jnp.concatenate(
            [product(back_scores, head, 0, 0), product(chance.astype(bf16), upstream, 0, 0)], 1
        )
    query_out[...] = turn(jnp.concatenate(turned, 1), cosine[...], -sine[...]).astype(bf16)
    own_out[0] = back_pair[:span]
    other_out[0] = back_pair[span:].astype(bf16)


def attend_back(at, query, key_values, attended, log_total, back, cosine, sine):
    count = query.shape[0]
    span = count // 2
    keys = key_values.shape[1]
    return call(
        attend_back_kernel,
        (2,),
        [SCALAR, row_block(span, QW), seq_block(keys, 2 * HD)]
        + [row_block(span, QW)] * 3
        + [fixed(span, 128)] * 2,
        [row_block(span, QW), seq_block(span, 2 * HD), seq_block(keys - span, 2 * HD)],
        [
            shape(count, QW, dtype=bf16),
            shape(2, span, 2 * HD),
            shape(2, keys - span, 2 * HD, dtype=bf16),
        ],
    )(at, query, key_values, attended, log_total, back, cosine, sine)


def extend(scratch, rim, mix):
    scratch[0:LEAD] = rim[0].astype(f32)
    scratch[LEAD:] = mix[...].astype(f32)


def prep_kernel(rim, mix, step, taps, heads, conv_out, prep_out, turned_out, message_out, ext):
    rows = mix.shape[0]
    extend(ext, rim, mix)
    conv = taps[KW : KW + 1] + taps[0:1] * ext[pl.ds(LEAD - KW + 1, rows)]
    for tap in range(1, KW):
        conv = conv + taps[tap : tap + 1] * ext[pl.ds(LEAD - KW + 1 + tap, rows)]
    conv = conv / (1.0 + jnp.exp(-conv))
    conv_out[...] = conv
    lane = lax.broadcasted_iota(jnp.int32, step.shape, 1)
    raw = step[...] + heads[0:1]
    steps = jnp.maximum(raw, 0.0) + jnp.log1p(jnp.exp(-jnp.abs(raw)))
    steps = jnp.where(lane < SH, steps, 0.0)
    rate = -jnp.exp(heads[1:2]) * steps
    below = lax.broadcasted_iota(jnp.int32, (rows, rows), 0)
    along = lax.broadcasted_iota(jnp.int32, (rows, rows), 1)
    lower = jnp.where(below >= along, 1.0, 0.0)
    curve = lax.dot_general(
        lower, rate, (((1,), (0,)), ((), ())), precision=HIGHEST, preferred_element_type=f32
    )
    prep_out[:, :128] = steps
    prep_out[:, 128:] = curve
    turned_out[0, :8] = steps.T[:8]
    turned_out[0, 8:] = curve.T[:8]
    last = curve[rows - 1 : rows]
    weights = jnp.exp(last - curve) * steps
    mask = head_mask()
    scaled = spread_heads(weights, mask) * conv[:, :SW]
    state = fine_product(scaled, conv[:, SW : SW + NS], 0, 0)
    message_out[0, :SW] = state.astype(bf16)
    high = last.astype(bf16)
    low = (last - high.astype(f32)).astype(bf16)
    row = lax.broadcasted_iota(jnp.int32, (16, 128), 0)
    tail = jnp.where(row == 0, high.astype(f32), jnp.where(row == 1, low.astype(f32), 0.0))
    message_out[0, SW:] = tail.astype(bf16)


def prep(rim, mix, step, taps, heads):
    count = mix.shape[0]
    rows = count // 2
    return call(
        prep_kernel,
        (2,),
        [
            seq_block(LEAD, MIXW),
            row_block(rows, MIXW),
            row_block(rows, 128),
            fixed(8, MIXW),
            fixed(8, 128),
        ],
        [
            row_block(rows, MIXW),
            row_block(rows, 256),
            seq_block(16, rows),
            seq_block(SW + 16, NS),
        ],
        [
            shape(count, MIXW),
            shape(count, 256),
            shape(2, 16, rows),
            shape(2, SW + 16, NS, dtype=bf16),
        ],
        [pltpu.VMEM((LEAD + rows, MIXW), f32)],
    )(rim, mix, step, taps, heads)


def head_column(tail):
    row = lax.broadcasted_iota(jnp.int32, (SW, 128), 0)
    lane = lax.broadcasted_iota(jnp.int32, (SW, 128), 1)
    return jnp.sum(jnp.where(row // MP == lane, tail, 0.0), 1, keepdims=True)


def decay_of(message, at):
    return message[0, at : at + 1].astype(f32) + message[0, at + 1 : at + 2].astype(f32)


def scan_kernel(
    parts, conv, prep, turned, skip, *refs
):
    messages = refs[:parts]
    mixed_out, state_out = refs[parts:]
    rows = conv.shape[0]
    between = jnp.zeros((1, 128), f32)
    state = jnp.zeros((SW, NS), f32)
    for message in messages:
        state = state + jnp.exp(head_column(between)) * message[0, :SW].astype(f32)
        between = between + decay_of(message, SW)
    state_out[0] = state
    entry = conv[:, SW : SW + NS]
    readout = conv[:, SW + NS :]
    meeting = fine_product(readout, entry, 1, 1)
    below = lax.broadcasted_iota(jnp.int32, (rows, rows), 0)
    along = lax.broadcasted_iota(jnp.int32, (rows, rows), 1)
    causal = below >= along
    meeting = jnp.where(causal, meeting, 0.0)
    parts_out = []
    for h in range(SH):
        spread = prep[:, 128 + h : 129 + h] - turned[0, 8 + h : 9 + h]
        mixing = jnp.exp(jnp.where(causal, spread, 0.0)) * meeting * turned[0, h : h + 1]
        signal = conv[:, MP * h : MP * (h + 1)].astype(bf16)
        parts_out.append(product(mixing.astype(bf16), signal))
    signal = conv[:, :SW]
    carried = fine_product(readout, state, 1, 1)
    grown = spread_heads(jnp.exp(prep[:, 128:]), head_mask())
    mixed = jnp.concatenate(parts_out, 1) + carried * grown + skip[...] * signal
    mixed_out[...] = mixed


def scan(conv, prepared, turned, skip, messages):
    count = conv.shape[0]
    rows = count // 2
    return call(
        lambda *refs: scan_kernel(len(messages), *refs),
        (2,),
        [
            row_block(rows, MIXW),
            row_block(rows, 256),
            seq_block(16, rows),
            fixed(1, SW),
        ]
        + [seq_block(SW + 16, NS)] * len(messages),
        [row_block(rows, SW), seq_block(SW, NS)],
        [shape(count, SW), shape(2, SW, NS)],
    )(conv, prepared, turned, skip, *messages)


def scan_back_kernel(parts, back, conv, prep, turned, skip, state, *refs):
    tails = refs[:parts]
    conv_out, prep_out, skip_out = refs[parts : parts + 3]
    sent_out = refs[parts + 3 :]
    rows = conv.shape[0]
    mask = head_mask()
    entry = conv[:, SW : SW + NS]
    readout = conv[:, SW + NS :]
    signal = conv[:, :SW]
    upstream = back[...]
    meeting = fine_product(readout, entry, 1, 1)
    below = lax.broadcasted_iota(jnp.int32, (rows, rows), 0)
    along = lax.broadcasted_iota(jnp.int32, (rows, rows), 1)
    causal = below >= along
    back_meeting = jnp.zeros((rows, rows), f32)
    lane = lax.broadcasted_iota(jnp.int32, (rows, 128), 1)
    place = lax.broadcasted_iota(jnp.int32, (8, rows), 0)
    back_steps = jnp.zeros((8, rows), f32)
    curve_along = jnp.zeros((8, rows), f32)
    back_curve = jnp.zeros((rows, 128), f32)
    back_signal = []
    for h in range(SH):
        part = slice(MP * h, MP * (h + 1))
        spread = prep[:, 128 + h : 129 + h] - turned[0, 8 + h : 9 + h]
        decay = jnp.where(causal, jnp.exp(jnp.where(causal, spread, 0.0)), 0.0)
        step = turned[0, h : h + 1]
        head_back = upstream[:, part].astype(bf16)
        back_mixing = product(head_back, signal[:, part].astype(bf16), 1, 1) * decay
        back_meeting = back_meeting + back_mixing * step
        scaled = back_mixing * meeting
        down = jnp.sum(scaled, 0, keepdims=True)
        across = jnp.sum(scaled * step, 1, keepdims=True)
        back_steps = jnp.where(place == h, down, back_steps)
        curve_along = jnp.where(place == h, -down * step, curve_along)
        back_curve = jnp.where(lane == h, across, back_curve)
        mixing = (decay * meeting * step).astype(bf16)
        back_signal.append(product(mixing, head_back, 0, 0))
    fold = jnp.concatenate([back_steps, curve_along, jnp.zeros((112, rows), f32)], 0).T
    grown = spread_heads(jnp.exp(prep[:, 128:]), mask)
    back_carried = upstream * grown
    carried = fine_product(readout, state[0], 1, 1)
    back_curve = back_curve + sum_heads(back_carried * carried, mask)
    back_curve = back_curve + jnp.where(lane < SH, pltpu.roll(fold, 120, 1), 0.0)
    conv_out[:, :SW] = jnp.concatenate(back_signal, 1) + skip[...] * upstream
    conv_out[:, SW : SW + NS] = low_product(back_meeting, readout, 0, 0)
    conv_out[:, SW + NS :] = low_product(back_meeting, entry) + low_product(
        back_carried, state[0]
    )
    prep_out[:, :128] = jnp.where(lane < SH, fold, 0.0)
    prep_out[:, 128:] = back_curve
    back_skip = jnp.sum(upstream * signal, 0, keepdims=True)
    skip_out[0] = jnp.broadcast_to(sum_heads(jnp.broadcast_to(back_skip, (8, SW)), mask), (8, 128))
    back_state = low_product(back_carried, readout, 0, 0)
    between = jnp.zeros((1, 128), f32)
    for tail, sent in zip(tails, sent_out):
        sent[0] = (jnp.exp(head_column(between)) * back_state).astype(bf16)
        between = between + decay_of(tail, 0)


def scan_back(back, conv, prepared, turned, skip, state, messages):
    count = conv.shape[0]
    rows = count // 2
    tail = pl.BlockSpec((1, 16, NS), lambda b: (b, SW // 16, 0))
    return call(
        lambda *refs: scan_back_kernel(len(messages), *refs),
        (2,),
        [
            row_block(rows, SW),
            row_block(rows, MIXW),
            row_block(rows, 256),
            seq_block(16, rows),
            fixed(1, SW),
            seq_block(SW, NS),
        ]
        + [tail] * len(messages),
        [row_block(rows, MIXW), row_block(rows, 256), seq_block(8, 128)]
        + [seq_block(SW, NS)] * len(messages),
        [shape(count, MIXW), shape(count, 256), shape(2, 8, 128)]
        + [shape(2, SW, NS, dtype=bf16)] * len(messages),
    )(back, conv, prepared, turned, skip, state, *messages)


def prep_back_kernel(
    parts,
    rim,
    mix,
    step,
    taps,
    heads,
    conv,
    prep,
    state,
    back_conv,
    back_prep,
    back_skip,
    *refs,
):
    received = refs[:parts]
    mix_out, step_out, rim_out, tap_out, head_out, ext, padded = refs[parts:]
    rows = mix.shape[0]
    mask = head_mask()
    next_back = jnp.zeros((SW, NS), f32)
    for piece in received:
        next_back = next_back + piece[0].astype(f32)
    steps, curve = prep[:, :128], prep[:, 128:]
    last = curve[rows - 1 : rows]
    decay = jnp.exp(last - curve)
    wide = spread_heads(decay * steps, mask)
    signal = conv[:, :SW]
    entry = conv[:, SW : SW + NS]
    back_scaled = low_product(entry, next_back, 1, 1)
    back_weights = sum_heads(back_scaled * signal, mask)
    both = back_weights * decay
    back_steps = back_prep[:, :128] + both
    weighed = both * steps
    whole = jnp.sum(next_back * state[0], 1, keepdims=True)
    row = lax.broadcasted_iota(jnp.int32, (SW, 128), 0)
    lane = lax.broadcasted_iota(jnp.int32, (SW, 128), 1)
    whole = jnp.sum(jnp.where(row // MP == lane, whole, 0.0), 0, keepdims=True) * jnp.exp(last)
    at_last = lax.broadcasted_iota(jnp.int32, (rows, 128), 0) == rows - 1
    back_curve = back_prep[:, 128:] - weighed
    back_curve = back_curve + jnp.where(
        at_last, jnp.sum(weighed, 0, keepdims=True) + whole, 0.0
    )
    below = lax.broadcasted_iota(jnp.int32, (rows, rows), 0)
    along = lax.broadcasted_iota(jnp.int32, (rows, rows), 1)
    upper = jnp.where(below <= along, 1.0, 0.0)
    back_rate = lax.dot_general(
        upper, back_curve, (((1,), (0,)), ((), ())), precision=HIGHEST, preferred_element_type=f32
    )
    pace = -jnp.exp(heads[1:2])
    back_decay = jnp.sum(back_rate * pace * steps, 0, keepdims=True)
    raw = step[...] + heads[0:1]
    back_steps = (back_steps + back_rate * pace) / (1.0 + jnp.exp(-raw))
    wide_lane = lax.broadcasted_iota(jnp.int32, (rows, 128), 1)
    back_steps = jnp.where(wide_lane < SH, back_steps, 0.0)
    step_out[...] = back_steps
    place = lax.broadcasted_iota(jnp.int32, (8, 128), 0)
    total = jnp.where(place == 0, jnp.sum(back_steps, 0, keepdims=True), 0.0)
    total = jnp.where(place == 1, back_decay, total)
    head_out[0] = jnp.where(place == 2, back_skip[0], total)

    extend(ext, rim, mix)
    before = taps[KW : KW + 1] + taps[0:1] * ext[pl.ds(LEAD - KW + 1, rows)]
    for tap in range(1, KW):
        before = before + taps[tap : tap + 1] * ext[pl.ds(LEAD - KW + 1 + tap, rows)]
    sigmoid = 1.0 / (1.0 + jnp.exp(-before))
    slope = sigmoid * (1.0 + before * (1.0 - sigmoid))
    scaled = wide * signal
    upstream = jnp.concatenate(
        [
            back_conv[:, :SW] + back_scaled * wide,
            back_conv[:, SW : SW + NS] + low_product(scaled, next_back),
            back_conv[:, SW + NS :],
        ],
        1,
    )
    back = upstream * slope
    place = lax.broadcasted_iota(jnp.int32, (8, MIXW), 0)
    sums = jnp.where(place == KW, jnp.sum(back, 0, keepdims=True), 0.0)
    for tap in range(KW):
        moved = jnp.sum(back * ext[pl.ds(LEAD - KW + 1 + tap, rows)], 0, keepdims=True)
        sums = jnp.where(place == tap, moved, sums)
    tap_out[0] = sums
    padded[0:LEAD] = jnp.zeros((LEAD, MIXW), f32)
    padded[LEAD : LEAD + rows] = back
    padded[LEAD + rows :] = jnp.zeros((LEAD, MIXW), f32)
    result = taps[KW - 1 : KW] * back
    first = jnp.zeros((LEAD, MIXW), f32)
    for tap in range(KW):
        if tap < KW - 1:
            result = result + taps[tap : tap + 1] * padded[pl.ds(LEAD + KW - 1 - tap, rows)]
        first = first + taps[tap : tap + 1] * padded[pl.ds(LEAD - tap, LEAD)]
    mix_out[...] = result
    rim_out[0] = jnp.where(place < KW - 1, first, 0.0)


def prep_back(rim, mix, step, taps, heads, conv, prepared, state, back_conv, back_prep, back_skip, received):
    count = mix.shape[0]
    rows = count // 2
    return call(
        lambda *refs: prep_back_kernel(len(received), *refs),
        (2,),
        [
            seq_block(LEAD, MIXW),
            row_block(rows, MIXW),
            row_block(rows, 128),
            fixed(8, MIXW),
            fixed(8, 128),
            row_block(rows, MIXW),
            row_block(rows, 256),
            seq_block(SW, NS),
            row_block(rows, MIXW),
            row_block(rows, 256),
            seq_block(8, 128),
        ]
        + [seq_block(SW, NS)] * len(received),
        [
            row_block(rows, MIXW),
            row_block(rows, 128),
            seq_block(LEAD, MIXW),
            seq_block(8, MIXW),
            seq_block(8, 128),
        ],
        [
            shape(count, MIXW),
            shape(count, 128),
            shape(2, LEAD, MIXW),
            shape(2, 8, MIXW),
            shape(2, 8, 128),
        ],
        [
            pltpu.VMEM((LEAD + rows, MIXW), f32),
            pltpu.VMEM((rows + 2 * LEAD, MIXW), f32),
        ],
    )(
        rim,
        mix,
        step,
        taps,
        heads,
        conv,
        prepared,
        state,
        back_conv,
        back_prep,
        back_skip,
        *received,
    )


def assemble_kernel(parts, side, gate, mix, rim, step, query, own, cosine, sine, *refs):
    received, out = refs[:parts], refs[parts]
    rows = mix.shape[0]
    out[:, WIDE:] = gate[...]
    mixed = slice(0, MIXW)
    out[:, mixed] = mix[...].astype(bf16)
    tail = mix[rows - 16 :]
    returned = jnp.concatenate([jnp.zeros((16 - LEAD, MIXW), f32), rim[0]], 0)
    tail = tail + pltpu.roll(returned, LEAD - KW + 1, 0)
    out[rows - 16 :, mixed] = tail.astype(bf16)
    at = MIXW
    out[:, at : at + QW] = query[...]
    half = jnp.zeros((rows // 2, 2 * HD), f32)
    for piece in received:
        half = half + piece[0].astype(f32)
    row = lax.broadcasted_iota(jnp.int32, (rows, 2 * HD), 0)
    pair = own[0] + jnp.where(row // (rows // 2) == side[0], jnp.concatenate([half, half], 0), 0.0)
    at += QW
    out[:, at : at + 2 * HD] = turn_first(pair, cosine[...], -sine[...]).astype(bf16)
    out[:, STEP_AT:WIDE] = step[...].astype(bf16)


def assemble(side, gate, mix, rim, step, query, own, received, cosine, sine):
    count = mix.shape[0]
    rows = count // 2
    return call(
        lambda *refs: assemble_kernel(len(received), *refs),
        (2,),
        [
            SCALAR,
            row_block(rows, SW),
            row_block(rows, MIXW),
            seq_block(LEAD, MIXW),
            row_block(rows, 128),
            row_block(rows, QW),
            seq_block(rows, 2 * HD),
            fixed(rows, 128),
            fixed(rows, 128),
        ]
        + [seq_block(rows // 2, 2 * HD)] * len(received),
        row_block(rows, FULL),
        shape(count, FULL, dtype=bf16),
    )(side, gate, mix, rim, step, query, own, cosine, sine, *received)


def sums_kernel(first_left, first_right, second_left, second_right, out):
    width = first_right.shape[1]
    out[:, :width] = product(first_left[...], first_right[...], 0, 0).astype(bf16)
    out[:, width:] = product(second_left[...], second_right[...], 0, 0).astype(bf16)


def weight_sums(first_left, first_right, second_left, second_right):
    count = first_left.shape[0]
    wide, more = first_right.shape[1], second_right.shape[1]
    rows = 512
    left = pl.BlockSpec((count, rows), lambda b: (0, b))
    return call(
        sums_kernel,
        (D // rows,),
        [left, fixed(count, wide), left, fixed(count, more)],
        row_block(rows, wide + more),
        shape(D, wide + more, dtype=bf16),
    )(first_left, first_right, second_left, second_right)


def local(
    tokens,
    out_cotangent,
    input_gain,
    mamba_gate_weight,
    mamba_mix_weight,
    mamba_step_weight,
    conv_kernel,
    conv_offset,
    step_offset,
    decay_log,
    skip_scale,
    mamba_norm_gain,
    mamba_out_weight,
    query_weight,
    key_weight,
    value_weight,
    attention_out_weight,
    ffn_gain,
    feed_gate_weight,
    feed_up_weight,
    feed_down_weight,
):
    rows = tokens.shape[1]
    span = 2 * rows
    count = 2 * span
    quads, spans = lax.axis_size("dp") // 4, lax.axis_size("ctx") // 2
    devices = 8 * quads * spans
    dp_at, ctx_at = lax.axis_index("dp"), lax.axis_index("ctx")
    side, span_at = ctx_at % 2, ctx_at // 2
    core, pair = dp_at % 2, dp_at // 2 % 2
    rank = core * 2 + side
    part = D // devices
    conv_part = CONV // devices
    gain_part = DSSM // devices
    groups = [
        [
            ((quad * 2 + y) * 2 + c) * 2 * spans + z * 2 + x
            for quad in range(quads)
            for z in range(spans)
            for y in range(2)
        ]
        for c in range(2)
        for x in range(2)
    ]
    feed_groups = [
        [(quad * 4 + d) * 2 * spans + z * 2 + x for quad in range(quads) for z in range(spans)]
        for d in range(4)
        for x in range(2)
    ]

    def order(value):
        lead = value.shape[:-1]
        value = value.reshape(*lead, quads, 4, spans, 2 * part)
        return jnp.swapaxes(value, -3, -2).reshape(*lead, D)

    def disorder(value):
        lead = value.shape[:-1]
        value = value.reshape(*lead, quads, spans, 4, 2 * part)
        return jnp.swapaxes(value, -3, -2).reshape(*lead, D)

    def gather(value, groups):
        return lax.all_gather(value, BOTH, axis=0, tiled=True, axis_index_groups=groups)

    def scatter(value, groups):
        return lax.psum_scatter(
            value, BOTH, scatter_dimension=0, tiled=True, axis_index_groups=groups
        )

    vector = jnp.concatenate([conv_kernel.reshape(-1), conv_offset, mamba_norm_gain])
    vector = jnp.pad(vector, (0, part * (VEC - 2) - vector.shape[0])).reshape(part, VEC - 2)
    tail = jnp.concatenate(
        [
            input_gain[:, None],
            ffn_gain[:, None],
            vector,
            jnp.zeros((part, WIDE - STEP_AT - SH - VEC), bf16),
        ],
        1,
    )
    def mixer_part(s):
        kv = s // 2
        return jnp.concatenate(
            [
                mamba_mix_weight[:, SW * s : SW * (s + 1)],
                mamba_mix_weight[:, DSSM:],
                query_weight[:, QW * s : QW * (s + 1)],
                key_weight[:, HD * kv : HD * (kv + 1)],
                value_weight[:, HD * kv : HD * (kv + 1)],
                mamba_step_weight[:, SH * s : SH * (s + 1)],
                tail,
            ],
            1,
        )

    mixer_own = group_swap(jnp.stack([mixer_part(s) for s in range(TP)]), core, side)
    later = (
        mamba_gate_weight,
        mamba_out_weight,
        attention_out_weight,
        feed_gate_weight,
        feed_up_weight,
        feed_down_weight,
        tokens,
        out_cotangent,
    )
    mixer_own, later = lax.optimization_barrier((mixer_own, later))
    mamba_gate_weight, mamba_out_weight, attention_out_weight = later[:3]
    feed_gate_weight, feed_up_weight, feed_down_weight, tokens, out_cotangent = later[3:]
    mixer = gather(mixer_own.reshape(TP * part, -1), groups)
    mamba_out_turned = mamba_out_weight.T
    attention_out_turned = attention_out_weight.T
    feed_down_turned = feed_down_weight.T

    def branch_part(s):
        return jnp.concatenate(
            [
                mamba_gate_weight[:, SW * s : SW * (s + 1)],
                mamba_out_turned[:, SW * s : SW * (s + 1)],
                attention_out_turned[:, QW * s : QW * (s + 1)],
            ],
            1,
        )

    branch_own = group_swap(jnp.stack([branch_part(s) for s in range(TP)]), core, side)
    branch_own = branch_own.reshape(TP * part, -1)
    def feed_part(s):
        return jnp.concatenate(
            [
                feed_gate_weight[:, FW * s : FW * (s + 1)],
                feed_up_weight[:, FW * s : FW * (s + 1)],
                feed_down_turned[:, FW * s : FW * (s + 1)],
            ],
            1,
        )

    feed_own = feed_swap(jnp.stack([feed_part(s) for s in range(FEED)]), pair, core, side)
    feed_own = feed_own.reshape(FEED * part, -1)
    own_low = order(tokens[0])
    own_hidden = own_low.astype(f32)
    own_scale_one = lax.rsqrt(jnp.mean(own_hidden * own_hidden, -1, keepdims=True) + EPSILON)
    hidden = group_gather(own_low, side)
    own_cotangent = order(out_cotangent[0])
    cosine, sine = rope_tables(span_at * span + jnp.arange(span, dtype=jnp.int32))
    upstream = feed_gather_slow(own_cotangent)
    rim_hidden = move_spans(hidden.reshape(2, span, D)[:, span - 16 :], 1)
    branch_own, feed_own, mixer, hidden, rim_hidden, upstream, cosine, sine = (
        lax.optimization_barrier(
            (branch_own, feed_own, mixer, hidden, rim_hidden, upstream, cosine, sine)
        )
    )
    branch = gather(branch_own, groups)
    full_gate, full_out = branch[:, :SW], branch[:, SW:]
    feed = gather(feed_own, feed_groups)

    at = STEP_AT + SH + 2
    vectors = mixer[:, at : at + VEC - 2]
    natural = vectors.reshape(quads, spans, 4, 2, part * (VEC - 2))
    natural = natural.transpose(0, 2, 1, 3, 4).reshape(devices, part * (VEC - 2))
    at = 0
    all_kernel = natural[:, at : at + KW * conv_part].reshape(devices, KW, conv_part)
    all_kernel = all_kernel.transpose(1, 0, 2).reshape(KW, CONV)
    at += KW * conv_part
    all_offset = natural[:, at : at + conv_part].reshape(1, CONV)
    at += conv_part
    all_mamba_gain = natural[:, at : at + gain_part].reshape(DSSM)
    taps = jnp.concatenate([all_kernel, all_offset], 0)
    taps = jnp.concatenate(
        [lax.dynamic_slice_in_dim(taps, rank * SW, SW, 1), taps[:, DSSM:]], 1
    ).astype(f32)
    kernel, offset = taps[:KW], taps[KW]
    mamba_gain = lax.dynamic_slice_in_dim(all_mamba_gain, rank * SW, SW, 0).astype(f32)
    own_step_offset = lax.dynamic_slice_in_dim(step_offset, rank * SH, SH, 0)
    own_decay_log = lax.dynamic_slice_in_dim(decay_log, rank * SH, SH, 0)
    own_skip = lax.dynamic_slice_in_dim(skip_scale, rank * SH, SH, 0)

    at = jnp.reshape(span_at, (1,)).astype(jnp.int32)
    taps = jnp.pad(taps, ((0, 8 - taps.shape[0]), (0, 0)))
    heads = jnp.stack([own_step_offset, own_decay_log])
    heads = jnp.pad(heads, ((0, 6), (0, 128 - SH)))
    skip = jnp.repeat(own_skip, MP)[None]

    low_normed, mix_rows, query, key_value, step_rows, gains, rim = project(
        hidden, rim_hidden, mixer, cosine, sine
    )
    full_gain, full_gain_two = gains[0], gains[1]
    key_value = key_value.reshape(2, span, 2 * HD)
    half = jnp.where(side == 0, key_value[:, :rows], key_value[:, rows:])
    halves_in = jnp.stack([move_spans(half, s) for s in range(1, spans)], 1)
    halves_other = swap_side(halves_in)
    reached = jnp.stack(
        [
            jnp.where(side == 0, halves_in, halves_other),
            jnp.where(side == 0, halves_other, halves_in),
        ],
        2,
    ).reshape(2, (spans - 1) * span, 2 * HD)
    key_values = jnp.concatenate([key_value, reached], 1)
    conv, prepared, turned, message = prep(rim, mix_rows, step_rows, taps, heads)
    messages = [move_spans(message, s) for s in range(1, spans)]
    attended, log_total = attend(at, query, key_values)
    mixed, state_in = scan(conv, prepared, turned, skip, messages)
    gate_rows = forward_product(low_normed, full_gate)
    gate_sigmoid = jax.nn.sigmoid(gate_rows)
    gate_silu = gate_rows * gate_sigmoid
    gated = mixed * gate_silu
    square = group_sum(jnp.sum(gated * gated, -1))
    mamba_scale = lax.rsqrt(square / DSSM + EPSILON)[:, None]
    mamba_rows = (gated * mamba_scale * mamba_gain).astype(bf16)
    branches = jnp.concatenate([mamba_rows, attended], 1)
    middle = own_hidden + group_scatter(input_product(branches, full_out), side)
    middle, feed = lax.optimization_barrier((middle, feed))

    scale_two = lax.rsqrt(jnp.mean(middle * middle, -1, keepdims=True) + EPSILON)
    low_two = feed_gather((middle * scale_two * full_gain_two).astype(bf16))
    back_feed, activation, own_partial, other_partial, layer_partial = feed_pass(
        low_two, upstream, feed
    )
    back_normed_two, feed_sums = feed_scatter(
        own_partial, other_partial, weight_sums(low_two, back_feed, upstream, activation)
    )
    gradient_feed = scatter(feed_sums, feed_groups)
    weighted = back_normed_two * full_gain_two
    gradient_gain_two = jnp.sum(back_normed_two * middle * scale_two, 0)
    back_middle = (
        own_cotangent.astype(f32)
        + scale_two * weighted
        - middle * scale_two**3 * jnp.mean(weighted * middle, -1, keepdims=True)
    )
    low_middle = group_gather(back_middle.astype(bf16), side)

    back_branches = forward_product(low_middle, full_out)
    back_attended = back_branches[:, SW:].astype(bf16)
    back_rows = back_branches[:, :SW]
    weighted = back_rows * mamba_gain
    gradient_mamba_gain = jnp.sum(back_rows * gated * mamba_scale, 0)
    mean = group_sum(jnp.sum(weighted * gated, -1))[:, None] / DSSM
    back_gated = mamba_scale * weighted - gated * mamba_scale**3 * mean
    back_mixed = back_gated * gate_silu
    low_gate = (
        back_gated * mixed * gate_sigmoid * (1.0 + gate_rows * (1.0 - gate_sigmoid))
    ).astype(bf16)
    back_attended, gradient_feed = lax.optimization_barrier((back_attended, gradient_feed))
    back_query, own_back, other_back = attend_back(
        at, query, key_values, attended, log_total, back_attended, cosine, sine
    )
    other_back = other_back.reshape(2, spans - 1, 2, rows, 2 * HD)
    low_half, high_half = other_back[:, :, 0], other_back[:, :, 1]
    half_back = jnp.where(side == 0, low_half, high_half).astype(f32)
    half_back = half_back + swap_side(jnp.where(side == 0, high_half, low_half)).astype(f32)
    half_back = half_back.astype(bf16)
    back_conv, back_prep, back_skip, *sent = scan_back(
        back_mixed, conv, prepared, turned, skip, state_in, messages
    )
    received = [move_spans(piece, -s) for s, piece in zip(range(1, spans), sent)]
    pieces = [move_spans(half_back[:, s - 1], -s) for s in range(1, spans)]
    back_mix, back_step, back_rim, tap_sums, head_sums = prep_back(
        rim,
        mix_rows,
        step_rows,
        taps,
        heads,
        conv,
        prepared,
        state_in,
        back_conv,
        back_prep,
        back_skip,
        received,
    )
    back_rim = move_spans(back_rim, -1)
    back_all = assemble(
        jnp.reshape(side, (1,)).astype(jnp.int32),
        low_gate,
        back_mix,
        back_rim,
        back_step,
        back_query,
        own_back,
        pieces,
        cosine,
        sine,
    )
    back_all, layer_partial = lax.optimization_barrier((back_all, layer_partial))
    layer_half = layer_partial.shape[0] // 2
    layer_out = middle + feed_scatter(layer_partial[:layer_half], layer_partial[layer_half:])[0]
    gradient_mixer = scatter(
        weight_sums(low_normed, back_all, low_middle, branches), groups
    )
    back_normed = group_scatter(
        input_product(back_all[:, :WIDE], mixer) + input_product(back_all[:, WIDE:], full_gate),
        side,
    )
    weighted = back_normed * full_gain
    gradient_gain_one = jnp.sum(back_normed * own_hidden * own_scale_one, 0)
    input_gradient = (
        back_middle
        + own_scale_one * weighted
        - own_hidden * own_scale_one**3 * jnp.mean(weighted * own_hidden, -1, keepdims=True)
    )

    def placed(value, width):
        wide = jnp.zeros(value.shape[:-1] + (width,), f32)
        return lax.dynamic_update_slice_in_dim(
            wide, value, rank * value.shape[-1], value.ndim - 1
        )

    tap_grads = jnp.sum(tap_sums, 0)[: KW + 1]
    tap_grads = jnp.concatenate([placed(tap_grads[:, :SW], DSSM), tap_grads[:, SW:]], 1)
    head_grads = jnp.sum(head_sums, 0)[:3, :SH]
    gain_grads, tap_grads, mamba_gain_grad, head_grads = lax.psum(
        (
            jnp.stack([gradient_gain_one, gradient_gain_two]),
            tap_grads,
            placed(gradient_mamba_gain, DSSM),
            placed(head_grads, MH),
        ),
        BOTH,
    )
    feature_at = (((dp_at // 4 * spans + span_at) * 2 + pair) * TP + rank) * part
    own_gains = lax.dynamic_slice_in_dim(gain_grads, feature_at, part, 1)
    device_at = dp_at * 2 * spans + ctx_at
    own_taps = lax.dynamic_slice_in_dim(tap_grads, device_at * conv_part, conv_part, 1)
    own_mamba_gain = lax.dynamic_slice_in_dim(
        mamba_gain_grad, device_at * gain_part, gain_part, 0
    )

    feed_parts = feed_swap(gradient_feed.reshape(FEED, part, -1), pair, core, side).astype(f32)
    mixer_parts = group_swap(gradient_mixer.reshape(TP, part, -1), core, side).astype(f32)

    def columns(parts, start, width):
        piece = parts[:, :, start : start + width]
        return piece.transpose(1, 0, 2).reshape(part, parts.shape[0] * width)

    def shared(start):
        piece = mixer_parts[:, :, start : start + HD].reshape(KVH, TP // KVH, part, HD)
        return jnp.sum(piece, 1).transpose(1, 0, 2).reshape(part, KVH * HD)

    at = MIXW
    mix_gradient = jnp.concatenate(
        [
            columns(mixer_parts, 0, SW),
            jnp.sum(mixer_parts[:, :, SW:MIXW], 0),
        ],
        1,
    )
    return (
        disorder(layer_out.astype(bf16))[None],
        disorder(input_gradient)[None],
        own_gains[0],
        columns(mixer_parts, WIDE, SW),
        mix_gradient,
        columns(mixer_parts, STEP_AT, SH),
        own_taps[:KW],
        own_taps[KW],
        head_grads[0],
        head_grads[1],
        head_grads[2],
        own_mamba_gain,
        columns(mixer_parts, FULL, SW).T,
        columns(mixer_parts, at, QW),
        shared(at + QW),
        shared(at + QW + HD),
        columns(mixer_parts, FULL + SW, QW).T,
        own_gains[1],
        columns(feed_parts, 0, FW),
        columns(feed_parts, FW, FW),
        columns(feed_parts, 2 * FW, FW).T,
    )


def solution(mesh):
    both = BOTH
    tokens = P("dp", "ctx", None)
    first = P(both, None)
    second = P(None, both)
    vector = P(both)
    whole = P()
    weights = (
        vector,
        first,
        first,
        first,
        second,
        vector,
        whole,
        whole,
        whole,
        vector,
        second,
        first,
        first,
        first,
        second,
        vector,
        first,
        first,
        second,
    )
    return jax.shard_map(
        local,
        mesh=mesh,
        in_specs=(tokens, tokens) + weights,
        out_specs=(tokens, tokens) + weights,
        check_vma=False,
    )
```
